32 devices in a mesh: ctx: 16 (over z, y, core), fsdp: 2 (over x).
Axes of the slice: x: 2, y: 2, z: 4, core: 2. Of those that a mesh axis runs over, the one named last changes fastest.
Arguments:
- tokens: bfloat16 [4, 2048, 512], P('fsdp', 'ctx'), may hold values from -6 to 6
- encoder: bfloat16 [4, 512, 512], P('fsdp', 'ctx'), may hold values from -6 to 6
- step_ids: int32 [4], P('fsdp'), may hold values from 0 to 49
- out_grad: bfloat16 [4, 2048, 512], P('fsdp', 'ctx'), may hold values from -6 to 6
- self_in: bfloat16 [512, 1536], P('fsdp'), may hold values from -0.25 to 0.25
- self_out: bfloat16 [512, 512], P('fsdp'), may hold values from -6 to 6
- cross_query: bfloat16 [512, 512], P('fsdp'), may hold values from -0.25 to 0.25
- cross_keyval: bfloat16 [512, 1024], P('fsdp'), may hold values from -0.25 to 0.25
- cross_out: bfloat16 [512, 512], P('fsdp'), may hold values from -3.5 to 3.5
- ffn_up: bfloat16 [512, 2048], P('fsdp'), may hold values from -0.25 to 0.25
- up_bias: bfloat16 [2048], P('fsdp'), may hold values from -4 to 4
- ffn_down: bfloat16 [2048, 512], P('fsdp'), may hold values from -0.125 to 0.125
- down_bias: bfloat16 [512], P('fsdp'), may hold values from -4 to 4
- norm_gain: bfloat16 [3, 512], P(None, 'fsdp'), may hold values from 0.5 to 1.5
- norm_shift: bfloat16 [3, 512], P(None, 'fsdp'), may hold values from -4 to 4
- step_table: bfloat16 [50, 512], P(None, 'fsdp'), may hold values from -6 to 6
Outputs:
- mixed: bfloat16 [4, 2048, 512], P('fsdp', 'ctx')
- tokens_grad: float32 [4, 2048, 512], P('fsdp', 'ctx')
- encoder_grad: float32 [4, 512, 512], P('fsdp', 'ctx')
- self_in_grad: float32 [512, 1536], P('fsdp')
- self_out_grad: float32 [512, 512], P('fsdp')
- cross_query_grad: float32 [512, 512], P('fsdp')
- cross_keyval_grad: float32 [512, 1024], P('fsdp')
- cross_out_grad: float32 [512, 512], P('fsdp')
- ffn_up_grad: float32 [512, 2048], P('fsdp')
- up_bias_grad: float32 [2048], P('fsdp')
- ffn_down_grad: float32 [2048, 512], P('fsdp')
- down_bias_grad: float32 [512], P('fsdp')
- norm_gain_grad: float32 [3, 512], P(None, 'fsdp')
- norm_shift_grad: float32 [3, 512], P(None, 'fsdp')
- step_table_grad: float32 [50, 512], P(None, 'fsdp')
The draws below stay inside these ranges and needn't reach their ends.
All inputs are finite; a program needn't handle non-finite values.
Results may differ from the reference program's by a relative error of at most 0.025.
Values may be sent and summed in bfloat16 or wider, within the bound.
No kernel may reach another device: no remote copies, remote signals or barrier semaphores. Data moves between devices by JAX's collectives and lax.ppermute only.
A program may use at most 192 MiB of HBM per device.

```python
import math
import jax
import jax.numpy as jnp
from jax import lax

D = 512
H = 8
FF = 2048
ENC = 512
STEPS = 50
LEN = 2048
SEQS = 4


def set_ends(array, rng, low, largest):
    place = [jax.random.randint(jax.random.fold_in(rng, axis), (), 0, length) for axis, length in enumerate(array.shape)]
    main_axis = array.shape.index(max(array.shape))
    next_to = place[:main_axis] + [(place[main_axis] + 1) % array.shape[main_axis]] + place[main_axis + 1:]
    return array.at[tuple(place)].set(low).at[tuple(next_to)].set(largest)


def block_levels(rng, shape, pieces, least, top_value):
    level, own = 1.0, jax.random.fold_in(rng, 6)
    for axis_at, parts in pieces:
        steps = jnp.exp(jax.random.uniform(jax.random.fold_in(own, axis_at), (parts,), jnp.float32, least / len(pieces), top_value / len(pieces)))
        level = level * jnp.repeat(steps, shape[axis_at] // parts).reshape([-1 if axis == axis_at else 1 for axis in range(len(shape))])
    return level


def normal_values(rng, shape, scale, reach, shards=(), kind=jnp.bfloat16):
    level = block_levels(rng, shape, shards, -0.22, 0.18) if shards else 1.0
    drawn = jax.random.normal(rng, shape, jnp.float32) * scale * level
    return jnp.minimum(jnp.maximum(drawn, -reach), reach).astype(kind)


def setup_inputs(seed: int = 0) -> dict:
    key_of = jax.random.split(jax.random.key(seed), 17)
    tokens = normal_values(key_of[0], (SEQS, LEN, D), 1.0, 6.0, ((0, 2), (1, 16)))
    encoder = normal_values(key_of[1], (SEQS, ENC, D), 1.0, 6.0, ((0, 2), (1, 16)))
    step_ids = set_ends(jax.random.randint(key_of[2], (SEQS,), 0, STEPS), jax.random.fold_in(key_of[2], 1), 0, STEPS - 1).astype(jnp.int32)
    out_grad = normal_values(key_of[3], (SEQS, LEN, D), 1.0, 6.0, ((0, 2), (1, 16)))
    self_in = normal_values(key_of[4], (D, 3 * D), D ** -0.5, 0.25, ((0, 2),))
    self_out = normal_values(key_of[5], (D, D), (1 + LEN // (8 * D)), 6.0, ((0, 2),))
    cross_query = normal_values(key_of[6], (D, D), D ** -0.5, 0.25, ((0, 2),))
    cross_keyval = normal_values(key_of[7], (D, 2 * D), D ** -0.5, 0.25, ((0, 2),))
    cross_out = normal_values(key_of[8], (D, D), (3 * D // ENC) ** -0.5, 3.5, ((0, 2),))
    ffn_up = normal_values(key_of[9], (D, FF), D ** -0.5, 0.25, ((0, 2),))
    up_bias = normal_values(key_of[10], (FF,), 0.3, 4.0, ((0, 2),))
    ffn_down = normal_values(key_of[11], (FF, D), FF ** -0.5, 0.125, ((0, 2),))
    down_bias = normal_values(key_of[12], (D,), 0.3, 4.0, ((0, 2),))
    norm_gain = jnp.clip(1.0 + 0.1 * jax.random.normal(key_of[13], (3, D), jnp.float32), 0.5, 1.5).astype(jnp.bfloat16)
    norm_shift = normal_values(key_of[14], (3, D), 0.3, 4.0, ((1, 2),))
    step_table = normal_values(key_of[15], (STEPS, D), 0.5, 6.0, ((1, 2),))
    return {"tokens": tokens, "encoder": encoder, "step_ids": step_ids, "out_grad": out_grad, "self_in": self_in, "self_out": self_out, "cross_query": cross_query, "cross_keyval": cross_keyval, "cross_out": cross_out, "ffn_up": ffn_up, "up_bias": up_bias, "ffn_down": ffn_down, "down_bias": down_bias, "norm_gain": norm_gain, "norm_shift": norm_shift, "step_table": step_table}


@jax.custom_vjp
def low(v):
    return lax.optimization_barrier(v.astype(jnp.bfloat16)).astype(jnp.float32)

@jax.custom_vjp
def low_back(v):
    return v

def low_keep(v):
    return (low(v), None)

def low_pass(kept, grad):
    return (grad,)

def back_keep(v):
    return (v, None)

def back_low(kept, grad):
    return (low(grad),)
low.defvjp(low_keep, low_pass)
low_back.defvjp(back_keep, back_low)
norm_epsilon = 1e-05
highest = lax.Precision.HIGHEST

def layer_norm(values, gain, shift):
    centre = lax.optimization_barrier(jnp.mean(values, axis=-1, keepdims=True))
    centred = values - centre
    spread = lax.optimization_barrier(jnp.mean(centred * centred, axis=-1, keepdims=True))
    return centred * lax.rsqrt(spread + norm_epsilon) * gain + shift

def matmul(left, right):
    return jnp.dot(left, right, precision=highest)

def softmax_rows(scores):
    peak_score = lax.optimization_barrier(jnp.max(scores, axis=-1, keepdims=True))
    shares = jnp.exp(scores - peak_score)
    return shares / lax.optimization_barrier(jnp.sum(shares, axis=-1, keepdims=True))

def attention(queries, keys, values, scale):
    length = queries.shape[0]
    head_width = queries.shape[2]
    block = math.gcd(length, 512)

    def attend(query_block):
        scores = low_back(scale * jnp.einsum('qhd,khd->qhk', query_block, keys, precision=highest))
        shares = softmax_rows(scores)
        return jnp.einsum('qhk,khd->qhd', low(shares), values, precision=highest)
    result = lax.map(jax.checkpoint(attend), queries.reshape(length // block, block, H, head_width))
    return result.reshape(length, H * head_width)

def layer(token_rows, enc_rows, onehot, weights):
    self_in, self_out, cross_query, cross_keyval, cross_out, ffn_up, up_bias, ffn_down, down_bias, norm_gain, norm_shift, step_table = weights
    length = token_rows.shape[0]
    enc_count = enc_rows.shape[0]
    head_width = D // H
    scale = 1.0 / math.sqrt(head_width)
    start = token_rows + matmul(onehot, step_table)[None, :]
    normed0 = low(layer_norm(start, norm_gain[0], norm_shift[0]))
    joined = low_back(low(matmul(normed0, self_in)))
    queries = joined[:, :D].reshape(length, H, head_width)
    keys = joined[:, D:2 * D].reshape(length, H, head_width)
    values = joined[:, 2 * D:].reshape(length, H, head_width)
    attended = low_back(low(attention(queries, keys, values, scale)))
    hidden1 = start + low_back(matmul(attended, self_out))
    normed1 = low(layer_norm(hidden1, norm_gain[1], norm_shift[1]))
    cross_q = low_back(low(matmul(normed1, cross_query))).reshape(length, H, head_width)
    cross_kv = low_back(low(matmul(enc_rows, cross_keyval)))
    cross_keys = cross_kv[:, :D].reshape(enc_count, H, head_width)
    cross_values = cross_kv[:, D:].reshape(enc_count, H, head_width)
    crossed = low_back(low(attention(cross_q, cross_keys, cross_values, scale)))
    hidden2 = hidden1 + low_back(matmul(crossed, cross_out))
    normed2 = low(layer_norm(hidden2, norm_gain[2], norm_shift[2]))
    pre_act = low_back(matmul(normed2, ffn_up) + up_bias)
    activated = low(jax.nn.gelu(pre_act))
    return hidden2 + low_back(matmul(activated, ffn_down) + down_bias)

def reference(tokens, encoder, step_ids, out_grad, self_in, self_out, cross_query, cross_keyval, cross_out, ffn_up, up_bias, ffn_down, down_bias, norm_gain, norm_shift, step_table):
    weights = (self_in.astype(jnp.float32), self_out.astype(jnp.float32), cross_query.astype(jnp.float32), cross_keyval.astype(jnp.float32), cross_out.astype(jnp.float32), ffn_up.astype(jnp.float32), up_bias.astype(jnp.float32), ffn_down.astype(jnp.float32), down_bias.astype(jnp.float32), norm_gain.astype(jnp.float32), norm_shift.astype(jnp.float32), step_table.astype(jnp.float32))

    def one_sequence(totals, inputs):
        token_rows, enc_rows, step_index, grad_rows = inputs
        onehot = (jnp.arange(STEPS, dtype=jnp.int32) == step_index).astype(jnp.float32)

        def forward(rows_value, enc_value, params):
            return layer(rows_value, enc_value, onehot, params)
        mixed, pullback = jax.vjp(forward, token_rows.astype(jnp.float32), enc_rows.astype(jnp.float32), weights)
        rows_grad, enc_grad, param_grads = pullback(grad_rows.astype(jnp.float32))
        totals = jax.tree.map(jnp.add, totals, param_grads)
        return (totals, (mixed.astype(jnp.bfloat16), rows_grad, enc_grad))
    zero_grads = tuple((jnp.zeros(weight.shape, jnp.float32) for weight in weights))
    totals, results = lax.scan(one_sequence, zero_grads, (tokens, encoder, step_ids, out_grad))
    mixed, tokens_grad, encoder_grad = results
    return (mixed, tokens_grad, encoder_grad, totals[0], totals[1], totals[2], totals[3], totals[4], totals[5], totals[6], totals[7], totals[8], totals[9], totals[10], totals[11])
```

```python
import functools
import math

import jax
import jax.numpy as jnp
from jax import lax
from jax.experimental import pallas as pl
from jax.experimental.pallas import tpu as pltpu
from jax.sharding import PartitionSpec as P

H = 8
EPS = 1e-05
F32 = jnp.float32
BF = jnp.bfloat16
LOG2E = 1.4426950408889634
VMEM_LIMIT = 56 * 1024 * 1024


def nn(a, b):
    return lax.dot_general(a, b, (((1,), (0,)), ((), ())), preferred_element_type=F32)


def nt(a, b):
    return lax.dot_general(a, b, (((1,), (1,)), ((), ())), preferred_element_type=F32)


def flip(v):
    return jnp.transpose(v)


def normalise(v):
    centred = v - jnp.mean(v, axis=-1, keepdims=True)
    r = lax.rsqrt(jnp.mean(centred * centred, axis=-1, keepdims=True) + EPS)
    return centred * r, r


def norm_back(grad, gain, xhat, r):
    u = grad * gain
    return r * (u - jnp.mean(u, axis=-1, keepdims=True) - xhat * jnp.mean(u * xhat, axis=-1, keepdims=True))


def aligned(index, size):
    return pl.ds(pl.multiple_of(index, size), size)


VM = pl.BlockSpec(memory_space=pltpu.VMEM)
SM = pl.BlockSpec(memory_space=pltpu.SMEM)
ANY = pl.BlockSpec(memory_space=pl.ANY)


def call(kernel, name, outs, in_specs, scratch, args, flops, nbytes, exps=0, out_specs=None):
    return pl.pallas_call(
        kernel,
        name=name,
        out_shape=[jax.ShapeDtypeStruct(s, d) for s, d in outs],
        in_specs=in_specs,
        out_specs=out_specs or [VM] * len(outs),
        scratch_shapes=scratch,
        compiler_params=pltpu.CompilerParams(vmem_limit_bytes=VMEM_LIMIT),
        cost_estimate=pl.CostEstimate(flops=flops, bytes_accessed=nbytes, transcendentals=exps),
    )(*args)


class Placer:
    def __init__(self, sems, x, c):
        self.sems, self.x, self.c, self.used = sems, x, c, 0

    def copy(self, src, dst):
        copy = pltpu.make_async_copy(src, dst, self.sems.at[self.used])
        self.used += 1
        copy.start()
        return copy

    def lay(self, own, near, far, dst, row0, blocks):
        rows = own.shape[0]
        half = rows // 2
        base = (1 - self.x) * rows
        copies = [self.copy(own, dst.at[aligned(self.x * rows, rows)])]
        for b in range(blocks):
            cols = pl.ds(b * 512, 512)
            part = pl.ds(row0 + b * half, half)
            copies.append(self.copy(near.at[part], dst.at[aligned(base + self.c * half, half), cols]))
            copies.append(self.copy(far.at[part], dst.at[aligned(base + (1 - self.c) * half, half), cols]))
        return copies


def wait(copies):
    for copy in copies:
        copy.wait()


def attend_kernel(
    meta, place, even, odd, step, gain, shift, wh_own, wh_other, xhat_out, joined_out, heads_out, full_out, stats_out,
    wh, normed, keys,
):
    x = meta[0]
    n, width = xhat_out.shape
    half = wh_own.shape[1]
    hd = joined_out.shape[0] // 3
    blocks, rows = even.shape[0], even.shape[1]
    wh[:, aligned(x * half, half)] = wh_own[...]
    wh[:, aligned((1 - x) * half, half)] = wh_other[...]
    stats_out[...] = jnp.zeros_like(stats_out)
    for k in range(2 * blocks):
        block = even[k] if k < blocks else odd[k - blocks]
        xhat, r = normalise(block.astype(F32) + step[...])
        at = aligned(place[k] * rows, rows)
        xhat_out[at, :] = xhat.astype(BF)
        normed[at, :] = (xhat * gain[...] + shift[...]).astype(BF)
        stats_out[1:2, at] = flip(jnp.broadcast_to(r, (rows, 128)))[0:1, :]
    for b in range(n // 512):
        cols = pl.ds(b * 512, 512)
        joined_out[:, cols] = nt(wh[...], normed[cols, :]).astype(BF)
    keys[...] = flip(joined_out[hd : 2 * hd, :].astype(F32)).astype(BF)
    factor = LOG2E / math.sqrt(hd)
    wide = 256

    def query_block(b, carry):
        cols = aligned(b * wide, wide)
        scores = nn(keys[...], joined_out[0:hd, cols]) * factor
        peak = jnp.max(scores, axis=0, keepdims=True)
        shares = jnp.exp2(scores - peak)
        total = jnp.sum(shares, axis=0, keepdims=True)
        out = nn(joined_out[2 * hd : 3 * hd, :], shares.astype(BF)) / total
        full_out[:, cols] = out
        stats_out[0:1, cols] = peak + jnp.log2(total)
        for part in range(wide // rows):
            heads_out[b * (wide // rows) + part] = out[:, part * rows : (part + 1) * rows].astype(BF)
        return carry

    lax.fori_loop(0, n // wide, query_block, 0)


def attend_back_kernel(
    meta, joined, full, stats, grads, xhat, gain, shift, wh_own, wh_other, extra, joined_grad_out, keep_out, send_out,
    wh, keys, values, gout, lhs, query_acc, whole,
):
    x, active, slot = meta[0], meta[3], meta[4]
    n, width = xhat.shape
    half = wh_own.shape[1]
    hd = joined.shape[0] // 3
    rows = grads.shape[2]
    scale = 1.0 / math.sqrt(hd)
    factor = LOG2E * scale
    wh[:, aligned(x * half, half)] = wh_own[...]
    wh[:, aligned((1 - x) * half, half)] = wh_other[...]
    for j in range(grads.shape[0]):
        gout[:, j * rows : (j + 1) * rows] = grads[j]
    keys[...] = flip(joined[hd : 2 * hd, :].astype(F32)).astype(BF)
    values[...] = flip(joined[2 * hd : 3 * hd, :].astype(F32)).astype(BF)
    delta = jnp.sum(gout[...].astype(F32) * full[...], axis=0, keepdims=True)
    lse = stats[0:1, :]
    query_acc[...] = jnp.zeros_like(query_acc)
    wide = 256

    def key_block(b, carry):
        at = aligned(b * wide, wide)
        queries = joined[0:hd, :]
        shares = jnp.exp2(nn(keys[at, :], queries) * factor - lse)
        share_grad = nn(values[at, :], gout[...])
        score_grad = (shares * (share_grad - delta)).astype(BF)
        lhs[hd : 2 * hd, at] = (nt(queries, score_grad) * scale).astype(BF)
        lhs[2 * hd : 3 * hd, at] = nt(gout[...], shares.astype(BF)).astype(BF)
        query_acc[...] += nn(joined[hd : 2 * hd, at], score_grad)
        return carry

    lax.fori_loop(0, n // wide, key_block, 0)
    lhs[0:hd, :] = (query_acc[...] * scale).astype(BF)
    for j in range(joined_grad_out.shape[0]):
        joined_grad_out[j] = lhs[0 : 3 * hd, j * rows : (j + 1) * rows]

    grad = lhs[0 : 3 * hd, :].astype(F32)
    r = stats[1:2, :]
    weight = wh[...].astype(F32)
    bias = jnp.sum(weight * shift[...], axis=1, keepdims=True)
    mixed_mean = jnp.sum(grad * (joined[...].astype(F32) - bias), axis=0, keepdims=True) * (1.0 / width)
    tail = lhs.shape[0] - 3 * hd
    first = lax.broadcasted_iota(jnp.int32, (tail, n), 0) == 0
    lhs[3 * hd :, :] = jnp.where(first, mixed_mean * r, 0.0).astype(BF)
    product = nn(lhs[...], xhat[...])
    m = product[0 : 3 * hd]
    sums = jnp.sum(grad, axis=1, keepdims=True)
    scaled_sums = jnp.sum(grad * r, axis=1, keepdims=True)
    lead = gain[...] * jnp.sum(weight * scaled_sums, axis=0, keepdims=True)
    start_sum = lead - jnp.mean(lead, axis=1, keepdims=True) - product[3 * hd : 3 * hd + 1]
    on = active.astype(F32)
    whole[0 : 3 * hd, :] = (m * gain[...] + sums * shift[...]) * on
    gain_grad = jnp.sum(weight * m, axis=0, keepdims=True) * on
    shift_grad = jnp.sum(weight * sums, axis=0, keepdims=True) * on
    row = lax.broadcasted_iota(jnp.int32, extra.shape, 0)
    more = jnp.where(row == 0, gain_grad, 0.0) + jnp.where(row == 1, shift_grad, 0.0)
    more = more + jnp.where(row == 2 + slot, start_sum * on, 0.0)
    whole[3 * hd :, :] = extra[...] + more
    keep_out[...] = whole[:, aligned(x * half, half)]
    send_out[...] = whole[:, aligned((1 - x) * half, half)].astype(BF)


def encoder_kernel(meta, enc, own, near, far, kvt_out, weight_out, sems):
    put = Placer(sems, meta[0], meta[1])
    wait(put.lay(own, near, far, weight_out, 0, 2))
    for s in range(enc.shape[0]):
        for b in range(2):
            kv = nn(enc[s], weight_out[:, b * 512 : (b + 1) * 512])
            kvt_out[s, b * 512 : (b + 1) * 512, :] = flip(kv).astype(BF)


def chunk_at(meta, k, xr):
    x, c = meta[0], meta[1]
    return x ^ xr, c ^ k


def forward_kernel(
    meta, tokens, steps, att, kvt, gains, shifts, up_bias, down_bias, out_grad,
    own_out, own_query, own_cross, own_up, own_down, near2, far2, near3, far3,
    mixed_out, h2g_out, h1_out, q_out, crossed_out, shares_out, extra_out, keep_out, send_out,
    w_out, w_query, w_cross, w_up, w_down, act_t, n2_t, pre_low, sems,
):
    seqs, rows, width = tokens.shape
    hd = width // H
    ff = w_down.shape[0]
    slots = extra_out.shape[0]
    put = Placer(sems, meta[0], meta[1])
    half = own_out.shape[0] // 2
    c_out = put.lay(own_out, near2, far2, w_out, 2 * half, 1)
    c_query = put.lay(own_query, near2, far2, w_query, 3 * half, 1)
    c_cross = put.lay(own_cross, near2, far2, w_cross, 4 * half, 1)
    c_up = put.lay(own_up, near3, far3, w_up, 0, 4)
    c_down = put.lay(own_down, near3, far3, w_down, 4 * half, 1)
    factor = LOG2E / math.sqrt(hd)

    wait(c_out)
    for s in range(seqs):
        at = pl.ds(s * rows, rows)
        start = tokens[s].astype(F32) + steps[s : s + 1, :]
        h1_out[at, :] = start + nn(flip(att[s]), w_out[...])
    hidden1 = h1_out[...]
    xhat1, unused = normalise(hidden1)
    wait(c_query)
    q_out[...] = nn((xhat1 * gains[1:2, :] + shifts[1:2, :]).astype(BF), w_query[...]).astype(BF)
    for s in range(seqs):
        for h in range(H):
            q = q_out[s * rows : (s + 1) * rows, h * hd : (h + 1) * hd]
            scores = nn(q, kvt[s, h * hd : (h + 1) * hd, :]) * factor
            shares = jnp.exp2(scores - jnp.max(scores, axis=1, keepdims=True))
            shares = (shares * (1.0 / jnp.sum(shares, axis=1, keepdims=True))).astype(BF)
            shares_out[s * H + h] = shares
            got = nt(kvt[s, width + h * hd : width + (h + 1) * hd, :], shares)
            crossed_out[s, h * hd : (h + 1) * hd, :] = got.astype(BF)
    wait(c_cross)
    crossed = jnp.concatenate([flip(crossed_out[s]) for s in range(seqs)], axis=0)
    hidden2 = hidden1 + nn(crossed, w_cross[...])
    xhat2, r2 = normalise(hidden2)
    n2 = (xhat2 * gains[2:3, :] + shifts[2:3, :]).astype(BF)
    n2_t[...] = flip(n2)
    grad = jnp.concatenate([out_grad[s] for s in range(seqs)], axis=0)
    top = grad.astype(F32)
    wait(c_up)
    wait(c_down)
    mixed = hidden2 + down_bias[...]
    n2_grad = jnp.zeros_like(hidden2)
    extra_out[...] = jnp.zeros_like(extra_out)
    root = math.sqrt(2.0 / math.pi)
    bias_row = slots - 10
    for b in range(ff // 512):
        cols = pl.ds(b * 512, 512)
        pre = nn(n2, w_up[:, cols]) + up_bias[:, cols]
        square = pre * pre
        bent = jnp.tanh(root * pre * (1.0 + 0.044715 * square))
        act = (0.5 * pre * (1.0 + bent)).astype(BF)
        slope = 0.5 * (1.0 + bent) + 0.5 * root * pre * (1.0 - bent * bent) * (1.0 + 3.0 * 0.044715 * square)
        mixed = mixed + nn(act, w_down[cols, :])
        act_t[cols, :] = flip(act)
        low = (nt(grad, w_down[cols, :]) * slope).astype(BF)
        pre_low[:, cols] = low
        n2_grad = n2_grad + nt(low, w_up[:, cols])
        sums = jnp.sum(low.astype(F32), axis=0, keepdims=True)
        per_half = ff // 512 // 2
        lanes = pl.ds((b // per_half) * 256, 256)
        for piece in range(2):
            row = bias_row + 1 + (b % per_half) * 2 + piece
            extra_out[row : row + 1, lanes] = sums[:, piece * 256 : (piece + 1) * 256]
    for s in range(seqs):
        mixed_out[s] = mixed[s * rows : (s + 1) * rows].astype(BF)
    h2g_out[...] = top + norm_back(n2_grad, gains[2:3, :], xhat2, r2)
    extra_out[bias_row : bias_row + 1, :] = jnp.sum(top, axis=0, keepdims=True)
    extra_out[bias_row + 5 : bias_row + 6, :] = jnp.sum(n2_grad * xhat2, axis=0, keepdims=True)
    extra_out[bias_row + 6 : bias_row + 7, :] = jnp.sum(n2_grad, axis=0, keepdims=True)

    me = meta[2]
    for k in (1, 0):
        out = send_out if k else keep_out
        for xr in (1, 0):
            xa, ca = chunk_at(meta, k, xr)
            down = nn(act_t[aligned(xa * (ff // 2) + ca * (ff // 4), ff // 4), :], grad).astype(BF)
            up = nn(n2_t[aligned(xa * (width // 2), width // 2), :], pre_low[:, aligned(ca * (ff // 2), ff // 2)])
            up = up.astype(BF)
            for a in range(8):
                out[xr, a ^ me, 0:64, :] = down[a * 64 : (a + 1) * 64]
                out[xr, a ^ me, 64:128, :] = up[(a % 4) * 64 : (a % 4 + 1) * 64, (a // 4) * 512 : (a // 4 + 1) * 512]


def backward_kernel(
    meta, h2g, hidden1, q, crossed, shares, kvt, att, enc, gains, shifts, extra_in,
    own_out, own_query, own_cross, near2, far2,
    h1g_out, att_grad_out, kv_keep, kv_send, extra_out, keep_out, send_out,
    w_out, w_query, w_cross, dc, dq, n1_t, part, enc_t, sems,
):
    width = h2g.shape[1]
    seqs, unused, rows = att.shape
    hd = width // H
    enc_rows = enc.shape[1]
    scale = 1.0 / math.sqrt(hd)
    put = Placer(sems, meta[0], meta[1])
    half = own_out.shape[0] // 2
    c_cross = put.lay(own_cross, near2, far2, w_cross, 4 * half, 1)
    c_query = put.lay(own_query, near2, far2, w_query, 3 * half, 1)
    c_out = put.lay(own_out, near2, far2, w_out, 2 * half, 1)
    grad2 = h2g[...]
    low2 = grad2.astype(BF)
    wait(c_cross)
    dc[...] = nt(low2, w_cross[...]).astype(BF)
    for s in range(seqs):
        at = slice(s * rows, (s + 1) * rows)
        q_t = flip(q[at, :])
        dc_t = flip(dc[at, :])
        enc_t[s] = flip(enc[s])
        for h in range(H):
            head = slice(h * hd, (h + 1) * hd)
            low = shares[s * H + h]
            wide = low.astype(F32)
            share_grad = nn(dc[at, head], kvt[s, width + h * hd : width + (h + 1) * hd, :])
            mean = jnp.sum(wide * share_grad, axis=1, keepdims=True)
            score_grad = (wide * (share_grad - mean)).astype(BF)
            dq[at, head] = (nt(score_grad, kvt[s, head, :]) * scale).astype(BF)
            part[s, head, :] = (nn(q_t[head], score_grad) * scale).astype(BF)
            part[s, width + h * hd : width + (h + 1) * hd, :] = nn(dc_t[head], low).astype(BF)
    kv_keep[...] = part[:, :, 0 : enc_rows // 2]
    kv_send[...] = part[:, :, enc_rows // 2 :]
    xhat1, r1 = normalise(hidden1[...])
    n1_t[...] = flip((xhat1 * gains[1:2, :] + shifts[1:2, :]).astype(BF))
    wait(c_query)
    n1_grad = nt(dq[...], w_query[...])
    grad1 = grad2 + norm_back(n1_grad, gains[1:2, :], xhat1, r1)
    h1g_out[...] = grad1
    low1 = grad1.astype(BF)
    wait(c_out)
    for s in range(seqs):
        att_grad_out[s] = nt(w_out[...], low1[s * rows : (s + 1) * rows]).astype(BF)
    extra_out[...] = extra_in[...]
    last = extra_out.shape[0] - 10
    extra_out[last + 7 : last + 8, :] = jnp.sum(n1_grad * xhat1, axis=0, keepdims=True)
    extra_out[last + 8 : last + 9, :] = jnp.sum(n1_grad, axis=0, keepdims=True)
    row = lax.broadcasted_iota(jnp.int32, extra_out.shape, 0)
    more = jnp.zeros(extra_out.shape, F32)
    for s in range(seqs):
        token_sum = jnp.sum(grad1[s * rows : (s + 1) * rows], axis=0, keepdims=True)
        more = more + jnp.where(row == 2 + meta[5] + s, token_sum, 0.0)
    extra_out[...] += more

    me = meta[2]
    for k in (1, 0):
        out = send_out if k else keep_out
        for xr in (1, 0):
            xa, ca = chunk_at(meta, k, xr)
            at = aligned(xa * (width // 2) + ca * (width // 4), width // 4)
            outer = jnp.zeros((width // 4, width), F32)
            cross = jnp.zeros((width // 4, width), F32)
            keyval = jnp.zeros((width // 2, width), F32)
            for s in range(seqs):
                mine = slice(s * rows, (s + 1) * rows)
                outer = outer + nn(att[s, at, :], low1[mine])
                cross = cross + nn(crossed[s, at, :], low2[mine])
                keyval = keyval + nt(enc_t[s, aligned(xa * (width // 2), width // 2), :], part[s, aligned(ca * width, width), :])
            query = nn(n1_t[at, :], dq[...]).astype(BF)
            outer, cross, keyval = outer.astype(BF), cross.astype(BF), keyval.astype(BF)
            for a in range(8):
                out[xr, a ^ me, 0:16, :] = outer[a * 16 : (a + 1) * 16]
                out[xr, a ^ me, 16:32, :] = query[a * 16 : (a + 1) * 16]
                out[xr, a ^ me, 32:48, :] = cross[a * 16 : (a + 1) * 16]
                out[xr, a ^ me, 48:80, :] = keyval[a * 32 : (a + 1) * 32]


def start_kernel(meta, grads, tokens, steps, gains, h1g, own, near, far, grad_out, weight, turned, sems):
    seqs, rows, width = tokens.shape
    hd = width // H
    put = Placer(sems, meta[0], meta[1])
    copies = put.lay(own, near, far, weight, 0, 3)
    for s in range(seqs):
        for h in range(H):
            for j in range(3):
                turned[s, j * width + h * hd : j * width + (h + 1) * hd, :] = grads[s, h, j * hd : (j + 1) * hd, :]
    wait(copies)
    for s in range(seqs):
        xhat, r = normalise(tokens[s].astype(F32) + steps[s : s + 1, :])
        grad = nt(flip(turned[s]), weight[...])
        grad_out[s] = h1g[s * rows : (s + 1) * rows, :] + norm_back(grad, gains[0:1, :], xhat, r)


def place_ffn_kernel(meta, *refs):
    pieces, (up_out, down_out) = refs[:-2], refs[-2:]
    c, me = meta[1], meta[2]
    for k, (core, mask, index) in enumerate(PIECES):
        block = pieces[k // 2][index].astype(F32)
        a = me ^ mask
        ca = c ^ core
        down_out[aligned(ca * 512 + a * 64, 64), :] = block[0:64]
        up_out[aligned((a % 4) * 64, 64), aligned(ca * 1024 + (a // 4) * 512, 512)] = block[64:128]


def place_cross_kernel(meta, *refs):
    pieces, (out_out, query_out, cross_out, keyval_out) = refs[:-4], refs[-4:]
    c, me = meta[1], meta[2]
    for k, (core, mask, index) in enumerate(PIECES):
        block = pieces[k // 2][index].astype(F32)
        a = me ^ mask
        ca = c ^ core
        at = aligned(ca * 128 + a * 16, 16)
        out_out[at, :] = block[0:16]
        query_out[at, :] = block[16:32]
        cross_out[at, :] = block[32:48]
        keyval_out[aligned(a * 32, 32), aligned(ca * 512, 512)] = block[48:80]


PIECES = [(core, mask + far, far) for core in (0, 1) for mask in (0, 2, 4, 6) for far in (0, 1)]


def place_joined_kernel(meta, *refs):
    pieces, (grad_out, extra_out, stacked) = refs[:-3], refs[-3:]
    low = meta[6]
    total = jnp.zeros(extra_out.shape, F32)
    hd = 64
    for k, mask in enumerate((0, 4, 2, 6, 1, 5, 3, 7)):
        block = pieces[k][...].astype(F32)
        head = low ^ mask
        for j in range(3):
            stacked[aligned(j * H * hd + head * hd, hd), :] = block[j * hd : (j + 1) * hd]
        total = total + block[3 * hd :]
    extra_out[...] = total
    for b in range(3):
        grad_out[:, b * 512 : (b + 1) * 512] = flip(stacked[b * 512 : (b + 1) * 512, :])


def over_ctx(value, mask):
    return lax.ppermute(value, "ctx", [(i, i ^ mask) for i in range(16)])


def over_x(value):
    return lax.ppermute(value, "fsdp", [(0, 1), (1, 0)])


def half_rows(weight, c):
    half = weight.shape[0] // 2
    part = lax.dynamic_slice_in_dim(weight, c * half, half, 0)
    return [part[:, b : b + 512] for b in range(0, weight.shape[1], 512)]


def fetch_group(weights, c):
    near = over_x(jnp.concatenate([p for w in weights for p in half_rows(w, c)], axis=0))
    return near, over_ctx(near, 1)


def add_low(*terms):
    return sum(t.astype(F32) for t in terms).astype(BF)


def reduce_blocks(keep, send):
    got = over_ctx(send, 1)
    got_x = over_x(add_low(keep[1], got[1]))
    kept = add_low(keep[0], got[0], got_x)
    kept = add_low(kept[0:4], over_ctx(kept[4:8], 2))
    kept = add_low(kept[0:2], over_ctx(kept[2:4], 4))
    return add_low(kept[0], over_ctx(kept[1], 8))


def gather_blocks(block):
    pair = jnp.stack([block, over_ctx(block, 8)])
    pieces = [pair] + [over_ctx(pair, mask) for mask in (4, 2, 6)]
    return pieces + [over_ctx(piece, 1) for piece in pieces]


def shards(
    tokens, encoder, step_ids, out_grad, self_in, self_out, cross_query, cross_keyval, cross_out,
    ffn_up, up_bias, ffn_down, down_bias, norm_gain, norm_shift, step_table,
):
    nctx, nx = lax.axis_size("ctx"), lax.axis_size("fsdp")
    i, x = lax.axis_index("ctx"), lax.axis_index("fsdp")
    seqs, rows, width = tokens.shape
    hd = width // H
    units = seqs * H
    rep = nctx // units
    unit = i // rep
    s_mine, head = unit // H, unit % H
    n = rows * nctx
    ff = 2048
    fast = nctx == 16 and nx == 2
    steps_count = step_table.shape[0]
    slots = seqs * nx
    extra_rows = -(-(slots + 12) // 16) * 16
    zero = jnp.int32(0)

    def small_rows(w):
        by_head = w.reshape(w.shape[0], 3, H, hd)
        mine = lax.dynamic_index_in_dim(by_head, head, 2, False).reshape(w.shape[0], 3 * hd)
        return mine.T

    if fast:
        c = i & 1
        me = ((i >> 1) & 1) * 4 + ((i >> 2) & 1) * 2 + ((i >> 3) & 1)
        ids = jnp.pad(step_ids.astype(BF)[None, :], ((0, 0), (0, width // 2 - seqs)))
        small = jnp.concatenate(
            [norm_gain, norm_shift, step_table, down_bias[None, :], up_bias.reshape(4, width // 2), ids,
             jnp.zeros((2, width // 2), BF)], axis=0)
        wh_own = small_rows(self_in)
        other_small = over_x(jnp.concatenate([wh_own, small], axis=0))
        wh_other = other_small[: 3 * hd]
        other = other_small[3 * hd :]
        swap = x == 1
        first = jnp.where(swap, other, small)
        second = jnp.where(swap, small, other)
        both = jnp.concatenate([first, second], axis=1)
        gains, shifts = both[0:3].astype(F32), both[3:6].astype(F32)
        table = both[6 : 6 + steps_count]
        bias_d = both[6 + steps_count : 7 + steps_count].astype(F32)
        at = 7 + steps_count
        bias_u = jnp.concatenate([first[at : at + 4].reshape(1, ff // 2), second[at : at + 4].reshape(1, ff // 2)], axis=1)
        bias_u = bias_u.astype(F32)
        all_ids = jnp.concatenate([first[at + 4, :seqs], second[at + 4, :seqs]])

        mine = lax.dynamic_index_in_dim(tokens, s_mine, 0, False)
        others = lax.dynamic_index_in_dim(tokens, 1 - s_mine, 0, False)
        got = over_ctx(others, 8)
        near = [mine] + [over_ctx(mine, mask) for mask in (4, 2, 6)]
        far = [got] + [over_ctx(got, mask) for mask in (4, 2, 6)]
        even = jnp.stack(near + far)
        odd = over_ctx(even, 1)
        place = i ^ jnp.array([0, 4, 2, 6, 8, 12, 10, 14, 1, 5, 3, 7, 9, 13, 11, 15], jnp.int32)

        enc8 = over_ctx(encoder, 8)
        pair = jnp.stack([encoder, enc8])
        through = {mask: over_ctx(pair, mask) for mask in (4, 2, 6)}
        enc_even = jnp.concatenate([pair, through[4], through[2], through[6]], axis=0)
        enc_all = jnp.concatenate([enc_even, over_ctx(enc_even, 1)], axis=0)
        enc_all = enc_all.transpose(1, 0, 2, 3).reshape(seqs, -1, width)

        own = dict(keyval=cross_keyval, out=self_out, query=cross_query, cross=cross_out, up=ffn_up, down=ffn_down, joined=self_in)
        near2, far2 = fetch_group([cross_keyval, self_out, cross_query, cross_out], c)
        near3, far3 = fetch_group([ffn_up, ffn_down], c)
        near4, far4 = fetch_group([self_in], c)
        xk, first_slot = x, seqs * x
    else:
        c, me, xk, first_slot = zero, zero, zero, seqs * x

        def gather(w, axis=0):
            return lax.all_gather(w, "fsdp", axis=axis, tiled=True)

        gains, shifts = gather(norm_gain, 1).astype(F32), gather(norm_shift, 1).astype(F32)
        table = gather(step_table, 1)
        bias_d, bias_u = gather(down_bias)[None, :].astype(F32), gather(up_bias)[None, :].astype(F32)
        all_ids = gather(step_ids.astype(BF))
        full = dict(keyval=gather(cross_keyval), out=gather(self_out), query=gather(cross_query), cross=gather(cross_out),
                    up=gather(ffn_up), down=gather(ffn_down), joined=gather(self_in))
        half_of = {name: w.shape[0] // 2 for name, w in full.items()}
        own = {name: w[: half_of[name]] for name, w in full.items()}

        def group(names, which):
            parts = []
            for name in names:
                rest = full[name][half_of[name] :]
                quarter = half_of[name] // 2
                part = rest[which * quarter : (which + 1) * quarter]
                parts += [part[:, b : b + 512] for b in range(0, part.shape[1], 512)]
            return jnp.concatenate(parts, axis=0)

        near2, far2 = (group(["keyval", "out", "query", "cross"], w) for w in (0, 1))
        near3, far3 = (group(["up", "down"], w) for w in (0, 1))
        near4, far4 = (group(["joined"], w) for w in (0, 1))
        wh = small_rows(full["joined"])
        wh_own, wh_other = wh[:, : width // 2], wh[:, width // 2 :]
        every = lax.all_gather(tokens, "ctx", axis=0, tiled=False)
        chosen = lax.dynamic_index_in_dim(every, s_mine, 1, False)
        even, odd = chosen[: nctx // 2], chosen[nctx // 2 :]
        place = jnp.arange(nctx, dtype=jnp.int32)
        enc_all = lax.all_gather(encoder, "ctx", axis=1, tiled=True)

    active = (i % rep == 0).astype(jnp.int32)
    slot = first_slot + s_mine
    meta = jnp.stack([xk, c, me, active, slot, jnp.int32(first_slot), i & 7, zero]).astype(jnp.int32)
    onehot = (jnp.arange(steps_count, dtype=jnp.int32)[None, :] == step_ids[:, None]).astype(BF)
    steps = jnp.dot(onehot, table, preferred_element_type=F32)
    step_mine = lax.dynamic_index_in_dim(steps, s_mine, 0, True)

    xhat0, joined, heads, attended_full, stats = call(
        attend_kernel, "attend",
        [((n, width), BF), ((3 * hd, n), BF), ((nctx, hd, rows), BF), ((hd, n), F32), ((8, n), F32)],
        [SM, SM] + [VM] * 7,
        [pltpu.VMEM((3 * hd, width), BF), pltpu.VMEM((n, width), BF), pltpu.VMEM((n, hd), BF)],
        (meta, place, even, odd, step_mine, gains[0:1], shifts[0:1], wh_own, wh_other),
        2 * n * width * 3 * hd + 4 * n * n * hd, 8 * n * width, n * n,
    )
    back = lax.all_to_all(heads, "ctx", 0, 0, tiled=True)
    att = back.reshape(units, rep, hd, rows)[:, 0].reshape(seqs, width, rows)

    kvt, w_keyval = call(
        encoder_kernel, "encoder_rows",
        [((seqs, 2 * width, enc_all.shape[1]), BF), ((width, 2 * width), BF)],
        [SM, VM, ANY, ANY, ANY],
        [pltpu.SemaphoreType.DMA((5,))],
        (meta, enc_all, own["keyval"], near2, far2),
        4 * seqs * enc_all.shape[1] * width * width, 4 << 20,
    )

    tall = seqs * rows
    enc_rows = enc_all.shape[1]
    mixed, h2g, hidden1, q, crossed, shares, extra1, f_keep, f_send = call(
        forward_kernel, "forward",
        [((seqs, rows, width), BF), ((tall, width), F32), ((tall, width), F32), ((tall, width), BF), ((seqs, width, rows), BF),
         ((units, rows, enc_rows), BF), ((extra_rows, width), F32), ((2, 8, 128, width), BF), ((2, 8, 128, width), BF)],
        [SM] + [VM] * 9 + [ANY] * 9,
        [pltpu.VMEM((width, width), BF)] * 3
        + [pltpu.VMEM((width, ff), BF), pltpu.VMEM((ff, width), BF), pltpu.VMEM((ff, tall), BF),
           pltpu.VMEM((width, tall), BF), pltpu.VMEM((tall, ff), BF), pltpu.SemaphoreType.DMA((21,))],
        (meta, tokens, steps, att, kvt, gains, shifts, bias_u, bias_d, out_grad,
         own["out"], own["query"], own["cross"], own["up"], own["down"], near2, far2, near3, far3),
        2 * tall * width * (2 * width + 2 * enc_rows + 6 * ff), 24 << 20, tall * (H * enc_rows + ff),
    )
    h1g, att_grad, kv_keep, kv_send, extra2, c_keep, c_send = call(
        backward_kernel, "backward",
        [((tall, width), F32), ((seqs, width, rows), BF), ((seqs, 2 * width, enc_rows // 2), BF),
         ((seqs, 2 * width, enc_rows // 2), BF), ((extra_rows, width), F32), ((2, 8, 80, width), BF), ((2, 8, 80, width), BF)],
        [SM] + [VM] * 11 + [ANY] * 5,
        [pltpu.VMEM((width, width), BF)] * 3
        + [pltpu.VMEM((tall, width), BF), pltpu.VMEM((tall, width), BF), pltpu.VMEM((width, tall), BF),
           pltpu.VMEM((seqs, 2 * width, enc_rows), BF), pltpu.VMEM((seqs, width, enc_rows), BF), pltpu.SemaphoreType.DMA((9,))],
        (meta, h2g, hidden1, q, crossed, shares, kvt, att, enc_all, gains, shifts, extra1,
         own["out"], own["query"], own["cross"], near2, far2),
        2 * tall * width * (6 * width + 4 * enc_rows) + 4 * seqs * enc_rows * width * width, 24 << 20, 0,
    )

    by_unit = att_grad.reshape(units, 1, hd, rows)
    grads = lax.all_to_all(jnp.broadcast_to(by_unit, (units, rep, hd, rows)).reshape(nctx, hd, rows), "ctx", 0, 0, tiled=True)
    joined_grad, u_keep, u_send = call(
        attend_back_kernel, "attend_back",
        [((nctx, 3 * hd, rows), BF), ((3 * hd + extra_rows, width // 2), F32), ((3 * hd + extra_rows, width // 2), BF)],
        [SM] + [VM] * 10,
        [pltpu.VMEM((3 * hd, width), BF), pltpu.VMEM((n, hd), BF), pltpu.VMEM((n, hd), BF), pltpu.VMEM((hd, n), BF),
         pltpu.VMEM((3 * hd + 16, n), BF), pltpu.VMEM((hd, n), F32), pltpu.VMEM((3 * hd + extra_rows, width), F32)],
        (meta, joined, attended_full, stats, grads, xhat0, gains[0:1], shifts[0:1], wh_own, wh_other, extra2),
        10 * n * n * hd + 2 * n * width * 3 * hd, 8 << 20, n * n,
    )
    dj = lax.all_to_all(joined_grad, "ctx", 0, 0, tiled=True)
    dj = dj.reshape(units, rep, 3 * hd, rows)[:, 0].reshape(seqs, H, 3 * hd, rows)
    (tokens_grad,) = call(
        start_kernel, "start_grad",
        [((seqs, rows, width), F32)],
        [SM] + [VM] * 5 + [ANY] * 3,
        [pltpu.VMEM((width, 3 * width), BF), pltpu.VMEM((seqs, 3 * width, rows), BF), pltpu.SemaphoreType.DMA((7,))],
        (meta, dj, tokens, steps, gains, h1g, own["joined"], near4, far4),
        6 * tall * width * width, 6 << 20,
    )

    if fast:
        whole_u = add_low(u_keep, over_x(u_send))
        whole_u = add_low(whole_u, over_ctx(whole_u, 8))
        pieces = [whole_u] + [over_ctx(whole_u, mask) for mask in (4, 2, 6)]
        pieces = pieces + [over_ctx(piece, 1) for piece in pieces]
        self_in_grad, extra = call(
            place_joined_kernel, "place_joined",
            [((width // 2, 3 * width), F32), ((extra_rows, width // 2), F32)],
            [SM] + [VM] * 8, [pltpu.VMEM((3 * width, width // 2), F32)], (meta, *pieces), 0, 4 << 20,
        )
        kv = over_ctx(kv_send, 1)
        wide = enc_rows // 4
        got = over_ctx(add_low(kv_keep[:, :, wide:], kv[:, :, wide:]), 2)
        kv = add_low(kv_keep[:, :, :wide], kv[:, :, :wide], got).transpose(0, 2, 1)
        kv = add_low(kv[:, : wide // 2], over_ctx(kv[:, wide // 2 :], 4))
        kv = add_low(kv[:, : wide // 4], over_ctx(kv[:, wide // 4 :], 8))
        f_pieces = gather_blocks(reduce_blocks(f_keep, f_send))
        c_pieces = gather_blocks(reduce_blocks(c_keep, c_send))
        up_grad, down_grad = call(
            place_ffn_kernel, "place_ffn", [((width // 2, ff), F32), ((ff // 2, width), F32)],
            [SM] + [VM] * 8, [], (meta, *f_pieces), 0, 8 << 20,
        )
        out_g, query_g, cross_g, keyval_g = call(
            place_cross_kernel, "place_cross",
            [((width // 2, width), F32)] * 3 + [((width // 2, 2 * width), F32)],
            [SM] + [VM] * 8, [], (meta, *c_pieces), 0, 6 << 20,
        )
        bias_row = extra_rows - 10
        up_bias_grad = extra[bias_row + 1 : bias_row + 5].reshape(-1)
        down_bias_grad = extra[bias_row]
    else:
        def scatter(g, axis=0):
            return lax.psum(lax.psum_scatter(g, "fsdp", scatter_dimension=axis, tiled=True), "ctx")

        f_all = jnp.stack([f_keep, f_send], axis=1)
        c_all = jnp.stack([c_keep, c_send], axis=1)
        down_g = scatter(f_all[..., 0:64, :].reshape(ff, width).astype(F32))
        up_g = f_all[..., 64:128, :].reshape(2, 2, 2, 4, 64, width).transpose(0, 3, 4, 1, 2, 5)
        up_grad, down_grad = scatter(up_g.reshape(width, ff).astype(F32)), down_g
        out_g, query_g, cross_g = (scatter(c_all[..., k : k + 16, :].reshape(width, width).astype(F32)) for k in (0, 16, 32))
        keyval_g = scatter(c_all[..., 48:80, :].transpose(0, 2, 3, 1, 4).reshape(width, 2 * width).astype(F32))
        kv = jnp.concatenate([kv_keep, kv_send], axis=2).transpose(0, 2, 1)
        kv = lax.psum_scatter(kv, "ctx", scatter_dimension=1, tiled=True)
        u = jnp.concatenate([u_keep, u_send.astype(F32)], axis=1)
        every_u = lax.all_gather(lax.psum(u[: 3 * hd], "fsdp"), "ctx", axis=0, tiled=False)
        by_head = every_u.reshape(seqs, H, rep, 3, hd, width).sum(axis=(0, 2))
        joined_g = by_head.transpose(3, 1, 0, 2).reshape(width, 3 * width) if False else by_head.transpose(3, 1, 0, 2).reshape(width, 3 * width)
        self_in_grad = lax.dynamic_slice_in_dim(joined_g, x * self_in.shape[0], self_in.shape[0], 0)
        sums = lax.psum(u[3 * hd :], ("ctx", "fsdp"))
        part = norm_gain.shape[1]
        extra = lax.dynamic_slice_in_dim(sums, x * part, part, 1)
        bias_row = extra_rows - 10
        down_bias_grad = extra[bias_row]
        up_all = sums[bias_row + 1 : bias_row + 5].reshape(4, 2, width // 2).transpose(1, 0, 2).reshape(-1)
        up_bias_grad = lax.dynamic_slice_in_dim(up_all, x * up_bias.shape[0], up_bias.shape[0], 0)

    enc_grad = jnp.einsum("sre,de->srd", kv, w_keyval, preferred_element_type=F32)
    gain_grad = jnp.stack([extra[0], extra[bias_row + 7], extra[bias_row + 5]])
    shift_grad = jnp.stack([extra[1], extra[bias_row + 8], extra[bias_row + 6]])
    hot = (jnp.arange(steps_count, dtype=jnp.int32).astype(F32)[:, None, None] == all_ids.astype(F32)[None, :, None]).astype(F32)
    table_grad = jnp.sum(hot * extra[None, 2 : 2 + slots, :], axis=1)
    return (
        mixed, tokens_grad, enc_grad, self_in_grad, out_g, query_g, keyval_g, cross_g, up_grad, up_bias_grad,
        down_grad, down_bias_grad, gain_grad, shift_grad, table_grad,
    )


def solution(mesh):
    tok = P("fsdp", "ctx", None)
    row, vec, col = P("fsdp", None), P("fsdp"), P(None, "fsdp")
    in_specs = (tok, tok, vec, tok, row, row, row, row, row, row, vec, row, vec, col, col, col)
    out_specs = (tok, tok, tok, row, row, row, row, row, row, vec, row, vec, col, col, col)
    return jax.shard_map(shards, mesh=mesh, in_specs=in_specs, out_specs=out_specs, check_vma=False)
```

```python
import functools
import math

import jax
import jax.numpy as jnp
from jax import lax
from jax.experimental import pallas as pl
from jax.experimental.pallas import tpu as pltpu
from jax.sharding import PartitionSpec as P

H = 8
EPS = 1e-05
F32 = jnp.float32
BF = jnp.bfloat16
LOG2E = 1.4426950408889634
VMEM_LIMIT = 56 * 1024 * 1024


def nn(a, b):
    return lax.dot_general(a, b, (((1,), (0,)), ((), ())), preferred_element_type=F32)


def nt(a, b):
    return lax.dot_general(a, b, (((1,), (1,)), ((), ())), preferred_element_type=F32)


def flip(v):
    return jnp.transpose(v)


def normalise(v):
    centred = v - jnp.mean(v, axis=-1, keepdims=True)
    r = lax.rsqrt(jnp.mean(centred * centred, axis=-1, keepdims=True) + EPS)
    return centred * r, r


def norm_back(grad, gain, xhat, r):
    u = grad * gain
    return r * (u - jnp.mean(u, axis=-1, keepdims=True) - xhat * jnp.mean(u * xhat, axis=-1, keepdims=True))


def aligned(index, size):
    return pl.ds(pl.multiple_of(index, size), size)


VM = pl.BlockSpec(memory_space=pltpu.VMEM)
SM = pl.BlockSpec(memory_space=pltpu.SMEM)
ANY = pl.BlockSpec(memory_space=pl.ANY)


TOOK = dict(
    split=1.7, prepare=2.0, pack=3.7, unpack=1.7, attend=15.0, encoder_rows=6.0, forward=15.0, cross_back=10.6, hidden_back=4.0,
    weights_back=7.2, attend_back_1=8.4, attend_back_2=10.3, start_grad=5.0, encoder_back=2.8, place=5.0, place_cross=3.1,
)
PER_MICROSECOND = 3_500_000


def cost_of(name):
    return pl.CostEstimate(flops=0, bytes_accessed=int(TOOK.get(name, 2.5) * PER_MICROSECOND), transcendentals=0)


def call(kernel, name, outs, in_specs, scratch, args, out_specs=None, after=(), grid=()):
    count = len(in_specs)

    def body(*refs):
        kernel(*refs[:count], *refs[count + len(after) :])

    return pl.pallas_call(
        body,
        name=name,
        grid=grid,
        out_shape=[jax.ShapeDtypeStruct(s, d) for s, d in outs],
        in_specs=list(in_specs) + [ANY] * len(after),
        out_specs=out_specs or [VM] * len(outs),
        scratch_shapes=scratch,
        compiler_params=pltpu.CompilerParams(vmem_limit_bytes=VMEM_LIMIT),
        cost_estimate=cost_of(name),
    )(*args, *after)


class Placer:
    def __init__(self, sems, x, c):
        self.sems, self.x, self.c, self.used = sems, x, c, 0

    def copy(self, src, dst):
        copy = pltpu.make_async_copy(src, dst, self.sems.at[self.used])
        self.used += 1
        copy.start()
        return copy

    def lay(self, own, near, far, dst, row0, blocks):
        rows = own.shape[0]
        half = rows // 2
        base = (1 - self.x) * rows
        copies = [self.copy(own, dst.at[aligned(self.x * rows, rows)])]
        for b in range(blocks):
            cols = pl.ds(b * 512, 512)
            part = pl.ds(row0 + b * half, half)
            copies.append(self.copy(near.at[part], dst.at[aligned(base + self.c * half, half), cols]))
            copies.append(self.copy(far.at[part], dst.at[aligned(base + (1 - self.c) * half, half), cols]))
        return copies


def wait(copies):
    for copy in copies:
        copy.wait()


def split_kernel(meta, tokens, encoder, mine, others):
    rows, span = tokens.shape[1], encoder.shape[1]
    for out, s in ((others, 1 - meta[9]), (mine, meta[9])):
        out[0:rows, :] = tokens[s]
        for k in range(encoder.shape[0]):
            out[rows + k * span : rows + (k + 1) * span, :] = encoder[k]


ORDER = (0, 4, 2, 6, 8, 12, 10, 14, 1, 5, 3, 7, 9, 13, 11, 15)


def attend_kernel(meta, step, gains, shifts, wh, *refs):
    blocks, (xhat_out, joined_out, heads_out, full_out, stats_out, normed, keys) = refs[:-7], refs[-7:]
    n, width = xhat_out.shape
    hd = joined_out.shape[0] // 3
    rows = heads_out.shape[2]
    stats_out[...] = jnp.zeros_like(stats_out)
    for k, block in enumerate(blocks):
        xhat, r = normalise(block[0:rows, :].astype(F32) + step[...])
        at = aligned((meta[7] ^ ORDER[k] if len(blocks) == 16 else k) * rows, rows)
        xhat_out[at, :] = xhat.astype(BF)
        normed[at, :] = (xhat * gains[0:1, :] + shifts[0:1, :]).astype(BF)
        stats_out[1:2, at] = flip(jnp.broadcast_to(r, (rows, 128)))[0:1, :]
    for b in range(n // 512):
        cols = pl.ds(b * 512, 512)
        joined_out[:, cols] = nt(wh[...], normed[cols, :]).astype(BF)
    keys[...] = flip(joined_out[hd : 2 * hd, :].astype(F32)).astype(BF)
    factor = LOG2E / math.sqrt(hd)
    wide = 256

    def query_block(b, carry):
        cols = aligned(b * wide, wide)
        scores = nn(keys[...], joined_out[0:hd, cols]) * factor
        peak = jnp.max(scores, axis=0, keepdims=True)
        shares = jnp.exp2(scores - peak)
        total = jnp.sum(shares, axis=0, keepdims=True)
        out = nn(joined_out[2 * hd : 3 * hd, :], shares.astype(BF)) / total
        full_out[:, cols] = out
        stats_out[0:1, cols] = peak + jnp.log2(total)
        for part in range(wide // rows):
            heads_out[b * (wide // rows) + part] = out[:, part * rows : (part + 1) * rows].astype(BF)
        return carry

    lax.fori_loop(0, n // wide, query_block, 0)


def key_blocks(first, joined, full, stats, grads, keys, values, gout, key_grads, query_acc):
    n = full.shape[1]
    hd = joined.shape[0] // 3
    rows = grads.shape[2]
    span = keys.shape[0]
    scale = 1.0 / math.sqrt(hd)
    factor = LOG2E * scale
    for j in range(grads.shape[0]):
        gout[:, j * rows : (j + 1) * rows] = grads[j]
    mine = pl.ds(first, span)
    keys[...] = flip(joined[hd : 2 * hd, mine].astype(F32)).astype(BF)
    values[...] = flip(joined[2 * hd : 3 * hd, mine].astype(F32)).astype(BF)
    delta = jnp.sum(gout[...].astype(F32) * full[...], axis=0, keepdims=True)
    lse = stats[0:1, :]
    wide = 256

    def key_block(b, carry):
        at = aligned(b * wide, wide)
        queries = joined[0:hd, :]
        shares = jnp.exp2(nn(keys[at, :], queries) * factor - lse)
        share_grad = nn(values[at, :], gout[...])
        score_grad = (shares * (share_grad - delta)).astype(BF)
        key_grads[0:hd, at] = (nt(queries, score_grad) * scale).astype(BF)
        key_grads[hd : 2 * hd, at] = nt(gout[...], shares.astype(BF)).astype(BF)
        query_acc[...] += nn(joined[hd : 2 * hd, aligned(first + b * wide, wide)], score_grad)
        return carry

    lax.fori_loop(0, span // wide, key_block, 0)


def attend_back_first(joined, full, stats, grads, query_out, key_out, keys, values, gout):
    query_out[...] = jnp.zeros_like(query_out)
    key_blocks(0, joined, full, stats, grads, keys, values, gout, key_out, query_out)


def attend_back_second(
    meta, joined, full, stats, grads, query_in, key_in, xhat, gains, shifts, wh, extra, joined_grad_out, keep_out, send_out,
    keys, values, gout, key_grads, query_acc, lhs, whole,
):
    x, active, slot = meta[0], meta[3], meta[4]
    n, width = xhat.shape
    hd = joined.shape[0] // 3
    half = width // 2
    rows = grads.shape[2]
    scale = 1.0 / math.sqrt(hd)
    query_acc[...] = query_in[...]
    key_blocks(n // 2, joined, full, stats, grads, keys, values, gout, key_grads, query_acc)
    lhs[0:hd, :] = (query_acc[...] * scale).astype(BF)
    lhs[hd : 3 * hd, 0 : n // 2] = key_in[...]
    lhs[hd : 3 * hd, n // 2 :] = key_grads[...]
    for j in range(joined_grad_out.shape[0]):
        joined_grad_out[j] = lhs[0 : 3 * hd, j * rows : (j + 1) * rows]

    gain, shift = gains[0:1, :], shifts[0:1, :]
    grad = lhs[0 : 3 * hd, :].astype(F32)
    r = stats[1:2, :]
    weight = wh[...].astype(F32)
    bias = jnp.sum(weight * shift, axis=1, keepdims=True)
    mixed_mean = jnp.sum(grad * (joined[...].astype(F32) - bias), axis=0, keepdims=True) * (1.0 / width)
    tail = lhs.shape[0] - 3 * hd
    first = lax.broadcasted_iota(jnp.int32, (tail, n), 0) == 0
    lhs[3 * hd :, :] = jnp.where(first, mixed_mean * r, 0.0).astype(BF)
    product = nn(lhs[...], xhat[...])
    m = product[0 : 3 * hd]
    sums = jnp.sum(grad, axis=1, keepdims=True)
    scaled_sums = jnp.sum(grad * r, axis=1, keepdims=True)
    lead = gain * jnp.sum(weight * scaled_sums, axis=0, keepdims=True)
    start_sum = lead - jnp.mean(lead, axis=1, keepdims=True) - product[3 * hd : 3 * hd + 1]
    on = active.astype(F32)
    whole[0 : 3 * hd, :] = (m * gain + sums * shift) * on
    gain_grad = jnp.sum(weight * m, axis=0, keepdims=True) * on
    shift_grad = jnp.sum(weight * sums, axis=0, keepdims=True) * on
    row = lax.broadcasted_iota(jnp.int32, extra.shape, 0)
    more = jnp.where(row == 0, gain_grad, 0.0) + jnp.where(row == 1, shift_grad, 0.0)
    more = more + jnp.where(row == 2 + slot, start_sum * on, 0.0)
    whole[3 * hd :, :] = extra[...] + more
    keep_out[...] = whole[:, aligned(x * half, half)]
    send_out[...] = whole[:, aligned((1 - x) * half, half)].astype(BF)


def prepare_kernel(meta, ids, weight, gain, shift, table, down_bias, up_bias, out, turned, small):
    width = weight.shape[1] // 3
    hd = width // H
    pair, odd = meta[8] // 2, meta[8] % 2
    for j in range(3):
        turned[...] = flip(weight[:, aligned(j * width + pair * 2 * hd, 2 * hd)])
        out[j * hd : (j + 1) * hd, :] = turned[aligned(odd * hd, hd), :]
    small[...] = jnp.zeros_like(small)
    at = 0
    for part in (gain, shift, table):
        small[at : at + part.shape[0], :] = part[...].astype(F32)
        at += part.shape[0]
    half = small.shape[1]
    for part in (down_bias, up_bias):
        for q in range(part.shape[0] // half):
            small[at : at + 1, :] = part[q * half : (q + 1) * half].astype(F32).reshape(1, half)
            at += 1
    lane = lax.broadcasted_iota(jnp.int32, (1, small.shape[1]), 1)
    line = jnp.zeros((1, small.shape[1]), F32)
    for s in range(2):
        line = line + jnp.where(lane == s, ids[s].astype(F32), 0.0)
    small[at : at + 1, :] = line
    out[3 * hd :, :] = small[...].astype(BF)


def unpack_kernel(
    meta, ids, mine, other, wh_out, gains_out, shifts_out, steps_out, step_out, up_out, down_out, ids_out, both,
):
    x = meta[0]
    rows, half = mine.shape
    head_rows = wh_out.shape[0]
    count = rows - head_rows
    for part, at in ((mine, x), (other, 1 - x)):
        lanes = aligned(at * half, half)
        wh_out[:, lanes] = part[0:head_rows, :]
        both[:, lanes] = part[head_rows:, :].astype(F32)
    gains_out[...] = both[0:3, :]
    shifts_out[...] = both[3:6, :]
    for s in range(2):
        steps_out[s : s + 1, :] = both[pl.ds(6 + ids[s], 1), :]
    step_out[...] = both[pl.ds(6 + ids[meta[9]], 1), :]
    last = count - 8
    down_out[...] = both[last : last + 1, :]
    for q in range(4):
        line = both[last + 1 + q : last + 2 + q, :]
        up_out[:, q * half : (q + 1) * half] = line[:, 0:half]
        up_out[:, (4 + q) * half : (5 + q) * half] = line[:, half:]
    ids_out[...] = both[last + 5 : last + 6, :]


def encoder_kernel(meta, own, near, far, *refs):
    blocks, (enc_out, kvt_out, weight_out, sems) = refs[:-4], refs[-4:]
    put = Placer(sems, meta[0], meta[1])
    copies = put.lay(own, near, far, weight_out, 0, 2)
    rows = enc_out.shape[1] // len(blocks)
    first = blocks[0].shape[0] - enc_out.shape[0] * rows
    for k, block in enumerate(blocks):
        at = aligned((meta[7] ^ ORDER[k] if len(blocks) == 16 else k) * rows, rows)
        for s in range(enc_out.shape[0]):
            enc_out[s, at, :] = block[first + s * rows : first + (s + 1) * rows, :]
    wait(copies)
    for s in range(enc_out.shape[0]):
        for b in range(2):
            kv = nn(enc_out[s], weight_out[:, b * 512 : (b + 1) * 512])
            kvt_out[s, b * 512 : (b + 1) * 512, :] = flip(kv).astype(BF)


def pack_kernel(counts, meta, *refs):
    total = sum(counts)
    weights, outs, sems = refs[:total], refs[total:-1], refs[-1]
    copies = []
    index = 0
    for out, count in zip(outs, counts):
        at = 0
        for weight in weights[index : index + count]:
            half = weight.shape[0] // 2
            for b in range(weight.shape[1] // 512):
                src = weight.at[aligned(meta[1] * half, half), pl.ds(b * 512, 512)]
                copies.append(pltpu.make_async_copy(src, out.at[pl.ds(at, half)], sems.at[len(copies)]))
                copies[-1].start()
                at += half
        index += count
    wait(copies)


GROUPS = (("keyval", "out", "query", "cross", "up", "down"), ("joined",))


def chunk_at(meta, k, xr):
    x, c = meta[0], meta[1]
    return x ^ xr, c ^ k


def forward_kernel(
    meta, tokens, steps, att, kvt, gains, shifts, own_out, own_query, own_cross, near2, far2,
    h2_out, h1_out, q_out, crossed_out, shares_out, w_out, w_query, w_cross, sems,
):
    seqs, rows, width = tokens.shape
    hd = width // H
    put = Placer(sems, meta[0], meta[1])
    half = own_out.shape[0] // 2
    c_out = put.lay(own_out, near2, far2, w_out, 2 * half, 1)
    c_query = put.lay(own_query, near2, far2, w_query, 3 * half, 1)
    c_cross = put.lay(own_cross, near2, far2, w_cross, 4 * half, 1)
    factor = LOG2E / math.sqrt(hd)

    wait(c_out)
    for s in range(seqs):
        at = pl.ds(s * rows, rows)
        start = tokens[s].astype(F32) + steps[s : s + 1, :]
        h1_out[at, :] = start + nn(flip(att[s]), w_out[...])
    hidden1 = h1_out[...]
    xhat1, unused = normalise(hidden1)
    wait(c_query)
    q_out[...] = nn((xhat1 * gains[1:2, :] + shifts[1:2, :]).astype(BF), w_query[...]).astype(BF)
    for s in range(seqs):
        for first in range(0, H, TOGETHER):
            heads = range(first, first + TOGETHER)
            scores = [
                nn(q_out[s * rows : (s + 1) * rows, h * hd : (h + 1) * hd], kvt[s, h * hd : (h + 1) * hd, :]) * factor for h in heads
            ]
            peaks = [jnp.max(score, axis=1, keepdims=True) for score in scores]
            shares = [jnp.exp2(score - peak) for score, peak in zip(scores, peaks)]
            totals = [jnp.sum(share, axis=1, keepdims=True) for share in shares]
            lows = [(share * (1.0 / total)).astype(BF) for share, total in zip(shares, totals)]
            got = [nt(kvt[s, width + h * hd : width + (h + 1) * hd, :], low) for h, low in zip(heads, lows)]
            for k, h in enumerate(heads):
                shares_out[s * H + h] = lows[k]
                crossed_out[s, h * hd : (h + 1) * hd, :] = got[k].astype(BF)
    wait(c_cross)
    for s in range(seqs):
        at = pl.ds(s * rows, rows)
        h2_out[at, :] = h1_out[at, :] + nn(flip(crossed_out[s]), w_cross[...])


TOGETHER = 4


def feed_kernel(
    meta, hidden2_in, gains, shifts, up_bias, down_bias, out_grad, own_up, own_down, near2, far2,
    mixed_out, h2g_out, extra_out, down_keep, down_send, up_keep, up_send, w_up, w_down, act_t, n2_t, pre_low, sems,
):
    seqs, rows, width = out_grad.shape
    ff = w_down.shape[0]
    slots = extra_out.shape[0]
    put = Placer(sems, meta[0], meta[1])
    c_up = put.lay(own_up, near2, far2, w_up, 5 * (own_up.shape[0] // 2), 4)
    c_down = put.lay(own_down, near2, far2, w_down, 9 * (own_up.shape[0] // 2), 1)
    hidden2 = hidden2_in[...]
    xhat2, r2 = normalise(hidden2)
    n2 = (xhat2 * gains[2:3, :] + shifts[2:3, :]).astype(BF)
    n2_t[...] = flip(n2)
    grad = jnp.concatenate([out_grad[s] for s in range(seqs)], axis=0)
    top = grad.astype(F32)
    wait(c_up)
    wait(c_down)
    mixed = hidden2 + down_bias[...]
    n2_grad = jnp.zeros_like(hidden2)
    extra_out[...] = jnp.zeros_like(extra_out)
    root = math.sqrt(2.0 / math.pi)
    bias_row = slots - 10
    for b in range(ff // 512):
        cols = pl.ds(b * 512, 512)
        pre = nn(n2, w_up[:, cols]) + up_bias[:, cols]
        square = pre * pre
        bent = jnp.tanh(root * pre * (1.0 + 0.044715 * square))
        act = (0.5 * pre * (1.0 + bent)).astype(BF)
        slope = 0.5 * (1.0 + bent) + 0.5 * root * pre * (1.0 - bent * bent) * (1.0 + 3.0 * 0.044715 * square)
        mixed = mixed + nn(act, w_down[cols, :])
        act_t[cols, :] = flip(act)
        low = (nt(grad, w_down[cols, :]) * slope).astype(BF)
        pre_low[:, cols] = low
        n2_grad = n2_grad + nt(low, w_up[:, cols])
        sums = jnp.sum(low.astype(F32), axis=0, keepdims=True)
        per_half = ff // 512 // 2
        lanes = pl.ds((b // per_half) * 256, 256)
        for piece in range(2):
            row = bias_row + 1 + (b % per_half) * 2 + piece
            extra_out[row : row + 1, lanes] = sums[:, piece * 256 : (piece + 1) * 256]
    for s in range(seqs):
        mixed_out[s] = mixed[s * rows : (s + 1) * rows].astype(BF)
    h2g_out[...] = top + norm_back(n2_grad, gains[2:3, :], xhat2, r2)
    extra_out[bias_row : bias_row + 1, :] = jnp.sum(top, axis=0, keepdims=True)
    extra_out[bias_row + 5 : bias_row + 6, :] = jnp.sum(n2_grad * xhat2, axis=0, keepdims=True)
    extra_out[bias_row + 6 : bias_row + 7, :] = jnp.sum(n2_grad, axis=0, keepdims=True)

    me = meta[2]
    for k in (1, 0):
        down_out, up_out = (down_send, up_send) if k else (down_keep, up_keep)
        for xr in (1, 0):
            xa, ca = chunk_at(meta, k, xr)
            down = nn(act_t[aligned(xa * (ff // 2) + ca * (ff // 4), ff // 4), :], grad).astype(BF)
            up = nn(n2_t[aligned(xa * (width // 2), width // 2), :], pre_low[:, aligned(ca * (ff // 2), ff // 2)])
            up = up.astype(BF)
            for a in range(8):
                at = a ^ me
                down_out[xr * 8 + at] = down[a * 64 : (a + 1) * 64]
                up_out[(at // 4) * 8 + xr * 4 + at % 4] = up[(a % 4) * 64 : (a % 4 + 1) * 64, (a // 4) * 512 : (a // 4 + 1) * 512]


def cross_back_kernel(meta, h2g, q, shares, kvt, own_cross, near2, far2, dq_out, part_out, w_cross, dc, sems):
    width = h2g.shape[1]
    seqs, unused, enc_rows = kvt.shape
    rows = h2g.shape[0] // seqs
    hd = width // H
    scale = 1.0 / math.sqrt(hd)
    put = Placer(sems, meta[0], meta[1])
    half = own_cross.shape[0] // 2
    wait(put.lay(own_cross, near2, far2, w_cross, 4 * half, 1))
    dc[...] = nt(h2g[...].astype(BF), w_cross[...]).astype(BF)
    for s in range(seqs):
        at = slice(s * rows, (s + 1) * rows)
        q_t = flip(q[at, :])
        dc_t = flip(dc[at, :])
        for first in range(0, H, TOGETHER):
            heads = range(first, first + TOGETHER)
            lows = [shares[s * H + h] for h in heads]
            wides = [low.astype(F32) for low in lows]
            share_grads = [nn(dc[at, h * hd : (h + 1) * hd], kvt[s, width + h * hd : width + (h + 1) * hd, :]) for h in heads]
            means = [jnp.sum(wide * grad, axis=1, keepdims=True) for wide, grad in zip(wides, share_grads)]
            score_grads = [(wide * (grad - mean)).astype(BF) for wide, grad, mean in zip(wides, share_grads, means)]
            q_grads = [nt(grad, kvt[s, h * hd : (h + 1) * hd, :]) for h, grad in zip(heads, score_grads)]
            k_grads = [nn(q_t[h * hd : (h + 1) * hd], grad) for h, grad in zip(heads, score_grads)]
            v_grads = [nn(dc_t[h * hd : (h + 1) * hd], low) for h, low in zip(heads, lows)]
            for k, h in enumerate(heads):
                head = slice(h * hd, (h + 1) * hd)
                dq_out[at, head] = (q_grads[k] * scale).astype(BF)
                part_out[s, head, :] = (k_grads[k] * scale).astype(BF)
                part_out[s, width + h * hd : width + (h + 1) * hd, :] = v_grads[k].astype(BF)


def hidden_back_kernel(
    meta, h2g, hidden1, dq, gains, extra_in, own_out, own_query, near2, far2, h1g_out, att_grad_out, extra_out,
    w_out, w_query, sems,
):
    width = h2g.shape[1]
    seqs, unused, rows = att_grad_out.shape
    put = Placer(sems, meta[0], meta[1])
    half = own_out.shape[0] // 2
    c_query = put.lay(own_query, near2, far2, w_query, 3 * half, 1)
    c_out = put.lay(own_out, near2, far2, w_out, 2 * half, 1)
    xhat1, r1 = normalise(hidden1[...])
    wait(c_query)
    n1_grad = nt(dq[...], w_query[...])
    grad1 = h2g[...] + norm_back(n1_grad, gains[1:2, :], xhat1, r1)
    h1g_out[...] = grad1
    low1 = grad1.astype(BF)
    wait(c_out)
    for s in range(seqs):
        att_grad_out[s] = nt(w_out[...], low1[s * rows : (s + 1) * rows]).astype(BF)
    last = extra_out.shape[0] - 10
    row = lax.broadcasted_iota(jnp.int32, extra_out.shape, 0)
    more = jnp.where(row == last + 7, jnp.sum(n1_grad * xhat1, axis=0, keepdims=True), 0.0)
    more = more + jnp.where(row == last + 8, jnp.sum(n1_grad, axis=0, keepdims=True), 0.0)
    for s in range(seqs):
        token_sum = jnp.sum(grad1[s * rows : (s + 1) * rows], axis=0, keepdims=True)
        more = more + jnp.where(row == 2 + meta[5] + s, token_sum, 0.0)
    extra_out[...] = extra_in[...] + more


def weights_back_kernel(
    meta, h2g, h1g, hidden1, crossed, att, dq, part, enc, gains, shifts, keep1, send1, keep0, send0, kv_keep, kv_send,
    n1_t, enc_t, part_t,
):
    width = h2g.shape[1]
    seqs, unused, rows = att.shape
    xhat1, unused = normalise(hidden1[...])
    n1_t[...] = flip((xhat1 * gains[1:2, :] + shifts[1:2, :]).astype(BF))
    low2, low1 = h2g[...].astype(BF), h1g[...].astype(BF)
    enc_rows = enc.shape[1]
    span = enc_rows // 16
    for s in range(seqs):
        enc_t[s] = flip(enc[s])
        part_t[s] = flip(part[s])
    for k in (1, 0):
        out = kv_send if k else kv_keep
        for at in range(8):
            a = at ^ meta[2]
            first = aligned(((a & 1) * 8 + (a & 2) * 2 + (a & 4) // 2 + (meta[1] ^ k)) * span, span)
            for s in range(seqs):
                for j in range(2):
                    row = (s * 2 + j) * span
                    out[at, row : row + span, :] = part_t[s, first, j * width : (j + 1) * width]
    me = meta[2]
    for k in (1, 0):
        for xr in (1, 0):
            out = ((keep0, keep1), (send0, send1))[k][xr]
            xa, ca = chunk_at(meta, k, xr)
            at = aligned(xa * (width // 2) + ca * (width // 4), width // 4)
            outer = jnp.zeros((width // 4, width), F32)
            cross = jnp.zeros((width // 4, width), F32)
            keyval = jnp.zeros((width // 2, width), F32)
            for s in range(seqs):
                mine = slice(s * rows, (s + 1) * rows)
                outer = outer + nn(att[s, at, :], low1[mine])
                cross = cross + nn(crossed[s, at, :], low2[mine])
                keyval = keyval + nt(enc_t[s, aligned(xa * (width // 2), width // 2), :], part[s, aligned(ca * width, width), :])
            query = nn(n1_t[at, :], dq[...]).astype(BF)
            outer, cross, keyval = outer.astype(BF), cross.astype(BF), keyval.astype(BF)
            for a in range(8):
                out[a ^ me, 0:16, :] = outer[a * 16 : (a + 1) * 16]
                out[a ^ me, 16:32, :] = query[a * 16 : (a + 1) * 16]
                out[a ^ me, 32:48, :] = cross[a * 16 : (a + 1) * 16]
                out[a ^ me, 48:80, :] = keyval[a * 32 : (a + 1) * 32]


def start_kernel(meta, grads, tokens, steps, gains, h1g, own, near, far, grad_out, weight, turned, sems):
    seqs, rows, width = tokens.shape
    hd = width // H
    put = Placer(sems, meta[0], meta[1])
    copies = put.lay(own, near, far, weight, 0, 3)
    for s in range(seqs):
        for h in range(H):
            for j in range(3):
                turned[s, j * width + h * hd : j * width + (h + 1) * hd, :] = grads[s, h, j * hd : (j + 1) * hd, :]
    wait(copies)
    for s in range(seqs):
        xhat, r = normalise(tokens[s].astype(F32) + steps[s : s + 1, :])
        grad = nt(flip(turned[s]), weight[...])
        grad_out[s] = h1g[s * rows : (s + 1) * rows, :] + norm_back(grad, gains[0:1, :], xhat, r)


PIECES = [(core, mask + far, far) for core in (0, 1) for mask in (0, 2, 4, 6) for far in (0, 1)]


def place_cross_kernel(meta, *refs):
    pieces, (out_out, query_out, cross_out, keyval_out) = refs[:-4], refs[-4:]
    c, me = meta[1], meta[2]
    for k, (core, mask, index) in enumerate(PIECES):
        block = pieces[k // 2][index].astype(F32)
        a = me ^ mask
        ca = c ^ core
        at = aligned(ca * 128 + a * 16, 16)
        out_out[at, :] = block[0:16]
        query_out[at, :] = block[16:32]
        cross_out[at, :] = block[32:48]
        keyval_out[aligned(a * 32, 32), aligned(ca * 512, 512)] = block[48:80]


def encoder_back_kernel(kv, got, weight, out):
    seqs, span, width = out.shape
    total = (kv[0].astype(F32) + got[0].astype(F32)).astype(BF)
    for s in range(seqs):
        first = s * 2 * span
        keys = nt(total[first : first + span], weight[:, 0:width])
        out[s] = keys + nt(total[first + span : first + 2 * span], weight[:, width:])


def merge_kernel(feed, feed_got, heads, heads_got, out):
    rows = feed.shape[1]
    for k in range(2):
        total = feed[k].astype(F32) + feed_got[1 - k].astype(F32)
        out[0, k * rows : (k + 1) * rows, :] = total.astype(BF)
    total = heads[0].astype(F32) + heads_got[0].astype(F32)
    count, half = total.shape
    split = out.shape[1] - 2 * rows
    out[0, 2 * rows :, 0:half] = total[0:split].astype(BF)
    rest = jnp.concatenate([total[split:], jnp.zeros((2 * split - count, half), F32)], axis=0)
    out[0, 2 * rows :, half:] = rest.astype(BF)


def place_kernel(meta, ids, *refs):
    pieces = refs[:8]
    feed_up, feed_down, grad_out, gain_out, shift_out, table_out, down_out, up_out, stacked = refs[8:]
    c, me, low = meta[1], meta[2], meta[6]
    for k, (core, mask, index) in enumerate(PIECES):
        block = pieces[k // 2][0, index * 128 : (index + 1) * 128, :].astype(F32)
        a = me ^ mask
        ca = c ^ core
        feed_down[aligned(ca * 512 + a * 64, 64), :] = block[0:64]
        feed_up[aligned((a % 4) * 64, 64), aligned(ca * 1024 + (a // 4) * 512, 512)] = block[64:128]
    hd = 64
    half = grad_out.shape[0]
    total = jnp.zeros((16, half), F32)
    for k, mask in enumerate((0, 4, 2, 6, 1, 5, 3, 7)):
        wide = pieces[k][0, 256:368, :].astype(F32)
        block = jnp.concatenate([wide[:, 0:half], wide[0:96, half:]], axis=0)
        head = low ^ mask
        for j in range(3):
            stacked[aligned(j * H * hd + head * hd, hd), :] = block[j * hd : (j + 1) * hd]
        total = total + block[3 * hd :]
    for b in range(3):
        grad_out[:, b * 512 : (b + 1) * 512] = flip(stacked[b * 512 : (b + 1) * 512, :])
    last = total.shape[0] - 10
    for row, (g, b) in enumerate(((0, 1), (last + 7, last + 8), (last + 5, last + 6))):
        gain_out[row : row + 1, :] = total[g : g + 1]
        shift_out[row : row + 1, :] = total[b : b + 1]
    down_out[...] = total[last : last + 1]
    up_out[...] = total[last + 1 : last + 5]
    step = lax.broadcasted_iota(jnp.int32, table_out.shape, 0).astype(F32)
    table = jnp.zeros(table_out.shape, F32)
    for k in range(4):
        lane = (k // 2) * half + k % 2
        table = table + jnp.where(step == ids[:, lane : lane + 1], total[2 + k : 3 + k], 0.0)
    table_out[...] = table


def sums(name, outs, after=()):
    arrays, specs, plan, shapes = [], [], [], []
    for groups in outs:
        rows = 0
        steps = []
        for terms in groups:
            spans = []
            for array, size, index, span, swap in terms:
                spans.append((len(arrays), span or (0, array.shape[1]), swap))
                arrays.append(array)
                specs.append(pl.BlockSpec((size,) + array.shape[1:], lambda g, index=index: (index, 0, 0)))
            high = spans[0][1][1] - spans[0][1][0]
            steps.append((rows, rows + high, spans))
            rows += high
        plan.append(steps)
        shapes.append((terms[0][1], rows, array.shape[2]))
    count = len(arrays)

    def kernel(*refs):
        results = refs[count + len(after) :]
        for out, steps in zip(results, plan):
            for low, high, spans in steps:
                total = None
                for k, (first, last), swap in spans:
                    value = refs[k][:, first:last, :].astype(F32)
                    if swap:
                        value = jnp.concatenate([value[1:2], value[0:1]], axis=0)
                    total = value if total is None else total + value
                out[:, low:high, :] = total.astype(BF)

    return pl.pallas_call(
        kernel,
        name=name,
        grid=(1,),
        out_shape=[jax.ShapeDtypeStruct(shape, BF) for shape in shapes],
        in_specs=specs + [ANY] * len(after),
        out_specs=[pl.BlockSpec(shape, lambda g: (0, 0, 0)) for shape in shapes],
        compiler_params=pltpu.CompilerParams(vmem_limit_bytes=VMEM_LIMIT),
        cost_estimate=cost_of(name),
    )(*arrays, *after)


def term(array, size, index, span=None, swap=False):
    return array, size, index, span, swap


def tie(value, *others):
    return lax.optimization_barrier((value,) + others)[0]


def over_ctx(value, mask):
    return lax.ppermute(value, "ctx", [(i, i ^ mask) for i in range(16)])


def over_x(value):
    return lax.ppermute(value, "fsdp", [(0, 1), (1, 0)])


def spread(piece, first=()):
    pieces = [piece] + [over_ctx(piece, mask) for mask in (4, 2, 6)]
    pieces = [tie(p, *first) for p in pieces]
    return pieces + [over_ctx(p, 1) for p in pieces]


def shards(
    tokens, encoder, step_ids, out_grad, self_in, self_out, cross_query, cross_keyval, cross_out,
    ffn_up, up_bias, ffn_down, down_bias, norm_gain, norm_shift, step_table,
):
    nctx, nx = lax.axis_size("ctx"), lax.axis_size("fsdp")
    i, x = lax.axis_index("ctx"), lax.axis_index("fsdp")
    seqs, rows, width = tokens.shape
    hd = width // H
    units = seqs * H
    rep = nctx // units
    unit = i // rep
    s_mine, head = unit // H, unit % H
    n = rows * nctx
    ff = 2048
    fast = nctx == 16 and nx == 2
    steps_count = step_table.shape[0]
    slots = seqs * nx
    extra_rows = -(-(slots + 12) // 16) * 16
    zero = jnp.int32(0)

    xk, c, me = zero, zero, zero
    if fast:
        xk, c, me = x, i & 1, ((i >> 1) & 1) * 4 + ((i >> 2) & 1) * 2 + ((i >> 3) & 1)
    active = (i % rep == 0).astype(jnp.int32)
    meta = jnp.stack([xk, c, me, active, seqs * x + s_mine, seqs * x, i & 7, i, head, s_mine]).astype(jnp.int32)

    if fast:
        mine, others = call(
            split_kernel, "split", [((rows + seqs * encoder.shape[1], width), BF)] * 2, [SM, VM, VM], [], (meta, tokens, encoder),
        )
        got = over_ctx(others, 8)
        blocks = [mine] + [over_ctx(mine, mask) for mask in (4, 2, 6)]
        blocks += [got] + [over_ctx(got, mask) for mask in (4, 2, 6)]
        blocks += [over_ctx(block, 1) for block in blocks]

        (small,) = call(
            prepare_kernel, "prepare", [((256, width // 2), BF)], [SM, SM] + [VM] * 6,
            [pltpu.VMEM((2 * hd, width // 2), BF), pltpu.VMEM((64, width // 2), F32)],
            (meta, step_ids, self_in, norm_gain, norm_shift, step_table, down_bias, up_bias),
            after=[mine],
        )
        own = dict(keyval=cross_keyval, out=self_out, query=cross_query, cross=cross_out, up=ffn_up, down=ffn_down, joined=self_in)

        weights = [own[name] for group in GROUPS for name in group]
        sizes = [sum(own[name].size for name in group) // 1024 for group in GROUPS]
        packed = call(
            functools.partial(pack_kernel, [len(group) for group in GROUPS]), "pack", [((size, 512), BF) for size in sizes],
            [SM] + [ANY] * len(weights), [pltpu.SemaphoreType.DMA((13,))], (meta, *weights), after=[small],
        )
        other_small = over_x(tie(small, packed[0], *blocks[1:5]))
        near2 = over_x(tie(packed[0], other_small))
        wh, gains, shifts, steps, step_mine, bias_u, bias_d, all_ids = call(
            unpack_kernel, "unpack",
            [((3 * hd, width), BF), ((3, width), F32), ((3, width), F32), ((seqs, width), F32), ((1, width), F32),
             ((1, ff), F32), ((1, width), F32), ((1, width), F32)],
            [SM, SM, VM, VM], [pltpu.VMEM((64, width), F32)], (meta, step_ids, small, other_small), after=[packed[0]],
        )
    else:
        def gather(w, axis=0):
            return lax.all_gather(w, "fsdp", axis=axis, tiled=True)

        gains, shifts = gather(norm_gain, 1).astype(F32), gather(norm_shift, 1).astype(F32)
        table = gather(step_table, 1)
        bias_d, bias_u = gather(down_bias)[None, :].astype(F32), gather(up_bias)[None, :].astype(F32)
        all_ids = gather(step_ids.astype(BF)).astype(F32)
        full = dict(keyval=gather(cross_keyval), out=gather(self_out), query=gather(cross_query), cross=gather(cross_out),
                    up=gather(ffn_up), down=gather(ffn_down), joined=gather(self_in))
        half_of = {name: w.shape[0] // 2 for name, w in full.items()}
        own = {name: w[: half_of[name]] for name, w in full.items()}

        def group(names, which):
            parts = []
            for name in names:
                rest = full[name][half_of[name] :]
                quarter = half_of[name] // 2
                part = rest[which * quarter : (which + 1) * quarter]
                parts += [part[:, b : b + 512] for b in range(0, part.shape[1], 512)]
            return jnp.concatenate(parts, axis=0)

        (near2, far2), (near4, far4) = ([group(names, w) for w in (0, 1)] for names in GROUPS)
        by_head = full["joined"].reshape(width, 3, H, hd)
        wh = lax.dynamic_index_in_dim(by_head, head, 2, False).reshape(width, 3 * hd).T
        onehot = (jnp.arange(steps_count, dtype=jnp.int32)[None, :] == step_ids[:, None]).astype(BF)
        steps = jnp.dot(onehot, table, preferred_element_type=F32)
        step_mine = lax.dynamic_index_in_dim(steps, s_mine, 0, True)
        every = lax.all_gather(tokens, "ctx", axis=0, tiled=False)
        chosen = lax.dynamic_index_in_dim(every, s_mine, 1, False)
        encs = lax.all_gather(encoder, "ctx", axis=0, tiled=False)
        blocks = [jnp.concatenate([chosen[j], encs[j].reshape(-1, width)], axis=0) for j in range(nctx)]
    xhat0, joined, heads, attended_full, stats = call(
        attend_kernel, "attend",
        [((n, width), BF), ((3 * hd, n), BF), ((nctx, hd, rows), BF), ((hd, n), F32), ((8, n), F32)],
        [SM] + [VM] * (4 + nctx),
        [pltpu.VMEM((n, width), BF), pltpu.VMEM((n, hd), BF)],
        (meta, step_mine, gains, shifts, wh, *blocks),
    )
    hold = []
    back = lax.all_to_all(heads, "ctx", 0, 0, tiled=True)
    if fast:
        far2 = over_ctx(tie(near2, heads), 1)
    att = back.reshape(units, rep, hd, rows)[:, 0].reshape(seqs, width, rows)

    enc_rows = nctx * encoder.shape[1]
    enc_all, kvt, w_keyval = call(
        encoder_kernel, "encoder_rows",
        [((seqs, enc_rows, width), BF), ((seqs, 2 * width, enc_rows), BF), ((width, 2 * width), BF)],
        [SM, ANY, ANY, ANY] + [VM] * nctx,
        [pltpu.SemaphoreType.DMA((5,))],
        (meta, own["keyval"], near2, far2, *blocks),
    )
    if fast:
        near4 = over_x(tie(packed[1], kvt))
        hold = [near4]

    tall = seqs * rows
    square = pltpu.VMEM((width, width), BF)
    hidden2, hidden1, q, crossed, shares = call(
        forward_kernel, "forward",
        [((tall, width), F32), ((tall, width), F32), ((tall, width), BF), ((seqs, width, rows), BF), ((units, rows, enc_rows), BF)],
        [SM] + [VM] * 6 + [ANY] * 5,
        [square] * 3 + [pltpu.SemaphoreType.DMA((9,))],
        (meta, tokens, steps, att, kvt, gains, shifts, own["out"], own["query"], own["cross"], near2, far2),
    )
    mixed, h2g, extra1, down_keep, down_send, up_keep, up_send = call(
        feed_kernel, "feed",
        [((seqs, rows, width), BF), ((tall, width), F32), ((extra_rows, width), F32)] + [((16, 64, width), BF)] * 4,
        [SM] + [VM] * 6 + [ANY] * 4,
        [pltpu.VMEM((width, ff), BF), pltpu.VMEM((ff, width), BF), pltpu.VMEM((ff, tall), BF),
         pltpu.VMEM((width, tall), BF), pltpu.VMEM((tall, ff), BF), pltpu.SemaphoreType.DMA((12,))],
        (meta, hidden2, gains, shifts, bias_u, bias_d, out_grad, own["up"], own["down"], near2, far2),
        after=hold,
    )
    hold = []
    if fast:
        far4 = over_ctx(tie(near4, h2g), 1)
        hold = [far4]
        down_got, up_got = over_ctx(down_send, 1), over_ctx(up_send, 1)
    dq, part = call(
        cross_back_kernel, "cross_back",
        [((tall, width), BF), ((seqs, 2 * width, enc_rows), BF)],
        [SM] + [VM] * 4 + [ANY] * 3,
        [square, pltpu.VMEM((tall, width), BF), pltpu.SemaphoreType.DMA((3,))],
        (meta, h2g, q, shares, kvt, own["cross"], near2, far2), after=hold,
    )
    hold = []
    if fast:
        down_x, up_y = sums(
            "reduce_1", [[[term(down_keep, 8, 1), term(down_got, 8, 1)]], [[term(up_keep, 8, 1), term(up_got, 8, 1)]]], [dq])
        down_x1, up_y1 = over_x(down_x), over_ctx(up_y, 2)
        hold = [down_x]
    h1g, att_grad, extra2 = call(
        hidden_back_kernel, "hidden_back",
        [((tall, width), F32), ((seqs, width, rows), BF), ((extra_rows, width), F32)],
        [SM] + [VM] * 5 + [ANY] * 4,
        [square, square, pltpu.SemaphoreType.DMA((6,))],
        (meta, h2g, hidden1, dq, gains, extra1, own["out"], own["query"], near2, far2),
        after=hold,
    )
    by_unit = att_grad.reshape(units, 1, hd, rows)
    grads = lax.all_to_all(jnp.broadcast_to(by_unit, (units, rep, hd, rows)).reshape(nctx, hd, rows), "ctx", 0, 0, tiled=True)
    keep1, send1, keep0, send0, kv_keep, kv_send = call(
        weights_back_kernel, "weights_back",
        [((8, 80, width), BF)] * 4 + [((8, enc_rows // 4, width), BF)] * 2,
        [SM] + [VM] * 10,
        [pltpu.VMEM((width, tall), BF), pltpu.VMEM((seqs, width, enc_rows), BF), pltpu.VMEM((seqs, enc_rows, 2 * width), BF)],
        (meta, h2g, h1g, hidden1, crossed, att, dq, part, enc_all, gains, shifts),
    )
    hold = []
    if fast:
        got1, got0, kv_0 = (over_ctx(tie(part, grads, down_x1, up_y1), 1) for part in (send1, send0, kv_send))

        def terms(arrays, size, index, whole=()):
            found = [term(array, size, index) for array in arrays]
            return found + [term(array, size, index, rows) for array, rows in whole]

        down_y, up_x = sums(
            "reduce_2", [[terms([down_keep, down_got, down_x1], 4, 1)], [terms([up_keep, up_got, up_y1], 4, 1)]], [grads, keep1],
        )
        down_y1, up_x1 = over_ctx(down_y, 2), over_x(up_x)
        hold = [down_y]

    head_scratch = [pltpu.VMEM((n // 2, hd), BF), pltpu.VMEM((n // 2, hd), BF), pltpu.VMEM((hd, n), BF)]
    query_acc, key_half = call(
        attend_back_first, "attend_back_1", [((hd, n), F32), ((2 * hd, n // 2), BF)], [VM] * 4, head_scratch,
        (joined, attended_full, stats, grads), after=hold,
    )
    hold = []
    if fast:
        downs, ups, kvs = [down_keep, down_got, down_x1, down_y1], [up_keep, up_got, up_y1, up_x1], [kv_keep, kv_0]
        feed_z, cross_x, kv_y = sums(
            "reduce_3", [[terms(downs, 2, 1), terms(ups, 2, 1)], [terms([keep1, got1], 8, 0)], [terms(kvs, 4, 1)]], [query_acc],
        )
        feed_z1, cross_x1, kv_1 = over_ctx(feed_z, 4), over_x(cross_x), over_ctx(kv_y, 2)
        kvs = kvs + [kv_1]
        hold = [feed_z]
    joined_grad, u_keep, u_send = call(
        attend_back_second, "attend_back_2",
        [((nctx, 3 * hd, rows), BF), ((3 * hd + extra_rows, width // 2), F32), ((3 * hd + extra_rows, width // 2), BF)],
        [SM] + [VM] * 11,
        head_scratch
        + [pltpu.VMEM((2 * hd, n // 2), BF), pltpu.VMEM((hd, n), F32), pltpu.VMEM((3 * hd + 16, n), BF),
           pltpu.VMEM((3 * hd + extra_rows, width), F32)],
        (meta, joined, attended_full, stats, grads, query_acc, key_half, xhat0, gains, shifts, wh, extra2),
        after=hold,
    )
    if fast:
        joined_grad, u_send = tie(joined_grad, feed_z1, kv_1), tie(u_send, feed_z1, kv_1)
        u_x1 = over_x(u_send)[None]
        u_keep = u_keep[None]
        crosses = [keep0, got0, cross_x1]
        feed_w, u_sum, kv_z, cross_y = sums(
            "reduce_4",
            [[terms(downs, 2, 0, [(feed_z1, (0, 64))]), terms(ups, 2, 0, [(feed_z1, (64, 128))])],
             [terms([u_keep, u_x1], 1, 0)], [terms(kvs, 2, 1)], [terms(crosses, 4, 1)]],
        )
        feed_w1, u_8, kv_2, cross_y1 = over_ctx(feed_w, 8), over_ctx(u_sum, 8), over_ctx(kv_z, 4), over_ctx(cross_y, 2)
        kvs, crosses = kvs + [kv_2], crosses + [cross_y1]
        (cross_z,) = sums("reduce_5", [[terms(crosses, 2, 1)]])
        cross_z1 = over_ctx(cross_z, 4)
        crosses = crosses + [cross_z1]
        (merged,) = call(
            merge_kernel, "reduce_6", [((1, 368, width), BF)], [VM] * 4, [], (feed_w, feed_w1, u_sum, u_8), after=[cross_z1, kv_2],
        )
        cross_w, kv_far, kv_near = sums(
            "reduce_7", [[terms(crosses, 2, 0)], [terms(kvs, 1, 1)], [terms(kvs, 1, 0)]], [merged],
        )
        cross_w1, kv_got = over_ctx(cross_w, 8), over_ctx(kv_far, 8)
        merged = tie(merged, cross_w)
        spread_out = [over_ctx(merged, mask) for mask in (4, 2, 6)]
        hold = [cross_w]
    dj = lax.all_to_all(joined_grad, "ctx", 0, 0, tiled=True)
    dj = dj.reshape(units, rep, 3 * hd, rows)[:, 0].reshape(seqs, H, 3 * hd, rows)
    (tokens_grad,) = call(
        start_kernel, "start_grad",
        [((seqs, rows, width), F32)],
        [SM] + [VM] * 5 + [ANY] * 3,
        [pltpu.VMEM((width, 3 * width), BF), pltpu.VMEM((seqs, 3 * width, rows), BF), pltpu.SemaphoreType.DMA((7,))],
        (meta, dj, tokens, steps, gains, h1g, own["joined"], near4, far4),
        after=hold,
    )

    if fast:
        (cross_pair,) = sums("reduce_8", [[[term(cross_w, 2, 0), term(cross_w1, 2, 0, None, True)]]], [kv_got, tokens_grad])
        pieces = [tie(piece, cross_pair) for piece in [merged] + spread_out]
        pieces = pieces + [over_ctx(piece, 1) for piece in pieces]
        (enc_grad,) = call(
            encoder_back_kernel, "encoder_back", [(encoder.shape, F32)], [VM] * 3, [], (kv_near, kv_got, w_keyval), after=[cross_pair],
        )
        up_grad, down_grad, self_in_grad, gain_grad, shift_grad, table_grad, down_bias_grad, up_bias_grad = call(
            place_kernel, "place",
            [((width // 2, ff), F32), ((ff // 2, width), F32), ((width // 2, 3 * width), F32), ((3, width // 2), F32),
             ((3, width // 2), F32), ((steps_count, width // 2), F32), ((1, width // 2), F32), ((4, width // 2), F32)],
            [SM] + [VM] * 9, [pltpu.VMEM((3 * width, width // 2), F32)], (meta, all_ids, *pieces), after=[enc_grad],
        )
        down_bias_grad, up_bias_grad = down_bias_grad.reshape(-1), up_bias_grad.reshape(-1)
        cross_pieces = spread(cross_pair, [up_grad])
        out_g, query_g, cross_g, keyval_g = call(
            place_cross_kernel, "place_cross",
            [((width // 2, width), F32)] * 3 + [((width // 2, 2 * width), F32)],
            [SM] + [VM] * 8, [], (meta, *cross_pieces),
        )
    else:
        def scatter(g, axis=0):
            return lax.psum(lax.psum_scatter(g, "fsdp", scatter_dimension=axis, tiled=True), "ctx")

        down_all = jnp.stack([down_keep, down_send]).reshape(2, 2, 8, 64, width).transpose(1, 0, 2, 3, 4)
        up_all = jnp.stack([up_keep, up_send]).reshape(2, 2, 2, 4, 64, width).transpose(2, 3, 4, 0, 1, 5)
        down_grad, up_grad = scatter(down_all.reshape(ff, width).astype(F32)), scatter(up_all.reshape(width, ff).astype(F32))
        c_all = jnp.stack([jnp.stack([keep0, send0]), jnp.stack([keep1, send1])])
        out_g, query_g, cross_g = (scatter(c_all[:, :, :, k : k + 16].reshape(width, width).astype(F32)) for k in (0, 16, 32))
        keyval_g = scatter(c_all[:, :, :, 48:80].transpose(0, 2, 3, 1, 4).reshape(width, 2 * width).astype(F32))
        kv = jnp.stack([kv_keep, kv_send]).reshape(2, 2, 2, 2, seqs, 2, enc_rows // 16, width).transpose(4, 3, 2, 1, 0, 6, 5, 7)
        kv = lax.psum_scatter(kv.reshape(seqs, enc_rows, 2 * width), "ctx", scatter_dimension=1, tiled=True)
        enc_grad = jnp.einsum("sre,de->srd", kv, w_keyval, preferred_element_type=F32)
        u = jnp.concatenate([u_keep, u_send.astype(F32)], axis=1)
        every_u = lax.all_gather(lax.psum(u[: 3 * hd], "fsdp"), "ctx", axis=0, tiled=False)
        by_head = every_u.reshape(seqs, H, rep, 3, hd, width).sum(axis=(0, 2))
        joined_g = by_head.transpose(3, 1, 0, 2).reshape(width, 3 * width)
        self_in_grad = lax.dynamic_slice_in_dim(joined_g, x * self_in.shape[0], self_in.shape[0], 0)
        total = lax.psum(u[3 * hd :], ("ctx", "fsdp"))
        wide = norm_gain.shape[1]
        extra = lax.dynamic_slice_in_dim(total, x * wide, wide, 1)
        last = extra_rows - 10
        down_bias_grad = extra[last]
        up_bias_all = total[last + 1 : last + 5].reshape(4, 2, width // 2).transpose(1, 0, 2).reshape(-1)
        up_bias_grad = lax.dynamic_slice_in_dim(up_bias_all, x * up_bias.shape[0], up_bias.shape[0], 0)
        gain_grad = jnp.stack([extra[0], extra[last + 7], extra[last + 5]])
        shift_grad = jnp.stack([extra[1], extra[last + 8], extra[last + 6]])
        hot = (jnp.arange(steps_count, dtype=jnp.int32).astype(F32)[:, None, None] == all_ids[None, :, None]).astype(F32)
        table_grad = jnp.sum(hot * extra[None, 2 : 2 + slots, :], axis=1)

    return (
        mixed, tokens_grad, enc_grad, self_in_grad, out_g, query_g, keyval_g, cross_g, up_grad, up_bias_grad,
        down_grad, down_bias_grad, gain_grad, shift_grad, table_grad,
    )


def solution(mesh):
    tok = P("fsdp", "ctx", None)
    row, vec, col = P("fsdp", None), P("fsdp"), P(None, "fsdp")
    in_specs = (tok, tok, vec, tok, row, row, row, row, row, row, vec, row, vec, col, col, col)
    out_specs = (tok, tok, tok, row, row, row, row, row, row, vec, row, vec, col, col, col)
    return jax.shard_map(shards, mesh=mesh, in_specs=in_specs, out_specs=out_specs, check_vma=False)
```

```python
import functools
import math

import jax
import jax.numpy as jnp
from jax import lax
from jax.experimental import pallas as pl
from jax.experimental.pallas import tpu as pltpu
from jax.sharding import PartitionSpec as P

H = 8
EPS = 1e-05
F32 = jnp.float32
BF = jnp.bfloat16
LOG2E = 1.4426950408889634
LARGE, SMALL = 62, 16
ROOMY = ("split", "prepare", "pack", "unpack", "attend", "encoder_rows", "weights_back", "start_grad")


def limit_of(name):
    return (LARGE if name in ROOMY else SMALL) * 1024 * 1024


def nn(a, b):
    return lax.dot_general(a, b, (((1,), (0,)), ((), ())), preferred_element_type=F32)


def nt(a, b):
    return lax.dot_general(a, b, (((1,), (1,)), ((), ())), preferred_element_type=F32)


def flip(v):
    return jnp.transpose(v)


def normalise(v):
    centred = v - jnp.mean(v, axis=-1, keepdims=True)
    r = lax.rsqrt(jnp.mean(centred * centred, axis=-1, keepdims=True) + EPS)
    return centred * r, r


def norm_back(grad, gain, xhat, r):
    u = grad * gain
    return r * (u - jnp.mean(u, axis=-1, keepdims=True) - xhat * jnp.mean(u * xhat, axis=-1, keepdims=True))


def aligned(index, size):
    return pl.ds(pl.multiple_of(index, size), size)


VM = pl.BlockSpec(memory_space=pltpu.VMEM)
SM = pl.BlockSpec(memory_space=pltpu.SMEM)
ANY = pl.BlockSpec(memory_space=pl.ANY)


def call(kernel, name, outs, in_specs, scratch, args, out_specs=None, after=(), grid=()):
    count = len(in_specs)

    def body(*refs):
        kernel(*refs[:count], *refs[count + len(after) :])

    return pl.pallas_call(
        body,
        name=name,
        grid=grid,
        out_shape=[jax.ShapeDtypeStruct(s, d) for s, d in outs],
        in_specs=list(in_specs) + [ANY] * len(after),
        out_specs=out_specs or [VM] * len(outs),
        scratch_shapes=scratch,
        compiler_params=pltpu.CompilerParams(vmem_limit_bytes=limit_of(name)),
        cost_estimate=pl.CostEstimate(flops=1000, bytes_accessed=1000, transcendentals=0),
    )(*args, *after)


class Placer:
    def __init__(self, sems, x, c):
        self.sems, self.x, self.c, self.used = sems, x, c, 0

    def copy(self, src, dst):
        copy = pltpu.make_async_copy(src, dst, self.sems.at[self.used])
        self.used += 1
        copy.start()
        return copy

    def lay(self, own, near, far, dst, row0, blocks):
        rows = own.shape[0]
        half = rows // 2
        base = (1 - self.x) * rows
        copies = [self.copy(own, dst.at[aligned(self.x * rows, rows)])]
        for b in range(blocks):
            cols = pl.ds(b * 512, 512)
            part = pl.ds(row0 + b * half, half)
            copies.append(self.copy(near.at[part], dst.at[aligned(base + self.c * half, half), cols]))
            copies.append(self.copy(far.at[part], dst.at[aligned(base + (1 - self.c) * half, half), cols]))
        return copies


def wait(copies):
    for copy in copies:
        copy.wait()


def split_kernel(meta, tokens, encoder, mine, others):
    rows, span = tokens.shape[1], encoder.shape[1]
    for out, s in ((others, 1 - meta[9]), (mine, meta[9])):
        out[0:rows, :] = tokens[s]
        for k in range(encoder.shape[0]):
            out[rows + k * span : rows + (k + 1) * span, :] = encoder[k]


ORDER = (0, 4, 2, 6, 8, 12, 10, 14, 1, 5, 3, 7, 9, 13, 11, 15)


def attend_kernel(meta, step, gains, shifts, wh, *refs):
    blocks, (xhat_out, joined_out, heads_out, full_out, stats_out, normed, keys) = refs[:-7], refs[-7:]
    n, width = xhat_out.shape
    hd = joined_out.shape[0] // 3
    rows = heads_out.shape[2]
    stats_out[...] = jnp.zeros_like(stats_out)
    for k, block in enumerate(blocks):
        xhat, r = normalise(block[0:rows, :].astype(F32) + step[...])
        at = aligned((meta[7] ^ ORDER[k] if len(blocks) == 16 else k) * rows, rows)
        xhat_out[at, :] = xhat.astype(BF)
        normed[at, :] = (xhat * gains[0:1, :] + shifts[0:1, :]).astype(BF)
        stats_out[1:2, at] = flip(jnp.broadcast_to(r, (rows, 128)))[0:1, :]
    for b in range(n // 512):
        cols = pl.ds(b * 512, 512)
        joined_out[:, cols] = nt(wh[...], normed[cols, :]).astype(BF)
    keys[...] = flip(joined_out[hd : 2 * hd, :].astype(F32)).astype(BF)
    factor = LOG2E / math.sqrt(hd)
    wide = 256

    def query_block(b, carry):
        cols = aligned(b * wide, wide)
        scores = nn(keys[...], joined_out[0:hd, cols]) * factor
        peak = jnp.max(scores, axis=0, keepdims=True)
        shares = jnp.exp2(scores - peak)
        total = jnp.sum(shares, axis=0, keepdims=True)
        out = nn(joined_out[2 * hd : 3 * hd, :], shares.astype(BF)) / total
        full_out[:, cols] = out
        stats_out[0:1, cols] = peak + jnp.log2(total)
        for part in range(wide // rows):
            heads_out[b * (wide // rows) + part] = out[:, part * rows : (part + 1) * rows].astype(BF)
        return carry

    lax.fori_loop(0, n // wide, query_block, 0)


def key_blocks(first, joined, full, stats, grads, keys, values, gout, key_grads, query_acc):
    n = full.shape[1]
    hd = joined.shape[0] // 3
    rows = grads.shape[2]
    span = keys.shape[0]
    scale = 1.0 / math.sqrt(hd)
    factor = LOG2E * scale
    for j in range(grads.shape[0]):
        gout[:, j * rows : (j + 1) * rows] = grads[j]
    mine = pl.ds(first, span)
    keys[...] = flip(joined[hd : 2 * hd, mine].astype(F32)).astype(BF)
    values[...] = flip(joined[2 * hd : 3 * hd, mine].astype(F32)).astype(BF)
    delta = jnp.sum(gout[...].astype(F32) * full[...], axis=0, keepdims=True)
    lse = stats[0:1, :]
    wide = 256

    def key_block(b, carry):
        at = aligned(b * wide, wide)
        queries = joined[0:hd, :]
        shares = jnp.exp2(nn(keys[at, :], queries) * factor - lse)
        share_grad = nn(values[at, :], gout[...])
        score_grad = (shares * (share_grad - delta)).astype(BF)
        key_grads[0:hd, at] = (nt(queries, score_grad) * scale).astype(BF)
        key_grads[hd : 2 * hd, at] = nt(gout[...], shares.astype(BF)).astype(BF)
        query_acc[...] += nn(joined[hd : 2 * hd, aligned(first + b * wide, wide)], score_grad)
        return carry

    lax.fori_loop(0, span // wide, key_block, 0)


def attend_back_first(joined, full, stats, grads, query_out, key_out, keys, values, gout):
    query_out[...] = jnp.zeros_like(query_out)
    key_blocks(0, joined, full, stats, grads, keys, values, gout, key_out, query_out)


def attend_back_second(
    meta, joined, full, stats, grads, query_in, key_in, xhat, gains, shifts, wh, extra, joined_grad_out, keep_out, send_out,
    keys, values, gout, key_grads, query_acc, lhs, whole,
):
    x, active, slot = meta[0], meta[3], meta[4]
    n, width = xhat.shape
    hd = joined.shape[0] // 3
    half = width // 2
    rows = grads.shape[2]
    scale = 1.0 / math.sqrt(hd)
    query_acc[...] = query_in[...]
    key_blocks(n // 2, joined, full, stats, grads, keys, values, gout, key_grads, query_acc)
    lhs[0:hd, :] = (query_acc[...] * scale).astype(BF)
    lhs[hd : 3 * hd, 0 : n // 2] = key_in[...]
    lhs[hd : 3 * hd, n // 2 :] = key_grads[...]
    for j in range(joined_grad_out.shape[0]):
        joined_grad_out[j] = lhs[0 : 3 * hd, j * rows : (j + 1) * rows]

    gain, shift = gains[0:1, :], shifts[0:1, :]
    grad = lhs[0 : 3 * hd, :].astype(F32)
    r = stats[1:2, :]
    weight = wh[...].astype(F32)
    bias = jnp.sum(weight * shift, axis=1, keepdims=True)
    mixed_mean = jnp.sum(grad * (joined[...].astype(F32) - bias), axis=0, keepdims=True) * (1.0 / width)
    tail = lhs.shape[0] - 3 * hd
    first = lax.broadcasted_iota(jnp.int32, (tail, n), 0) == 0
    lhs[3 * hd :, :] = jnp.where(first, mixed_mean * r, 0.0).astype(BF)
    product = nn(lhs[...], xhat[...])
    m = product[0 : 3 * hd]
    sums = jnp.sum(grad, axis=1, keepdims=True)
    scaled_sums = jnp.sum(grad * r, axis=1, keepdims=True)
    lead = gain * jnp.sum(weight * scaled_sums, axis=0, keepdims=True)
    start_sum = lead - jnp.mean(lead, axis=1, keepdims=True) - product[3 * hd : 3 * hd + 1]
    on = active.astype(F32)
    whole[0 : 3 * hd, :] = (m * gain + sums * shift) * on
    gain_grad = jnp.sum(weight * m, axis=0, keepdims=True) * on
    shift_grad = jnp.sum(weight * sums, axis=0, keepdims=True) * on
    row = lax.broadcasted_iota(jnp.int32, extra.shape, 0)
    more = jnp.where(row == 0, gain_grad, 0.0) + jnp.where(row == 1, shift_grad, 0.0)
    more = more + jnp.where(row == 2 + slot, start_sum * on, 0.0)
    whole[3 * hd :, :] = extra[...] + more
    keep_out[...] = whole[:, aligned(x * half, half)]
    send_out[...] = whole[:, aligned((1 - x) * half, half)].astype(BF)


def prepare_kernel(meta, ids, weight, gain, shift, table, down_bias, up_bias, out, turned, small):
    width = weight.shape[1] // 3
    hd = width // H
    pair, odd = meta[8] // 2, meta[8] % 2
    for j in range(3):
        turned[...] = flip(weight[:, aligned(j * width + pair * 2 * hd, 2 * hd)])
        out[j * hd : (j + 1) * hd, :] = turned[aligned(odd * hd, hd), :]
    small[...] = jnp.zeros_like(small)
    at = 0
    for part in (gain, shift, table):
        small[at : at + part.shape[0], :] = part[...].astype(F32)
        at += part.shape[0]
    half = small.shape[1]
    for part in (down_bias, up_bias):
        for q in range(part.shape[0] // half):
            small[at : at + 1, :] = part[q * half : (q + 1) * half].astype(F32).reshape(1, half)
            at += 1
    lane = lax.broadcasted_iota(jnp.int32, (1, small.shape[1]), 1)
    line = jnp.zeros((1, small.shape[1]), F32)
    for s in range(2):
        line = line + jnp.where(lane == s, ids[s].astype(F32), 0.0)
    small[at : at + 1, :] = line
    out[3 * hd :, :] = small[...].astype(BF)


def unpack_kernel(
    meta, ids, mine, other, wh_out, gains_out, shifts_out, steps_out, step_out, up_out, down_out, ids_out, both,
):
    x = meta[0]
    rows, half = mine.shape
    head_rows = wh_out.shape[0]
    count = rows - head_rows
    for part, at in ((mine, x), (other, 1 - x)):
        lanes = aligned(at * half, half)
        wh_out[:, lanes] = part[0:head_rows, :]
        both[:, lanes] = part[head_rows:, :].astype(F32)
    gains_out[...] = both[0:3, :]
    shifts_out[...] = both[3:6, :]
    for s in range(2):
        steps_out[s : s + 1, :] = both[pl.ds(6 + ids[s], 1), :]
    step_out[...] = both[pl.ds(6 + ids[meta[9]], 1), :]
    last = count - 8
    down_out[...] = both[last : last + 1, :]
    for q in range(4):
        line = both[last + 1 + q : last + 2 + q, :]
        up_out[:, q * half : (q + 1) * half] = line[:, 0:half]
        up_out[:, (4 + q) * half : (5 + q) * half] = line[:, half:]
    ids_out[...] = both[last + 5 : last + 6, :]


def encoder_kernel(meta, own, near, far, *refs):
    blocks, (enc_out, kvt_out, weight_out, sems) = refs[:-4], refs[-4:]
    put = Placer(sems, meta[0], meta[1])
    copies = put.lay(own, near, far, weight_out, 0, 2)
    rows = enc_out.shape[1] // len(blocks)
    first = blocks[0].shape[0] - enc_out.shape[0] * rows
    for k, block in enumerate(blocks):
        at = aligned((meta[7] ^ ORDER[k] if len(blocks) == 16 else k) * rows, rows)
        for s in range(enc_out.shape[0]):
            enc_out[s, at, :] = block[first + s * rows : first + (s + 1) * rows, :]
    wait(copies)
    for s in range(enc_out.shape[0]):
        for b in range(2):
            kv = nn(enc_out[s], weight_out[:, b * 512 : (b + 1) * 512])
            kvt_out[s, b * 512 : (b + 1) * 512, :] = flip(kv).astype(BF)


def pack_kernel(counts, meta, *refs):
    total = sum(counts)
    weights, outs, sems = refs[:total], refs[total:-1], refs[-1]
    copies = []
    index = 0
    for out, count in zip(outs, counts):
        at = 0
        for weight in weights[index : index + count]:
            half = weight.shape[0] // 2
            for b in range(weight.shape[1] // 512):
                src = weight.at[aligned(meta[1] * half, half), pl.ds(b * 512, 512)]
                copies.append(pltpu.make_async_copy(src, out.at[pl.ds(at, half)], sems.at[len(copies)]))
                copies[-1].start()
                at += half
        index += count
    wait(copies)


GROUPS = (("keyval", "out", "query", "cross", "up", "down"), ("joined",))


def chunk_at(meta, k, xr):
    x, c = meta[0], meta[1]
    return x ^ xr, c ^ k


def forward_kernel(
    meta, tokens, steps, att, kvt, gains, shifts, own_out, own_query, own_cross, near2, far2,
    h2_out, h1_out, q_out, crossed_out, shares_out, w_out, w_query, w_cross, sems,
):
    seqs, rows, width = tokens.shape
    hd = width // H
    put = Placer(sems, meta[0], meta[1])
    half = own_out.shape[0] // 2
    c_out = put.lay(own_out, near2, far2, w_out, 2 * half, 1)
    c_query = put.lay(own_query, near2, far2, w_query, 3 * half, 1)
    c_cross = put.lay(own_cross, near2, far2, w_cross, 4 * half, 1)
    factor = LOG2E / math.sqrt(hd)

    wait(c_out)
    for s in range(seqs):
        at = pl.ds(s * rows, rows)
        start = tokens[s].astype(F32) + steps[s : s + 1, :]
        h1_out[at, :] = start + nn(flip(att[s]), w_out[...])
    hidden1 = h1_out[...]
    xhat1, unused = normalise(hidden1)
    wait(c_query)
    q_out[...] = nn((xhat1 * gains[1:2, :] + shifts[1:2, :]).astype(BF), w_query[...]).astype(BF)
    for s in range(seqs):
        for first in range(0, H, TOGETHER):
            heads = range(first, first + TOGETHER)
            scores = [
                nn(q_out[s * rows : (s + 1) * rows, h * hd : (h + 1) * hd], kvt[s, h * hd : (h + 1) * hd, :]) * factor for h in heads
            ]
            peaks = [jnp.max(score, axis=1, keepdims=True) for score in scores]
            shares = [jnp.exp2(score - peak) for score, peak in zip(scores, peaks)]
            totals = [jnp.sum(share, axis=1, keepdims=True) for share in shares]
            lows = [(share * (1.0 / total)).astype(BF) for share, total in zip(shares, totals)]
            got = [nt(kvt[s, width + h * hd : width + (h + 1) * hd, :], low) for h, low in zip(heads, lows)]
            for k, h in enumerate(heads):
                shares_out[s * H + h] = lows[k]
                crossed_out[s, h * hd : (h + 1) * hd, :] = got[k].astype(BF)
    wait(c_cross)
    for s in range(seqs):
        at = pl.ds(s * rows, rows)
        h2_out[at, :] = h1_out[at, :] + nn(flip(crossed_out[s]), w_cross[...])


TOGETHER = 4


def feed_kernel(
    meta, hidden2_in, gains, shifts, up_bias, down_bias, out_grad, own_up, own_down, near2, far2,
    mixed_out, h2g_out, extra_out, down_keep, down_send, up_keep, up_send, w_up, w_down, act_t, n2_t, pre_low, sems,
):
    seqs, rows, width = out_grad.shape
    ff = w_down.shape[0]
    slots = extra_out.shape[0]
    put = Placer(sems, meta[0], meta[1])
    c_up = put.lay(own_up, near2, far2, w_up, 5 * (own_up.shape[0] // 2), 4)
    c_down = put.lay(own_down, near2, far2, w_down, 9 * (own_up.shape[0] // 2), 1)
    hidden2 = hidden2_in[...]
    xhat2, r2 = normalise(hidden2)
    n2 = (xhat2 * gains[2:3, :] + shifts[2:3, :]).astype(BF)
    n2_t[...] = flip(n2)
    grad = jnp.concatenate([out_grad[s] for s in range(seqs)], axis=0)
    top = grad.astype(F32)
    wait(c_up)
    wait(c_down)
    mixed = hidden2 + down_bias[...]
    n2_grad = jnp.zeros_like(hidden2)
    extra_out[...] = jnp.zeros_like(extra_out)
    root = math.sqrt(2.0 / math.pi)
    bias_row = slots - 10
    for b in range(ff // 512):
        cols = pl.ds(b * 512, 512)
        pre = nn(n2, w_up[:, cols]) + up_bias[:, cols]
        square = pre * pre
        bent = jnp.tanh(root * pre * (1.0 + 0.044715 * square))
        act = (0.5 * pre * (1.0 + bent)).astype(BF)
        slope = 0.5 * (1.0 + bent) + 0.5 * root * pre * (1.0 - bent * bent) * (1.0 + 3.0 * 0.044715 * square)
        mixed = mixed + nn(act, w_down[cols, :])
        act_t[cols, :] = flip(act)
        low = (nt(grad, w_down[cols, :]) * slope).astype(BF)
        pre_low[:, cols] = low
        n2_grad = n2_grad + nt(low, w_up[:, cols])
        sums = jnp.sum(low.astype(F32), axis=0, keepdims=True)
        per_half = ff // 512 // 2
        lanes = pl.ds((b // per_half) * 256, 256)
        for piece in range(2):
            row = bias_row + 1 + (b % per_half) * 2 + piece
            extra_out[row : row + 1, lanes] = sums[:, piece * 256 : (piece + 1) * 256]
    for s in range(seqs):
        mixed_out[s] = mixed[s * rows : (s + 1) * rows].astype(BF)
    h2g_out[...] = top + norm_back(n2_grad, gains[2:3, :], xhat2, r2)
    extra_out[bias_row : bias_row + 1, :] = jnp.sum(top, axis=0, keepdims=True)
    extra_out[bias_row + 5 : bias_row + 6, :] = jnp.sum(n2_grad * xhat2, axis=0, keepdims=True)
    extra_out[bias_row + 6 : bias_row + 7, :] = jnp.sum(n2_grad, axis=0, keepdims=True)

    me = meta[2]
    for k in (1, 0):
        down_out, up_out = (down_send, up_send) if k else (down_keep, up_keep)
        for xr in (1, 0):
            xa, ca = chunk_at(meta, k, xr)
            down = nn(act_t[aligned(xa * (ff // 2) + ca * (ff // 4), ff // 4), :], grad).astype(BF)
            up = nn(n2_t[aligned(xa * (width // 2), width // 2), :], pre_low[:, aligned(ca * (ff // 2), ff // 2)])
            up = up.astype(BF)
            for a in range(8):
                at = a ^ me
                down_out[xr * 8 + at] = down[a * 64 : (a + 1) * 64]
                up_out[(at // 4) * 8 + xr * 4 + at % 4] = up[(a % 4) * 64 : (a % 4 + 1) * 64, (a // 4) * 512 : (a // 4 + 1) * 512]


def cross_back_kernel(meta, h2g, q, shares, kvt, own_cross, near2, far2, dq_out, part_out, w_cross, dc, sems):
    width = h2g.shape[1]
    seqs, unused, enc_rows = kvt.shape
    rows = h2g.shape[0] // seqs
    hd = width // H
    scale = 1.0 / math.sqrt(hd)
    put = Placer(sems, meta[0], meta[1])
    half = own_cross.shape[0] // 2
    wait(put.lay(own_cross, near2, far2, w_cross, 4 * half, 1))
    dc[...] = nt(h2g[...].astype(BF), w_cross[...]).astype(BF)
    for s in range(seqs):
        at = slice(s * rows, (s + 1) * rows)
        q_t = flip(q[at, :])
        dc_t = flip(dc[at, :])
        for first in range(0, H, TOGETHER):
            heads = range(first, first + TOGETHER)
            lows = [shares[s * H + h] for h in heads]
            wides = [low.astype(F32) for low in lows]
            share_grads = [nn(dc[at, h * hd : (h + 1) * hd], kvt[s, width + h * hd : width + (h + 1) * hd, :]) for h in heads]
            means = [jnp.sum(wide * grad, axis=1, keepdims=True) for wide, grad in zip(wides, share_grads)]
            score_grads = [(wide * (grad - mean)).astype(BF) for wide, grad, mean in zip(wides, share_grads, means)]
            q_grads = [nt(grad, kvt[s, h * hd : (h + 1) * hd, :]) for h, grad in zip(heads, score_grads)]
            k_grads = [nn(q_t[h * hd : (h + 1) * hd], grad) for h, grad in zip(heads, score_grads)]
            v_grads = [nn(dc_t[h * hd : (h + 1) * hd], low) for h, low in zip(heads, lows)]
            for k, h in enumerate(heads):
                head = slice(h * hd, (h + 1) * hd)
                dq_out[at, head] = (q_grads[k] * scale).astype(BF)
                part_out[s, head, :] = (k_grads[k] * scale).astype(BF)
                part_out[s, width + h * hd : width + (h + 1) * hd, :] = v_grads[k].astype(BF)


def hidden_back_kernel(
    meta, h2g, hidden1, dq, gains, extra_in, own_out, own_query, near2, far2, h1g_out, att_grad_out, extra_out,
    w_out, w_query, sems,
):
    width = h2g.shape[1]
    seqs, unused, rows = att_grad_out.shape
    put = Placer(sems, meta[0], meta[1])
    half = own_out.shape[0] // 2
    c_query = put.lay(own_query, near2, far2, w_query, 3 * half, 1)
    c_out = put.lay(own_out, near2, far2, w_out, 2 * half, 1)
    xhat1, r1 = normalise(hidden1[...])
    wait(c_query)
    n1_grad = nt(dq[...], w_query[...])
    grad1 = h2g[...] + norm_back(n1_grad, gains[1:2, :], xhat1, r1)
    h1g_out[...] = grad1
    low1 = grad1.astype(BF)
    wait(c_out)
    for s in range(seqs):
        att_grad_out[s] = nt(w_out[...], low1[s * rows : (s + 1) * rows]).astype(BF)
    last = extra_out.shape[0] - 10
    row = lax.broadcasted_iota(jnp.int32, extra_out.shape, 0)
    more = jnp.where(row == last + 7, jnp.sum(n1_grad * xhat1, axis=0, keepdims=True), 0.0)
    more = more + jnp.where(row == last + 8, jnp.sum(n1_grad, axis=0, keepdims=True), 0.0)
    for s in range(seqs):
        token_sum = jnp.sum(grad1[s * rows : (s + 1) * rows], axis=0, keepdims=True)
        more = more + jnp.where(row == 2 + meta[5] + s, token_sum, 0.0)
    extra_out[...] = extra_in[...] + more


def weights_back_kernel(
    meta, h2g, h1g, hidden1, crossed, att, dq, part, enc, gains, shifts, keep1, send1, keep0, send0, kv_keep, kv_send,
    n1_t, enc_t, part_t,
):
    width = h2g.shape[1]
    seqs, unused, rows = att.shape
    xhat1, unused = normalise(hidden1[...])
    n1_t[...] = flip((xhat1 * gains[1:2, :] + shifts[1:2, :]).astype(BF))
    low2, low1 = h2g[...].astype(BF), h1g[...].astype(BF)
    enc_rows = enc.shape[1]
    span = enc_rows // 16
    for s in range(seqs):
        enc_t[s] = flip(enc[s])
        part_t[s] = flip(part[s])
    for k in (1, 0):
        out = kv_send if k else kv_keep
        for at in range(8):
            a = at ^ meta[2]
            first = aligned(((a & 1) * 8 + (a & 2) * 2 + (a & 4) // 2 + (meta[1] ^ k)) * span, span)
            for s in range(seqs):
                for j in range(2):
                    row = (s * 2 + j) * span
                    out[at, row : row + span, :] = part_t[s, first, j * width : (j + 1) * width]
    me = meta[2]
    for k in (1, 0):
        for xr in (1, 0):
            out = ((keep0, keep1), (send0, send1))[k][xr]
            xa, ca = chunk_at(meta, k, xr)
            at = aligned(xa * (width // 2) + ca * (width // 4), width // 4)
            outer = jnp.zeros((width // 4, width), F32)
            cross = jnp.zeros((width // 4, width), F32)
            keyval = jnp.zeros((width // 2, width), F32)
            for s in range(seqs):
                mine = slice(s * rows, (s + 1) * rows)
                outer = outer + nn(att[s, at, :], low1[mine])
                cross = cross + nn(crossed[s, at, :], low2[mine])
                keyval = keyval + nt(enc_t[s, aligned(xa * (width // 2), width // 2), :], part[s, aligned(ca * width, width), :])
            query = nn(n1_t[at, :], dq[...]).astype(BF)
            outer, cross, keyval = outer.astype(BF), cross.astype(BF), keyval.astype(BF)
            for a in range(8):
                out[a ^ me, 0:16, :] = outer[a * 16 : (a + 1) * 16]
                out[a ^ me, 16:32, :] = query[a * 16 : (a + 1) * 16]
                out[a ^ me, 32:48, :] = cross[a * 16 : (a + 1) * 16]
                out[a ^ me, 48:80, :] = keyval[a * 32 : (a + 1) * 32]


def start_kernel(meta, grads, tokens, steps, gains, h1g, own, near, far, grad_out, weight, turned, sems):
    seqs, rows, width = tokens.shape
    hd = width // H
    put = Placer(sems, meta[0], meta[1])
    copies = put.lay(own, near, far, weight, 0, 3)
    for s in range(seqs):
        for h in range(H):
            for j in range(3):
                turned[s, j * width + h * hd : j * width + (h + 1) * hd, :] = grads[s, h, j * hd : (j + 1) * hd, :]
    wait(copies)
    for s in range(seqs):
        xhat, r = normalise(tokens[s].astype(F32) + steps[s : s + 1, :])
        grad = nt(flip(turned[s]), weight[...])
        grad_out[s] = h1g[s * rows : (s + 1) * rows, :] + norm_back(grad, gains[0:1, :], xhat, r)


PIECES = [(core, mask + far, far) for core in (0, 1) for mask in (0, 2, 4, 6) for far in (0, 1)]


def place_cross_kernel(meta, *refs):
    pieces, (out_out, query_out, cross_out, keyval_out) = refs[:-4], refs[-4:]
    c, me = meta[1], meta[2]
    for k, (core, mask, index) in enumerate(PIECES):
        block = pieces[k // 2][index].astype(F32)
        a = me ^ mask
        ca = c ^ core
        at = aligned(ca * 128 + a * 16, 16)
        out_out[at, :] = block[0:16]
        query_out[at, :] = block[16:32]
        cross_out[at, :] = block[32:48]
        keyval_out[aligned(a * 32, 32), aligned(ca * 512, 512)] = block[48:80]


def encoder_back_kernel(kv, got, weight, out):
    seqs, span, width = out.shape
    total = (kv[0].astype(F32) + got[0].astype(F32)).astype(BF)
    for s in range(seqs):
        first = s * 2 * span
        keys = nt(total[first : first + span], weight[:, 0:width])
        out[s] = keys + nt(total[first + span : first + 2 * span], weight[:, width:])


def merge_kernel(feed, feed_got, heads, heads_got, out):
    rows = feed.shape[1]
    for k in range(2):
        total = feed[k].astype(F32) + feed_got[1 - k].astype(F32)
        out[0, k * rows : (k + 1) * rows, :] = total.astype(BF)
    total = heads[0].astype(F32) + heads_got[0].astype(F32)
    count, half = total.shape
    split = out.shape[1] - 2 * rows
    out[0, 2 * rows :, 0:half] = total[0:split].astype(BF)
    rest = jnp.concatenate([total[split:], jnp.zeros((2 * split - count, half), F32)], axis=0)
    out[0, 2 * rows :, half:] = rest.astype(BF)


def place_kernel(meta, ids, *refs):
    pieces = refs[:8]
    feed_up, feed_down, grad_out, gain_out, shift_out, table_out, down_out, up_out, stacked = refs[8:]
    c, me, low = meta[1], meta[2], meta[6]
    for k, (core, mask, index) in enumerate(PIECES):
        block = pieces[k // 2][0, index * 128 : (index + 1) * 128, :].astype(F32)
        a = me ^ mask
        ca = c ^ core
        feed_down[aligned(ca * 512 + a * 64, 64), :] = block[0:64]
        feed_up[aligned((a % 4) * 64, 64), aligned(ca * 1024 + (a // 4) * 512, 512)] = block[64:128]
    hd = 64
    half = grad_out.shape[0]
    total = jnp.zeros((16, half), F32)
    for k, mask in enumerate((0, 4, 2, 6, 1, 5, 3, 7)):
        wide = pieces[k][0, 256:368, :].astype(F32)
        block = jnp.concatenate([wide[:, 0:half], wide[0:96, half:]], axis=0)
        head = low ^ mask
        for j in range(3):
            stacked[aligned(j * H * hd + head * hd, hd), :] = block[j * hd : (j + 1) * hd]
        total = total + block[3 * hd :]
    for b in range(3):
        grad_out[:, b * 512 : (b + 1) * 512] = flip(stacked[b * 512 : (b + 1) * 512, :])
    last = total.shape[0] - 10
    for row, (g, b) in enumerate(((0, 1), (last + 7, last + 8), (last + 5, last + 6))):
        gain_out[row : row + 1, :] = total[g : g + 1]
        shift_out[row : row + 1, :] = total[b : b + 1]
    down_out[...] = total[last : last + 1]
    up_out[...] = total[last + 1 : last + 5]
    step = lax.broadcasted_iota(jnp.int32, table_out.shape, 0).astype(F32)
    table = jnp.zeros(table_out.shape, F32)
    for k in range(4):
        lane = (k // 2) * half + k % 2
        table = table + jnp.where(step == ids[:, lane : lane + 1], total[2 + k : 3 + k], 0.0)
    table_out[...] = table


def sums(name, jobs, after=()):
    arrays, plan, outs = [], [], []
    for groups, split in jobs:
        steps, row = [], 0
        for group in groups:
            steps.append((row, range(len(arrays), len(arrays) + len(group))))
            row += group[0].shape[1]
            arrays += group
        blocks, width = groups[0][0].shape[0], groups[0][0].shape[2]
        plan.append((len(outs), blocks, split, steps))
        outs += [((blocks // 2, row, width), BF)] * 2 if split else [((blocks, row, width), BF)]
    count = len(arrays)

    def kernel(*refs):
        results = refs[count:]
        for first, blocks, split, steps in plan:
            for row, which in steps:
                total = refs[which[0]][...].astype(F32)
                for k in which[1:]:
                    total = total + refs[k][...].astype(F32)
                total = total.astype(BF)
                rows = pl.ds(row, total.shape[1])
                if split:
                    results[first][:, rows, :] = total[blocks // 2 :]
                    results[first + 1][:, rows, :] = total[: blocks // 2]
                else:
                    results[first][:, rows, :] = total

    return call(kernel, name, outs, [VM] * count, [], arrays, after=after)


def pair_kernel(mine, got, out):
    for k in range(2):
        out[k] = (mine[k].astype(F32) + got[1 - k].astype(F32)).astype(BF)


def tie(value, *others):
    return lax.optimization_barrier((value,) + others)[0]


def over_ctx(value, mask):
    return lax.ppermute(value, "ctx", [(i, i ^ mask) for i in range(16)])


def over_x(value):
    return lax.ppermute(value, "fsdp", [(0, 1), (1, 0)])


def spread(piece, first=()):
    pieces = [piece] + [over_ctx(piece, mask) for mask in (4, 2, 6)]
    pieces = [tie(p, *first) for p in pieces]
    return pieces + [over_ctx(p, 1) for p in pieces]


def shards(
    tokens, encoder, step_ids, out_grad, self_in, self_out, cross_query, cross_keyval, cross_out,
    ffn_up, up_bias, ffn_down, down_bias, norm_gain, norm_shift, step_table,
):
    nctx, nx = lax.axis_size("ctx"), lax.axis_size("fsdp")
    i, x = lax.axis_index("ctx"), lax.axis_index("fsdp")
    seqs, rows, width = tokens.shape
    hd = width // H
    units = seqs * H
    rep = nctx // units
    unit = i // rep
    s_mine, head = unit // H, unit % H
    n = rows * nctx
    ff = 2048
    fast = nctx == 16 and nx == 2
    steps_count = step_table.shape[0]
    slots = seqs * nx
    extra_rows = -(-(slots + 12) // 16) * 16
    zero = jnp.int32(0)

    xk, c, me = zero, zero, zero
    if fast:
        xk, c, me = x, i & 1, ((i >> 1) & 1) * 4 + ((i >> 2) & 1) * 2 + ((i >> 3) & 1)
    active = (i % rep == 0).astype(jnp.int32)
    meta = jnp.stack([xk, c, me, active, seqs * x + s_mine, seqs * x, i & 7, i, head, s_mine]).astype(jnp.int32)

    if fast:
        mine, others = call(
            split_kernel, "split", [((rows + seqs * encoder.shape[1], width), BF)] * 2, [SM, VM, VM], [], (meta, tokens, encoder),
        )
        got = over_ctx(others, 8)
        blocks = [mine] + [over_ctx(mine, mask) for mask in (4, 2, 6)]
        blocks += [got] + [over_ctx(got, mask) for mask in (4, 2, 6)]
        blocks += [over_ctx(block, 1) for block in blocks]

        (small,) = call(
            prepare_kernel, "prepare", [((256, width // 2), BF)], [SM, SM] + [VM] * 6,
            [pltpu.VMEM((2 * hd, width // 2), BF), pltpu.VMEM((64, width // 2), F32)],
            (meta, step_ids, self_in, norm_gain, norm_shift, step_table, down_bias, up_bias),
            after=[mine],
        )
        own = dict(keyval=cross_keyval, out=self_out, query=cross_query, cross=cross_out, up=ffn_up, down=ffn_down, joined=self_in)

        weights = [own[name] for group in GROUPS for name in group]
        sizes = [sum(own[name].size for name in group) // 1024 for group in GROUPS]
        packed = call(
            functools.partial(pack_kernel, [len(group) for group in GROUPS]), "pack", [((size, 512), BF) for size in sizes],
            [SM] + [ANY] * len(weights), [pltpu.SemaphoreType.DMA((13,))], (meta, *weights), after=[small],
        )
        other_small = over_x(small)
        near2 = over_x(tie(packed[0], other_small, *blocks[1:5]))
        wh, gains, shifts, steps, step_mine, bias_u, bias_d, all_ids = call(
            unpack_kernel, "unpack",
            [((3 * hd, width), BF), ((3, width), F32), ((3, width), F32), ((seqs, width), F32), ((1, width), F32),
             ((1, ff), F32), ((1, width), F32), ((1, width), F32)],
            [SM, SM, VM, VM], [pltpu.VMEM((64, width), F32)], (meta, step_ids, small, other_small), after=[packed[0]],
        )
    else:
        def gather(w, axis=0):
            return lax.all_gather(w, "fsdp", axis=axis, tiled=True)

        gains, shifts = gather(norm_gain, 1).astype(F32), gather(norm_shift, 1).astype(F32)
        table = gather(step_table, 1)
        bias_d, bias_u = gather(down_bias)[None, :].astype(F32), gather(up_bias)[None, :].astype(F32)
        all_ids = gather(step_ids.astype(BF)).astype(F32)
        full = dict(keyval=gather(cross_keyval), out=gather(self_out), query=gather(cross_query), cross=gather(cross_out),
                    up=gather(ffn_up), down=gather(ffn_down), joined=gather(self_in))
        half_of = {name: w.shape[0] // 2 for name, w in full.items()}
        own = {name: w[: half_of[name]] for name, w in full.items()}

        def group(names, which):
            parts = []
            for name in names:
                rest = full[name][half_of[name] :]
                quarter = half_of[name] // 2
                part = rest[which * quarter : (which + 1) * quarter]
                parts += [part[:, b : b + 512] for b in range(0, part.shape[1], 512)]
            return jnp.concatenate(parts, axis=0)

        (near2, far2), (near4, far4) = ([group(names, w) for w in (0, 1)] for names in GROUPS)
        by_head = full["joined"].reshape(width, 3, H, hd)
        wh = lax.dynamic_index_in_dim(by_head, head, 2, False).reshape(width, 3 * hd).T
        onehot = (jnp.arange(steps_count, dtype=jnp.int32)[None, :] == step_ids[:, None]).astype(BF)
        steps = jnp.dot(onehot, table, preferred_element_type=F32)
        step_mine = lax.dynamic_index_in_dim(steps, s_mine, 0, True)
        every = lax.all_gather(tokens, "ctx", axis=0, tiled=False)
        chosen = lax.dynamic_index_in_dim(every, s_mine, 1, False)
        encs = lax.all_gather(encoder, "ctx", axis=0, tiled=False)
        blocks = [jnp.concatenate([chosen[j], encs[j].reshape(-1, width)], axis=0) for j in range(nctx)]
    xhat0, joined, heads, attended_full, stats = call(
        attend_kernel, "attend",
        [((n, width), BF), ((3 * hd, n), BF), ((nctx, hd, rows), BF), ((hd, n), F32), ((8, n), F32)],
        [SM] + [VM] * (4 + nctx),
        [pltpu.VMEM((n, width), BF), pltpu.VMEM((n, hd), BF)],
        (meta, step_mine, gains, shifts, wh, *blocks),
    )
    hold = []
    back = lax.all_to_all(heads, "ctx", 0, 0, tiled=True)
    if fast:
        far2 = over_ctx(tie(near2, heads), 1)
    att = back.reshape(units, rep, hd, rows)[:, 0].reshape(seqs, width, rows)

    enc_rows = nctx * encoder.shape[1]
    enc_all, kvt, w_keyval = call(
        encoder_kernel, "encoder_rows",
        [((seqs, enc_rows, width), BF), ((seqs, 2 * width, enc_rows), BF), ((width, 2 * width), BF)],
        [SM, ANY, ANY, ANY] + [VM] * nctx,
        [pltpu.SemaphoreType.DMA((5,))],
        (meta, own["keyval"], near2, far2, *blocks),
    )
    if fast:
        near4 = over_x(tie(packed[1], kvt))
        hold = [near4]

    tall = seqs * rows
    square = pltpu.VMEM((width, width), BF)
    hidden2, hidden1, q, crossed, shares = call(
        forward_kernel, "forward",
        [((tall, width), F32), ((tall, width), F32), ((tall, width), BF), ((seqs, width, rows), BF), ((units, rows, enc_rows), BF)],
        [SM] + [VM] * 6 + [ANY] * 5,
        [square] * 3 + [pltpu.SemaphoreType.DMA((9,))],
        (meta, tokens, steps, att, kvt, gains, shifts, own["out"], own["query"], own["cross"], near2, far2),
    )
    mixed, h2g, extra1, down_keep, down_send, up_keep, up_send = call(
        feed_kernel, "feed",
        [((seqs, rows, width), BF), ((tall, width), F32), ((extra_rows, width), F32)] + [((16, 64, width), BF)] * 4,
        [SM] + [VM] * 6 + [ANY] * 4,
        [pltpu.VMEM((width, ff), BF), pltpu.VMEM((ff, width), BF), pltpu.VMEM((ff, tall), BF),
         pltpu.VMEM((width, tall), BF), pltpu.VMEM((tall, ff), BF), pltpu.SemaphoreType.DMA((12,))],
        (meta, hidden2, gains, shifts, bias_u, bias_d, out_grad, own["up"], own["down"], near2, far2),
        after=hold,
    )
    hold, hold_far = [], []
    if fast:
        far4 = over_ctx(tie(near4, h2g), 1)
        hold_far = [far4]
        down_got, up_got = over_ctx(down_send, 1), over_ctx(up_send, 1)
    dq, part = call(
        cross_back_kernel, "cross_back",
        [((tall, width), BF), ((seqs, 2 * width, enc_rows), BF)],
        [SM] + [VM] * 4 + [ANY] * 3,
        [square, pltpu.VMEM((tall, width), BF), pltpu.SemaphoreType.DMA((3,))],
        (meta, h2g, q, shares, kvt, own["cross"], near2, far2), after=hold,
    )
    hold = []
    if fast:
        down_x, down_kept, up_y, up_kept = sums(
            "reduce_1", [([[down_keep, down_got]], True), ([[up_keep, up_got]], True)], [dq])
        down_x1, up_y1 = over_x(down_x), over_ctx(up_y, 2)
        hold = [down_x]
    h1g, att_grad, extra2 = call(
        hidden_back_kernel, "hidden_back",
        [((tall, width), F32), ((seqs, width, rows), BF), ((extra_rows, width), F32)],
        [SM] + [VM] * 5 + [ANY] * 4,
        [square, square, pltpu.SemaphoreType.DMA((6,))],
        (meta, h2g, hidden1, dq, gains, extra1, own["out"], own["query"], near2, far2),
        after=hold,
    )
    by_unit = att_grad.reshape(units, 1, hd, rows)
    grads = lax.all_to_all(jnp.broadcast_to(by_unit, (units, rep, hd, rows)).reshape(nctx, hd, rows), "ctx", 0, 0, tiled=True)
    keep1, send1, keep0, send0, kv_keep, kv_send = call(
        weights_back_kernel, "weights_back",
        [((8, 80, width), BF)] * 4 + [((8, enc_rows // 4, width), BF)] * 2,
        [SM] + [VM] * 10,
        [pltpu.VMEM((width, tall), BF), pltpu.VMEM((seqs, width, enc_rows), BF), pltpu.VMEM((seqs, enc_rows, 2 * width), BF)],
        (meta, h2g, h1g, hidden1, crossed, att, dq, part, enc_all, gains, shifts), after=hold_far,
    )
    hold = []
    if fast:
        got1, got0, kv_0 = (over_ctx(tie(part, grads, down_x1, up_y1), 1) for part in (send1, send0, kv_send))

        down_y, down_kept, up_x, up_kept = sums(
            "reduce_2", [([[down_kept, down_x1]], True), ([[up_kept, up_y1]], True)], [grads, keep1],
        )
        down_y1, up_x1 = over_ctx(down_y, 2), over_x(up_x)
        hold = [down_y]

    head_scratch = [pltpu.VMEM((n // 2, hd), BF), pltpu.VMEM((n // 2, hd), BF), pltpu.VMEM((hd, n), BF)]
    query_acc, key_half = call(
        attend_back_first, "attend_back_1", [((hd, n), F32), ((2 * hd, n // 2), BF)], [VM] * 4, head_scratch,
        (joined, attended_full, stats, grads), after=hold,
    )
    hold = []
    if fast:
        feed_z, feed_kept, cross_x, cross_kept, kv_y, kv_kept = sums(
            "reduce_3",
            [([[down_kept, down_y1], [up_kept, up_x1]], True), ([[keep1, got1]], False), ([[keep0, got0]], False), ([[kv_keep, kv_0]], True)],
            [query_acc],
        )
        feed_z1, cross_x1, kv_1 = over_ctx(feed_z, 4), over_x(cross_x), over_ctx(kv_y, 2)
        hold = [feed_z]
    joined_grad, u_keep, u_send = call(
        attend_back_second, "attend_back_2",
        [((nctx, 3 * hd, rows), BF), ((3 * hd + extra_rows, width // 2), F32), ((3 * hd + extra_rows, width // 2), BF)],
        [SM] + [VM] * 11,
        head_scratch
        + [pltpu.VMEM((2 * hd, n // 2), BF), pltpu.VMEM((hd, n), F32), pltpu.VMEM((3 * hd + 16, n), BF),
           pltpu.VMEM((3 * hd + extra_rows, width), F32)],
        (meta, joined, attended_full, stats, grads, query_acc, key_half, xhat0, gains, shifts, wh, extra2),
        after=hold,
    )
    if fast:
        joined_grad, u_send = tie(joined_grad, feed_z1, kv_1), tie(u_send, feed_z1, kv_1)
        u_x1 = over_x(u_send)[None]
        feed_w, kv_z, kv_kept, cross_y, cross_kept = sums(
            "reduce_4", [([[feed_kept, feed_z1]], False), ([[kv_kept, kv_1]], True), ([[cross_kept, cross_x1]], True)], [u_send],
        )
        feed_w1, kv_2, cross_y1 = over_ctx(feed_w, 8), over_ctx(kv_z, 4), over_ctx(cross_y, 2)
        cross_z, cross_kept, u_sum = sums("reduce_5", [([[cross_kept, cross_y1]], True), ([[u_keep[None], u_x1]], False)])
        cross_z1, u_8 = over_ctx(cross_z, 4), over_ctx(u_sum, 8)
        (merged,) = call(
            merge_kernel, "reduce_6", [((1, 368, width), BF)], [VM] * 4, [], (feed_w, feed_w1, u_sum, u_8), after=[cross_z1, kv_2],
        )
        cross_w, kv_far, kv_near = sums("reduce_7", [([[cross_kept, cross_z1]], False), ([[kv_kept, kv_2]], True)], [merged])
        cross_w1, kv_got = over_ctx(cross_w, 8), over_ctx(kv_far, 8)
        merged = tie(merged, cross_w)
        spread_out = [over_ctx(merged, mask) for mask in (4, 2, 6)]
        hold = [cross_w]
    dj = lax.all_to_all(joined_grad, "ctx", 0, 0, tiled=True)
    dj = dj.reshape(units, rep, 3 * hd, rows)[:, 0].reshape(seqs, H, 3 * hd, rows)
    (tokens_grad,) = call(
        start_kernel, "start_grad",
        [((seqs, rows, width), F32)],
        [SM] + [VM] * 5 + [ANY] * 3,
        [pltpu.VMEM((width, 3 * width), BF), pltpu.VMEM((seqs, 3 * width, rows), BF), pltpu.SemaphoreType.DMA((7,))],
        (meta, dj, tokens, steps, gains, h1g, own["joined"], near4, far4),
        after=hold,
    )

    if fast:
        (cross_pair,) = call(
            pair_kernel, "reduce_8", [((2, 80, width), BF)], [VM] * 2, [], (cross_w, cross_w1), after=[kv_got, tokens_grad],
        )
        pieces = [tie(piece, cross_pair) for piece in [merged] + spread_out]
        pieces = pieces + [over_ctx(piece, 1) for piece in pieces]
        (enc_grad,) = call(
            encoder_back_kernel, "encoder_back", [(encoder.shape, F32)], [VM] * 3, [], (kv_near, kv_got, w_keyval), after=[cross_pair],
        )
        up_grad, down_grad, self_in_grad, gain_grad, shift_grad, table_grad, down_bias_grad, up_bias_grad = call(
            place_kernel, "place",
            [((width // 2, ff), F32), ((ff // 2, width), F32), ((width // 2, 3 * width), F32), ((3, width // 2), F32),
             ((3, width // 2), F32), ((steps_count, width // 2), F32), ((1, width // 2), F32), ((4, width // 2), F32)],
            [SM] + [VM] * 9, [pltpu.VMEM((3 * width, width // 2), F32)], (meta, all_ids, *pieces), after=[enc_grad],
        )
        down_bias_grad, up_bias_grad = down_bias_grad.reshape(-1), up_bias_grad.reshape(-1)
        cross_pieces = spread(cross_pair, [up_grad])
        out_g, query_g, cross_g, keyval_g = call(
            place_cross_kernel, "place_cross",
            [((width // 2, width), F32)] * 3 + [((width // 2, 2 * width), F32)],
            [SM] + [VM] * 8, [], (meta, *cross_pieces),
        )
    else:
        def scatter(g, axis=0):
            return lax.psum(lax.psum_scatter(g, "fsdp", scatter_dimension=axis, tiled=True), "ctx")

        down_all = jnp.stack([down_keep, down_send]).reshape(2, 2, 8, 64, width).transpose(1, 0, 2, 3, 4)
        up_all = jnp.stack([up_keep, up_send]).reshape(2, 2, 2, 4, 64, width).transpose(2, 3, 4, 0, 1, 5)
        down_grad, up_grad = scatter(down_all.reshape(ff, width).astype(F32)), scatter(up_all.reshape(width, ff).astype(F32))
        c_all = jnp.stack([jnp.stack([keep0, send0]), jnp.stack([keep1, send1])])
        out_g, query_g, cross_g = (scatter(c_all[:, :, :, k : k + 16].reshape(width, width).astype(F32)) for k in (0, 16, 32))
        keyval_g = scatter(c_all[:, :, :, 48:80].transpose(0, 2, 3, 1, 4).reshape(width, 2 * width).astype(F32))
        kv = jnp.stack([kv_keep, kv_send]).reshape(2, 2, 2, 2, seqs, 2, enc_rows // 16, width).transpose(4, 3, 2, 1, 0, 6, 5, 7)
        kv = lax.psum_scatter(kv.reshape(seqs, enc_rows, 2 * width), "ctx", scatter_dimension=1, tiled=True)
        enc_grad = jnp.einsum("sre,de->srd", kv, w_keyval, preferred_element_type=F32)
        u = jnp.concatenate([u_keep, u_send.astype(F32)], axis=1)
        every_u = lax.all_gather(lax.psum(u[: 3 * hd], "fsdp"), "ctx", axis=0, tiled=False)
        by_head = every_u.reshape(seqs, H, rep, 3, hd, width).sum(axis=(0, 2))
        joined_g = by_head.transpose(3, 1, 0, 2).reshape(width, 3 * width)
        self_in_grad = lax.dynamic_slice_in_dim(joined_g, x * self_in.shape[0], self_in.shape[0], 0)
        total = lax.psum(u[3 * hd :], ("ctx", "fsdp"))
        wide = norm_gain.shape[1]
        extra = lax.dynamic_slice_in_dim(total, x * wide, wide, 1)
        last = extra_rows - 10
        down_bias_grad = extra[last]
        up_bias_all = total[last + 1 : last + 5].reshape(4, 2, width // 2).transpose(1, 0, 2).reshape(-1)
        up_bias_grad = lax.dynamic_slice_in_dim(up_bias_all, x * up_bias.shape[0], up_bias.shape[0], 0)
        gain_grad = jnp.stack([extra[0], extra[last + 7], extra[last + 5]])
        shift_grad = jnp.stack([extra[1], extra[last + 8], extra[last + 6]])
        hot = (jnp.arange(steps_count, dtype=jnp.int32).astype(F32)[:, None, None] == all_ids[None, :, None]).astype(F32)
        table_grad = jnp.sum(hot * extra[None, 2 : 2 + slots, :], axis=1)

    return (
        mixed, tokens_grad, enc_grad, self_in_grad, out_g, query_g, keyval_g, cross_g, up_grad, up_bias_grad,
        down_grad, down_bias_grad, gain_grad, shift_grad, table_grad,
    )


def solution(mesh):
    tok = P("fsdp", "ctx", None)
    row, vec, col = P("fsdp", None), P("fsdp"), P(None, "fsdp")
    in_specs = (tok, tok, vec, tok, row, row, row, row, row, row, vec, row, vec, col, col, col)
    out_specs = (tok, tok, tok, row, row, row, row, row, row, vec, row, vec, col, col, col)
    return jax.shard_map(shards, mesh=mesh, in_specs=in_specs, out_specs=out_specs, check_vma=False)
```

```python
import functools
import math

import jax
import jax.numpy as jnp
from jax import lax
from jax.experimental import pallas as pl
from jax.experimental.pallas import tpu as pltpu
from jax.sharding import PartitionSpec as P

H = 8
EPS = 1e-05
F32 = jnp.float32
BF = jnp.bfloat16
LOG2E = 1.4426950408889634
LARGE, SMALL = 62, 16
ROOMY = ("split", "prepare", "pack", "unpack", "attend", "encoder_rows", "weights_back", "start_grad")


def limit_of(name):
    return (LARGE if name in ROOMY else SMALL) * 1024 * 1024


def nn(a, b):
    return lax.dot_general(a, b, (((1,), (0,)), ((), ())), preferred_element_type=F32)


def nt(a, b):
    return lax.dot_general(a, b, (((1,), (1,)), ((), ())), preferred_element_type=F32)


def flip(v):
    return jnp.transpose(v)


def normalise(v):
    centred = v - jnp.mean(v, axis=-1, keepdims=True)
    r = lax.rsqrt(jnp.mean(centred * centred, axis=-1, keepdims=True) + EPS)
    return centred * r, r


def norm_back(grad, gain, xhat, r):
    u = grad * gain
    return r * (u - jnp.mean(u, axis=-1, keepdims=True) - xhat * jnp.mean(u * xhat, axis=-1, keepdims=True))


def aligned(index, size):
    return pl.ds(pl.multiple_of(index, size), size)


VM = pl.BlockSpec(memory_space=pltpu.VMEM)
SM = pl.BlockSpec(memory_space=pltpu.SMEM)
ANY = pl.BlockSpec(memory_space=pl.ANY)


def call(kernel, name, outs, in_specs, scratch, args, out_specs=None, after=()):
    args = list(args)
    if after:
        args[0] = tie(args[0], *after)
    return pl.pallas_call(
        kernel,
        name=name,
        out_shape=[jax.ShapeDtypeStruct(s, d) for s, d in outs],
        in_specs=in_specs,
        out_specs=out_specs or [VM] * len(outs),
        scratch_shapes=scratch,
        compiler_params=pltpu.CompilerParams(vmem_limit_bytes=limit_of(name)),
        cost_estimate=pl.CostEstimate(flops=1000, bytes_accessed=1000, transcendentals=0),
    )(*args)


class Placer:
    def __init__(self, sems, x, c):
        self.sems, self.x, self.c, self.used = sems, x, c, 0

    def copy(self, src, dst):
        copy = pltpu.make_async_copy(src, dst, self.sems.at[self.used])
        self.used += 1
        copy.start()
        return copy

    def lay(self, own, near, far, dst, row0, blocks):
        rows = own.shape[0]
        half = rows // 2
        base = (1 - self.x) * rows
        copies = [self.copy(own, dst.at[aligned(self.x * rows, rows)])]
        for b in range(blocks):
            cols = pl.ds(b * 512, 512)
            part = pl.ds(row0 + b * half, half)
            copies.append(self.copy(near.at[part], dst.at[aligned(base + self.c * half, half), cols]))
            copies.append(self.copy(far.at[part], dst.at[aligned(base + (1 - self.c) * half, half), cols]))
        return copies


def wait(copies):
    for copy in copies:
        copy.wait()


def split_kernel(meta, tokens, encoder, mine, others):
    rows, span = tokens.shape[1], encoder.shape[1]
    for out, s in ((others, 1 - meta[9]), (mine, meta[9])):
        out[0:rows, :] = tokens[s]
        for k in range(encoder.shape[0]):
            out[rows + k * span : rows + (k + 1) * span, :] = encoder[k]


ORDER = (0, 4, 2, 6, 8, 12, 10, 14, 1, 5, 3, 7, 9, 13, 11, 15)


def attend_kernel(meta, step, gains, shifts, wh, *refs):
    blocks, (xhat_out, joined_out, heads_out, full_out, stats_out, normed, keys) = refs[:-7], refs[-7:]
    n, width = xhat_out.shape
    hd = joined_out.shape[0] // 3
    rows = heads_out.shape[2]
    stats_out[...] = jnp.zeros_like(stats_out)
    for k, block in enumerate(blocks):
        xhat, r = normalise(block[0:rows, :].astype(F32) + step[...])
        at = aligned((meta[7] ^ ORDER[k] if len(blocks) == 16 else k) * rows, rows)
        xhat_out[at, :] = xhat.astype(BF)
        normed[at, :] = (xhat * gains[0:1, :] + shifts[0:1, :]).astype(BF)
        stats_out[1:2, at] = flip(jnp.broadcast_to(r, (rows, 128)))[0:1, :]
    for b in range(n // 512):
        cols = pl.ds(b * 512, 512)
        joined_out[:, cols] = nt(wh[...], normed[cols, :]).astype(BF)
    keys[...] = flip(joined_out[hd : 2 * hd, :].astype(F32)).astype(BF)
    factor = LOG2E / math.sqrt(hd)
    wide = 1024

    def query_block(b, carry):
        cols = aligned(b * wide, wide)
        scores = nn(keys[...], joined_out[0:hd, cols]) * factor
        peak = jnp.max(scores, axis=0, keepdims=True)
        shares = jnp.exp2(scores - peak)
        total = jnp.sum(shares, axis=0, keepdims=True)
        out = nn(joined_out[2 * hd : 3 * hd, :], shares.astype(BF)) * (1.0 / total)
        full_out[:, cols] = out
        stats_out[0:1, cols] = peak + jnp.log2(total)
        for part in range(wide // rows):
            heads_out[b * (wide // rows) + part] = out[:, part * rows : (part + 1) * rows].astype(BF)
        return carry

    lax.fori_loop(0, n // wide, query_block, 0)


def key_blocks(first, joined, full, stats, grads, keys, values, gout, key_grads, query_acc):
    n = full.shape[1]
    hd = joined.shape[0] // 3
    rows = grads.shape[2]
    span = keys.shape[0]
    scale = 1.0 / math.sqrt(hd)
    factor = LOG2E * scale
    for j in range(grads.shape[0]):
        gout[:, j * rows : (j + 1) * rows] = grads[j]
    mine = pl.ds(first, span)
    keys[...] = flip(joined[hd : 2 * hd, mine].astype(F32)).astype(BF)
    values[...] = flip(joined[2 * hd : 3 * hd, mine].astype(F32)).astype(BF)
    delta = jnp.sum(gout[...].astype(F32) * full[...], axis=0, keepdims=True)
    lse = stats[0:1, :]
    wide = 256

    def key_block(b, carry):
        at = aligned(b * wide, wide)
        queries = joined[0:hd, :]
        shares = jnp.exp2(nn(keys[at, :], queries) * factor - lse)
        share_grad = nn(values[at, :], gout[...])
        score_grad = (shares * (share_grad - delta)).astype(BF)
        key_grads[0:hd, at] = (nt(queries, score_grad) * scale).astype(BF)
        key_grads[hd : 2 * hd, at] = nt(gout[...], shares.astype(BF)).astype(BF)
        query_acc[...] += nn(joined[hd : 2 * hd, aligned(first + b * wide, wide)], score_grad)
        return carry

    lax.fori_loop(0, span // wide, key_block, 0)


def attend_back_first(joined, full, stats, grads, query_out, key_out, keys, values, gout):
    query_out[...] = jnp.zeros_like(query_out)
    key_blocks(0, joined, full, stats, grads, keys, values, gout, key_out, query_out)


def attend_back_second(
    meta, joined, full, stats, grads, query_in, key_in, xhat, gains, shifts, wh, extra, joined_grad_out, keep_out, send_out,
    keys, values, gout, key_grads, query_acc, lhs, whole,
):
    x, active, slot = meta[0], meta[3], meta[4]
    n, width = xhat.shape
    hd = joined.shape[0] // 3
    half = width // 2
    rows = grads.shape[2]
    scale = 1.0 / math.sqrt(hd)
    query_acc[...] = query_in[...]
    key_blocks(n // 2, joined, full, stats, grads, keys, values, gout, key_grads, query_acc)
    lhs[0:hd, :] = (query_acc[...] * scale).astype(BF)
    lhs[hd : 3 * hd, 0 : n // 2] = key_in[...]
    lhs[hd : 3 * hd, n // 2 :] = key_grads[...]
    for j in range(joined_grad_out.shape[0]):
        joined_grad_out[j] = lhs[0 : 3 * hd, j * rows : (j + 1) * rows]

    gain, shift = gains[0:1, :], shifts[0:1, :]
    grad = lhs[0 : 3 * hd, :].astype(F32)
    r = stats[1:2, :]
    weight = wh[...].astype(F32)
    bias = jnp.sum(weight * shift, axis=1, keepdims=True)
    mixed_mean = jnp.sum(grad * (joined[...].astype(F32) - bias), axis=0, keepdims=True) * (1.0 / width)
    tail = lhs.shape[0] - 3 * hd
    first = lax.broadcasted_iota(jnp.int32, (tail, n), 0) == 0
    lhs[3 * hd :, :] = jnp.where(first, mixed_mean * r, 0.0).astype(BF)
    product = nn(lhs[...], xhat[...])
    m = product[0 : 3 * hd]
    sums = jnp.sum(grad, axis=1, keepdims=True)
    scaled_sums = jnp.sum(grad * r, axis=1, keepdims=True)
    lead = gain * jnp.sum(weight * scaled_sums, axis=0, keepdims=True)
    start_sum = lead - jnp.mean(lead, axis=1, keepdims=True) - product[3 * hd : 3 * hd + 1]
    on = active.astype(F32)
    whole[0 : 3 * hd, :] = (m * gain + sums * shift) * on
    gain_grad = jnp.sum(weight * m, axis=0, keepdims=True) * on
    shift_grad = jnp.sum(weight * sums, axis=0, keepdims=True) * on
    row = lax.broadcasted_iota(jnp.int32, extra.shape, 0)
    more = jnp.where(row == 0, gain_grad, 0.0) + jnp.where(row == 1, shift_grad, 0.0)
    more = more + jnp.where(row == 2 + slot, start_sum * on, 0.0)
    whole[3 * hd :, :] = extra[...] + more
    keep_out[...] = whole[:, aligned(x * half, half)]
    send_out[...] = whole[:, aligned((1 - x) * half, half)].astype(BF)


def prepare_kernel(meta, ids, weight, gain, shift, table, down_bias, up_bias, out, turned, small):
    width = weight.shape[1] // 3
    hd = width // H
    pair, odd = meta[8] // 2, meta[8] % 2
    for j in range(3):
        turned[...] = flip(weight[:, aligned(j * width + pair * 2 * hd, 2 * hd)])
        out[j * hd : (j + 1) * hd, :] = turned[aligned(odd * hd, hd), :]
    small[...] = jnp.zeros_like(small)
    at = 0
    for part in (gain, shift, table):
        small[at : at + part.shape[0], :] = part[...].astype(F32)
        at += part.shape[0]
    half = small.shape[1]
    for part in (down_bias, up_bias):
        for q in range(part.shape[0] // half):
            small[at : at + 1, :] = part[q * half : (q + 1) * half].astype(F32).reshape(1, half)
            at += 1
    lane = lax.broadcasted_iota(jnp.int32, (1, small.shape[1]), 1)
    line = jnp.zeros((1, small.shape[1]), F32)
    for s in range(2):
        line = line + jnp.where(lane == s, ids[s].astype(F32), 0.0)
    small[at : at + 1, :] = line
    out[3 * hd :, :] = small[...].astype(BF)


def unpack_kernel(
    meta, ids, mine, other, wh_out, gains_out, shifts_out, steps_out, step_out, up_out, down_out, ids_out, both,
):
    x = meta[0]
    rows, half = mine.shape
    head_rows = wh_out.shape[0]
    count = rows - head_rows
    for part, at in ((mine, x), (other, 1 - x)):
        lanes = aligned(at * half, half)
        wh_out[:, lanes] = part[0:head_rows, :]
        both[:, lanes] = part[head_rows:, :].astype(F32)
    gains_out[...] = both[0:3, :]
    shifts_out[...] = both[3:6, :]
    for s in range(2):
        steps_out[s : s + 1, :] = both[pl.ds(6 + ids[s], 1), :]
    step_out[...] = both[pl.ds(6 + ids[meta[9]], 1), :]
    last = count - 8
    down_out[...] = both[last : last + 1, :]
    for q in range(4):
        line = both[last + 1 + q : last + 2 + q, :]
        up_out[:, q * half : (q + 1) * half] = line[:, 0:half]
        up_out[:, (4 + q) * half : (5 + q) * half] = line[:, half:]
    ids_out[...] = both[last + 5 : last + 6, :]


def encoder_kernel(meta, own, near, far, *refs):
    blocks, (enc_out, kvt_out, weight_out, sems) = refs[:-4], refs[-4:]
    put = Placer(sems, meta[0], meta[1])
    copies = put.lay(own, near, far, weight_out, 0, 2)
    rows = enc_out.shape[1] // len(blocks)
    first = blocks[0].shape[0] - enc_out.shape[0] * rows
    for k, block in enumerate(blocks):
        at = aligned((meta[7] ^ ORDER[k] if len(blocks) == 16 else k) * rows, rows)
        for s in range(enc_out.shape[0]):
            enc_out[s, at, :] = block[first + s * rows : first + (s + 1) * rows, :]
    wait(copies)
    for s in range(enc_out.shape[0]):
        for b in range(2):
            kv = nn(enc_out[s], weight_out[:, b * 512 : (b + 1) * 512])
            kvt_out[s, b * 512 : (b + 1) * 512, :] = flip(kv).astype(BF)


def pack_kernel(counts, meta, *refs):
    total = sum(counts)
    weights, outs, sems = refs[:total], refs[total:-1], refs[-1]
    copies = []
    index = 0
    for out, count in zip(outs, counts):
        at = 0
        for weight in weights[index : index + count]:
            half = weight.shape[0] // 2
            for b in range(weight.shape[1] // 512):
                src = weight.at[aligned(meta[1] * half, half), pl.ds(b * 512, 512)]
                copies.append(pltpu.make_async_copy(src, out.at[pl.ds(at, half)], sems.at[len(copies)]))
                copies[-1].start()
                at += half
        index += count
    wait(copies)


GROUPS = (("keyval", "out", "query", "cross", "up"), ("down",), ("joined",))


def chunk_at(meta, k, xr):
    x, c = meta[0], meta[1]
    return x ^ xr, c ^ k


def forward_kernel(
    meta, tokens, steps, att, kvt, gains, shifts, own_out, own_query, own_cross, near2, far2,
    h2_out, h1_out, q_out, crossed_out, shares_out, w_out, w_query, w_cross, sems,
):
    seqs, rows, width = tokens.shape
    hd = width // H
    put = Placer(sems, meta[0], meta[1])
    half = own_out.shape[0] // 2
    c_out = put.lay(own_out, near2, far2, w_out, 2 * half, 1)
    c_query = put.lay(own_query, near2, far2, w_query, 3 * half, 1)
    c_cross = put.lay(own_cross, near2, far2, w_cross, 4 * half, 1)
    factor = LOG2E / math.sqrt(hd)

    wait(c_out)
    for s in range(seqs):
        at = pl.ds(s * rows, rows)
        start = tokens[s].astype(F32) + steps[s : s + 1, :]
        h1_out[at, :] = start + nn(flip(att[s]), w_out[...])
    hidden1 = h1_out[...]
    xhat1, unused = normalise(hidden1)
    wait(c_query)
    q_out[...] = nn((xhat1 * gains[1:2, :] + shifts[1:2, :]).astype(BF), w_query[...]).astype(BF)
    for s in range(seqs):
        for first in range(0, H, TOGETHER):
            heads = range(first, first + TOGETHER)
            scores = [
                nn(q_out[s * rows : (s + 1) * rows, h * hd : (h + 1) * hd], kvt[s, h * hd : (h + 1) * hd, :]) * factor for h in heads
            ]
            peaks = [jnp.max(score, axis=1, keepdims=True) for score in scores]
            shares = [jnp.exp2(score - peak) for score, peak in zip(scores, peaks)]
            totals = [jnp.sum(share, axis=1, keepdims=True) for share in shares]
            lows = [(share * (1.0 / total)).astype(BF) for share, total in zip(shares, totals)]
            got = [nt(kvt[s, width + h * hd : width + (h + 1) * hd, :], low) for h, low in zip(heads, lows)]
            for k, h in enumerate(heads):
                shares_out[s * H + h] = lows[k]
                crossed_out[s, h * hd : (h + 1) * hd, :] = got[k].astype(BF)
    wait(c_cross)
    for s in range(seqs):
        at = pl.ds(s * rows, rows)
        h2_out[at, :] = h1_out[at, :] + nn(flip(crossed_out[s]), w_cross[...])


TOGETHER = 8


def feed_kernel(
    meta, hidden2_in, gains, shifts, up_bias, down_bias, out_grad, own_up, own_down, near2, far2, near3, far3,
    mixed_out, h2g_out, extra_out, down_keep, down_send, up_keep, up_send, w_up, w_down, act_t, n2_t, pre_low, sems,
):
    seqs, rows, width = out_grad.shape
    ff = w_down.shape[0]
    slots = extra_out.shape[0]
    put = Placer(sems, meta[0], meta[1])
    c_up = put.lay(own_up, near2, far2, w_up, 5 * (own_up.shape[0] // 2), 4)
    c_down = put.lay(own_down, near3, far3, w_down, 0, 1)
    hidden2 = hidden2_in[...]
    xhat2, r2 = normalise(hidden2)
    n2 = (xhat2 * gains[2:3, :] + shifts[2:3, :]).astype(BF)
    n2_t[...] = flip(n2)
    grad = jnp.concatenate([out_grad[s] for s in range(seqs)], axis=0)
    top = grad.astype(F32)
    wait(c_up)
    wait(c_down)
    mixed = hidden2 + down_bias[...]
    n2_grad = jnp.zeros_like(hidden2)
    extra_out[...] = jnp.zeros_like(extra_out)
    root = math.sqrt(2.0 / math.pi)
    bias_row = slots - 10
    for b in range(ff // 512):
        cols = pl.ds(b * 512, 512)
        pre = nn(n2, w_up[:, cols]) + up_bias[:, cols]
        square = pre * pre
        bent = jnp.tanh(root * pre * (1.0 + 0.044715 * square))
        act = (0.5 * pre * (1.0 + bent)).astype(BF)
        slope = 0.5 * (1.0 + bent) + 0.5 * root * pre * (1.0 - bent * bent) * (1.0 + 3.0 * 0.044715 * square)
        mixed = mixed + nn(act, w_down[cols, :])
        act_t[cols, :] = flip(act)
        low = (nt(grad, w_down[cols, :]) * slope).astype(BF)
        pre_low[:, cols] = low
        n2_grad = n2_grad + nt(low, w_up[:, cols])
        sums = jnp.sum(low.astype(F32), axis=0, keepdims=True)
        per_half = ff // 512 // 2
        lanes = pl.ds((b // per_half) * 256, 256)
        for piece in range(2):
            row = bias_row + 1 + (b % per_half) * 2 + piece
            extra_out[row : row + 1, lanes] = sums[:, piece * 256 : (piece + 1) * 256]
    for s in range(seqs):
        mixed_out[s] = mixed[s * rows : (s + 1) * rows].astype(BF)
    h2g_out[...] = top + norm_back(n2_grad, gains[2:3, :], xhat2, r2)
    extra_out[bias_row : bias_row + 1, :] = jnp.sum(top, axis=0, keepdims=True)
    extra_out[bias_row + 5 : bias_row + 6, :] = jnp.sum(n2_grad * xhat2, axis=0, keepdims=True)
    extra_out[bias_row + 6 : bias_row + 7, :] = jnp.sum(n2_grad, axis=0, keepdims=True)

    me = meta[2]
    for k in (1, 0):
        down_out, up_out = (down_send, up_send) if k else (down_keep, up_keep)
        for xr in (1, 0):
            xa, ca = chunk_at(meta, k, xr)
            down = nn(act_t[aligned(xa * (ff // 2) + ca * (ff // 4), ff // 4), :], grad).astype(BF)
            up = nn(n2_t[aligned(xa * (width // 2), width // 2), :], pre_low[:, aligned(ca * (ff // 2), ff // 2)])
            up = up.astype(BF)
            for a in range(8):
                at = a ^ me
                down_out[xr * 8 + at] = down[a * 64 : (a + 1) * 64]
                up_out[(at // 4) * 8 + xr * 4 + at % 4] = up[(a % 4) * 64 : (a % 4 + 1) * 64, (a // 4) * 512 : (a // 4 + 1) * 512]


def cross_back_kernel(meta, h2g, q, shares, kvt, own_cross, near2, far2, dq_out, part_out, w_cross, dc, sems):
    width = h2g.shape[1]
    seqs, unused, enc_rows = kvt.shape
    rows = h2g.shape[0] // seqs
    hd = width // H
    scale = 1.0 / math.sqrt(hd)
    put = Placer(sems, meta[0], meta[1])
    half = own_cross.shape[0] // 2
    wait(put.lay(own_cross, near2, far2, w_cross, 4 * half, 1))
    dc[...] = nt(h2g[...].astype(BF), w_cross[...]).astype(BF)
    for s in range(seqs):
        at = slice(s * rows, (s + 1) * rows)
        q_t = flip(q[at, :])
        dc_t = flip(dc[at, :])
        for first in range(0, H, TOGETHER):
            heads = range(first, first + TOGETHER)
            lows = [shares[s * H + h] for h in heads]
            wides = [low.astype(F32) for low in lows]
            share_grads = [nn(dc[at, h * hd : (h + 1) * hd], kvt[s, width + h * hd : width + (h + 1) * hd, :]) for h in heads]
            means = [jnp.sum(wide * grad, axis=1, keepdims=True) for wide, grad in zip(wides, share_grads)]
            score_grads = [(wide * (grad - mean)).astype(BF) for wide, grad, mean in zip(wides, share_grads, means)]
            q_grads = [nt(grad, kvt[s, h * hd : (h + 1) * hd, :]) for h, grad in zip(heads, score_grads)]
            k_grads = [nn(q_t[h * hd : (h + 1) * hd], grad) for h, grad in zip(heads, score_grads)]
            v_grads = [nn(dc_t[h * hd : (h + 1) * hd], low) for h, low in zip(heads, lows)]
            for k, h in enumerate(heads):
                head = slice(h * hd, (h + 1) * hd)
                dq_out[at, head] = (q_grads[k] * scale).astype(BF)
                part_out[s, head, :] = (k_grads[k] * scale).astype(BF)
                part_out[s, width + h * hd : width + (h + 1) * hd, :] = v_grads[k].astype(BF)


def hidden_back_kernel(
    meta, h2g, hidden1, dq, gains, extra_in, own_out, own_query, near2, far2, h1g_out, att_grad_out, extra_out,
    w_out, w_query, sems,
):
    width = h2g.shape[1]
    seqs, unused, rows = att_grad_out.shape
    put = Placer(sems, meta[0], meta[1])
    half = own_out.shape[0] // 2
    c_query = put.lay(own_query, near2, far2, w_query, 3 * half, 1)
    c_out = put.lay(own_out, near2, far2, w_out, 2 * half, 1)
    xhat1, r1 = normalise(hidden1[...])
    wait(c_query)
    n1_grad = nt(dq[...], w_query[...])
    grad1 = h2g[...] + norm_back(n1_grad, gains[1:2, :], xhat1, r1)
    h1g_out[...] = grad1
    low1 = grad1.astype(BF)
    wait(c_out)
    for s in range(seqs):
        att_grad_out[s] = nt(w_out[...], low1[s * rows : (s + 1) * rows]).astype(BF)
    last = extra_out.shape[0] - 10
    row = lax.broadcasted_iota(jnp.int32, extra_out.shape, 0)
    more = jnp.where(row == last + 7, jnp.sum(n1_grad * xhat1, axis=0, keepdims=True), 0.0)
    more = more + jnp.where(row == last + 8, jnp.sum(n1_grad, axis=0, keepdims=True), 0.0)
    for s in range(seqs):
        token_sum = jnp.sum(grad1[s * rows : (s + 1) * rows], axis=0, keepdims=True)
        more = more + jnp.where(row == 2 + meta[5] + s, token_sum, 0.0)
    extra_out[...] = extra_in[...] + more


def weights_back_kernel(
    meta, h2g, h1g, hidden1, crossed, att, dq, part, enc, gains, shifts, keep1, send1, keep0, send0, kv_keep, kv_send,
    n1_t, enc_t, part_t,
):
    width = h2g.shape[1]
    seqs, unused, rows = att.shape
    xhat1, unused = normalise(hidden1[...])
    n1_t[...] = flip((xhat1 * gains[1:2, :] + shifts[1:2, :]).astype(BF))
    low2, low1 = h2g[...].astype(BF), h1g[...].astype(BF)
    enc_rows = enc.shape[1]
    span = enc_rows // 16
    for s in range(seqs):
        enc_t[s] = flip(enc[s])
        part_t[s] = flip(part[s])
    for k in (1, 0):
        out = kv_send if k else kv_keep
        for at in range(8):
            a = at ^ meta[2]
            first = aligned(((a & 1) * 8 + (a & 2) * 2 + (a & 4) // 2 + (meta[1] ^ k)) * span, span)
            for s in range(seqs):
                for j in range(2):
                    row = (s * 2 + j) * span
                    out[at, row : row + span, :] = part_t[s, first, j * width : (j + 1) * width]
    me = meta[2]
    for k in (1, 0):
        for xr in (1, 0):
            out = ((keep0, keep1), (send0, send1))[k][xr]
            xa, ca = chunk_at(meta, k, xr)
            at = aligned(xa * (width // 2) + ca * (width // 4), width // 4)
            outer = jnp.zeros((width // 4, width), F32)
            cross = jnp.zeros((width // 4, width), F32)
            keyval = jnp.zeros((width // 2, width), F32)
            for s in range(seqs):
                mine = slice(s * rows, (s + 1) * rows)
                outer = outer + nn(att[s, at, :], low1[mine])
                cross = cross + nn(crossed[s, at, :], low2[mine])
                keyval = keyval + nt(enc_t[s, aligned(xa * (width // 2), width // 2), :], part[s, aligned(ca * width, width), :])
            query = nn(n1_t[at, :], dq[...]).astype(BF)
            outer, cross, keyval = outer.astype(BF), cross.astype(BF), keyval.astype(BF)
            for a in range(8):
                out[a ^ me, 0:16, :] = outer[a * 16 : (a + 1) * 16]
                out[a ^ me, 16:32, :] = query[a * 16 : (a + 1) * 16]
                out[a ^ me, 32:48, :] = cross[a * 16 : (a + 1) * 16]
                out[a ^ me, 48:80, :] = keyval[a * 32 : (a + 1) * 32]


def start_kernel(meta, grads, tokens, steps, gains, h1g, own, near, far, grad_out, weight, turned, sems):
    seqs, rows, width = tokens.shape
    hd = width // H
    put = Placer(sems, meta[0], meta[1])
    copies = put.lay(own, near, far, weight, 0, 3)
    for s in range(seqs):
        for h in range(H):
            for j in range(3):
                turned[s, j * width + h * hd : j * width + (h + 1) * hd, :] = grads[s, h, j * hd : (j + 1) * hd, :]
    wait(copies)
    for s in range(seqs):
        xhat, r = normalise(tokens[s].astype(F32) + steps[s : s + 1, :])
        grad = nt(flip(turned[s]), weight[...])
        grad_out[s] = h1g[s * rows : (s + 1) * rows, :] + norm_back(grad, gains[0:1, :], xhat, r)


PIECES = [(core, mask + far, far) for core in (0, 1) for mask in (0, 2, 4, 6) for far in (0, 1)]


def place_cross_kernel(meta, *refs):
    pieces, (out_out, query_out, cross_out, keyval_out) = refs[:-4], refs[-4:]
    c, me = meta[1], meta[2]
    for k, (core, mask, index) in enumerate(PIECES):
        block = pieces[k // 2][index].astype(F32)
        a = me ^ mask
        ca = c ^ core
        at = aligned(ca * 128 + a * 16, 16)
        out_out[at, :] = block[0:16]
        query_out[at, :] = block[16:32]
        cross_out[at, :] = block[32:48]
        keyval_out[aligned(a * 32, 32), aligned(ca * 512, 512)] = block[48:80]


def encoder_back_kernel(kv, got, weight, out):
    seqs, span, width = out.shape
    total = (kv[0].astype(F32) + got[0].astype(F32)).astype(BF)
    for s in range(seqs):
        first = s * 2 * span
        keys = nt(total[first : first + span], weight[:, 0:width])
        out[s] = keys + nt(total[first + span : first + 2 * span], weight[:, width:])


def merge_kernel(feed, feed_got, heads, heads_got, out):
    rows = feed.shape[1]
    for k in range(2):
        total = feed[k].astype(F32) + feed_got[1 - k].astype(F32)
        out[0, k * rows : (k + 1) * rows, :] = total.astype(BF)
    total = heads[0].astype(F32) + heads_got[0].astype(F32)
    count, half = total.shape
    split = out.shape[1] - 2 * rows
    out[0, 2 * rows :, 0:half] = total[0:split].astype(BF)
    rest = jnp.concatenate([total[split:], jnp.zeros((2 * split - count, half), F32)], axis=0)
    out[0, 2 * rows :, half:] = rest.astype(BF)


def place_kernel(meta, ids, *refs):
    pieces = refs[:8]
    feed_up, feed_down, grad_out, gain_out, shift_out, table_out, down_out, up_out, stacked = refs[8:]
    c, me, low = meta[1], meta[2], meta[6]
    for k, (core, mask, index) in enumerate(PIECES):
        block = pieces[k // 2][0, index * 128 : (index + 1) * 128, :].astype(F32)
        a = me ^ mask
        ca = c ^ core
        feed_down[aligned(ca * 512 + a * 64, 64), :] = block[0:64]
        feed_up[aligned((a % 4) * 64, 64), aligned(ca * 1024 + (a // 4) * 512, 512)] = block[64:128]
    hd = 64
    half = grad_out.shape[0]
    total = jnp.zeros((16, half), F32)
    for k, mask in enumerate((0, 4, 2, 6, 1, 5, 3, 7)):
        wide = pieces[k][0, 256:368, :].astype(F32)
        block = jnp.concatenate([wide[:, 0:half], wide[0:96, half:]], axis=0)
        head = low ^ mask
        for j in range(3):
            stacked[aligned(j * H * hd + head * hd, hd), :] = block[j * hd : (j + 1) * hd]
        total = total + block[3 * hd :]
    for b in range(3):
        grad_out[:, b * 512 : (b + 1) * 512] = flip(stacked[b * 512 : (b + 1) * 512, :])
    last = total.shape[0] - 10
    for row, (g, b) in enumerate(((0, 1), (last + 7, last + 8), (last + 5, last + 6))):
        gain_out[row : row + 1, :] = total[g : g + 1]
        shift_out[row : row + 1, :] = total[b : b + 1]
    down_out[...] = total[last : last + 1]
    up_out[...] = total[last + 1 : last + 5]
    step = lax.broadcasted_iota(jnp.int32, table_out.shape, 0).astype(F32)
    table = jnp.zeros(table_out.shape, F32)
    for k in range(4):
        lane = (k // 2) * half + k % 2
        table = table + jnp.where(step == ids[:, lane : lane + 1], total[2 + k : 3 + k], 0.0)
    table_out[...] = table


def sums(name, jobs, after=()):
    arrays, plan, outs = [], [], []
    for groups, split in jobs:
        steps, row = [], 0
        for group in groups:
            steps.append((row, range(len(arrays), len(arrays) + len(group))))
            row += group[0].shape[1]
            arrays += group
        blocks, width = groups[0][0].shape[0], groups[0][0].shape[2]
        plan.append((len(outs), blocks, split, steps))
        outs += [((blocks // 2, row, width), BF)] * 2 if split else [((blocks, row, width), BF)]
    count = len(arrays)

    def kernel(*refs):
        results = refs[count:]
        for first, blocks, split, steps in plan:
            for row, which in steps:
                total = refs[which[0]][...].astype(F32)
                for k in which[1:]:
                    total = total + refs[k][...].astype(F32)
                total = total.astype(BF)
                rows = pl.ds(row, total.shape[1])
                if split:
                    results[first][:, rows, :] = total[blocks // 2 :]
                    results[first + 1][:, rows, :] = total[: blocks // 2]
                else:
                    results[first][:, rows, :] = total

    return call(kernel, name, outs, [VM] * count, [], arrays, after=after)


def pair_kernel(mine, got, out):
    for k in range(2):
        out[k] = (mine[k].astype(F32) + got[1 - k].astype(F32)).astype(BF)


def tie(value, *others):
    return lax.optimization_barrier((value,) + others)[0]


def over_ctx(value, mask):
    return lax.ppermute(value, "ctx", [(i, i ^ mask) for i in range(16)])


def over_x(value):
    return lax.ppermute(value, "fsdp", [(0, 1), (1, 0)])


def spread(piece, first=()):
    pieces = [piece] + [over_ctx(piece, mask) for mask in (4, 2, 6)]
    pieces = [tie(p, *first) for p in pieces]
    return pieces + [over_ctx(p, 1) for p in pieces]


def shards(
    tokens, encoder, step_ids, out_grad, self_in, self_out, cross_query, cross_keyval, cross_out,
    ffn_up, up_bias, ffn_down, down_bias, norm_gain, norm_shift, step_table,
):
    nctx, nx = lax.axis_size("ctx"), lax.axis_size("fsdp")
    i, x = lax.axis_index("ctx"), lax.axis_index("fsdp")
    seqs, rows, width = tokens.shape
    hd = width // H
    units = seqs * H
    rep = nctx // units
    unit = i // rep
    s_mine, head = unit // H, unit % H
    n = rows * nctx
    ff = 2048
    fast = nctx == 16 and nx == 2
    steps_count = step_table.shape[0]
    slots = seqs * nx
    extra_rows = -(-(slots + 12) // 16) * 16
    zero = jnp.int32(0)

    xk, c, me = zero, zero, zero
    if fast:
        xk, c, me = x, i & 1, ((i >> 1) & 1) * 4 + ((i >> 2) & 1) * 2 + ((i >> 3) & 1)
    active = (i % rep == 0).astype(jnp.int32)
    meta = jnp.stack([xk, c, me, active, seqs * x + s_mine, seqs * x, i & 7, i, head, s_mine]).astype(jnp.int32)

    if fast:
        mine, others = call(
            split_kernel, "split", [((rows + seqs * encoder.shape[1], width), BF)] * 2, [SM, VM, VM], [], (meta, tokens, encoder),
        )
        got = over_ctx(others, 8)
        blocks = [mine] + [over_ctx(mine, mask) for mask in (4, 2, 6)]
        blocks += [got] + [over_ctx(got, mask) for mask in (4, 2, 6)]
        blocks += [over_ctx(block, 1) for block in blocks]

        (small,) = call(
            prepare_kernel, "prepare", [((256, width // 2), BF)], [SM, SM] + [VM] * 6,
            [pltpu.VMEM((2 * hd, width // 2), BF), pltpu.VMEM((64, width // 2), F32)],
            (meta, step_ids, self_in, norm_gain, norm_shift, step_table, down_bias, up_bias),
            after=[mine],
        )
        own = dict(keyval=cross_keyval, out=self_out, query=cross_query, cross=cross_out, up=ffn_up, down=ffn_down, joined=self_in)

        weights = [own[name] for group in GROUPS for name in group]
        sizes = [sum(own[name].size for name in group) // 1024 for group in GROUPS]
        packed = call(
            functools.partial(pack_kernel, [len(group) for group in GROUPS]), "pack", [((size, 512), BF) for size in sizes],
            [SM] + [ANY] * len(weights), [pltpu.SemaphoreType.DMA((13,))], (meta, *weights), after=[small],
        )
        other_small = over_x(small)
        near2, near3 = (over_x(tie(p, other_small, *blocks[1:5])) for p in packed[:2])
        wh, gains, shifts, steps, step_mine, bias_u, bias_d, all_ids = call(
            unpack_kernel, "unpack",
            [((3 * hd, width), BF), ((3, width), F32), ((3, width), F32), ((seqs, width), F32), ((1, width), F32),
             ((1, ff), F32), ((1, width), F32), ((1, width), F32)],
            [SM, SM, VM, VM], [pltpu.VMEM((64, width), F32)], (meta, step_ids, small, other_small), after=[packed[0]],
        )
    else:
        def gather(w, axis=0):
            return lax.all_gather(w, "fsdp", axis=axis, tiled=True)

        gains, shifts = gather(norm_gain, 1).astype(F32), gather(norm_shift, 1).astype(F32)
        table = gather(step_table, 1)
        bias_d, bias_u = gather(down_bias)[None, :].astype(F32), gather(up_bias)[None, :].astype(F32)
        all_ids = gather(step_ids.astype(BF)).astype(F32)
        full = dict(keyval=gather(cross_keyval), out=gather(self_out), query=gather(cross_query), cross=gather(cross_out),
                    up=gather(ffn_up), down=gather(ffn_down), joined=gather(self_in))
        half_of = {name: w.shape[0] // 2 for name, w in full.items()}
        own = {name: w[: half_of[name]] for name, w in full.items()}

        def group(names, which):
            parts = []
            for name in names:
                rest = full[name][half_of[name] :]
                quarter = half_of[name] // 2
                part = rest[which * quarter : (which + 1) * quarter]
                parts += [part[:, b : b + 512] for b in range(0, part.shape[1], 512)]
            return jnp.concatenate(parts, axis=0)

        (near2, far2), (near3, far3), (near4, far4) = ([group(names, w) for w in (0, 1)] for names in GROUPS)
        by_head = full["joined"].reshape(width, 3, H, hd)
        wh = lax.dynamic_index_in_dim(by_head, head, 2, False).reshape(width, 3 * hd).T
        onehot = (jnp.arange(steps_count, dtype=jnp.int32)[None, :] == step_ids[:, None]).astype(BF)
        steps = jnp.dot(onehot, table, preferred_element_type=F32)
        step_mine = lax.dynamic_index_in_dim(steps, s_mine, 0, True)
        every = lax.all_gather(tokens, "ctx", axis=0, tiled=False)
        chosen = lax.dynamic_index_in_dim(every, s_mine, 1, False)
        encs = lax.all_gather(encoder, "ctx", axis=0, tiled=False)
        blocks = [jnp.concatenate([chosen[j], encs[j].reshape(-1, width)], axis=0) for j in range(nctx)]
    xhat0, joined, heads, attended_full, stats = call(
        attend_kernel, "attend",
        [((n, width), BF), ((3 * hd, n), BF), ((nctx, hd, rows), BF), ((hd, n), F32), ((8, n), F32)],
        [SM] + [VM] * (4 + nctx),
        [pltpu.VMEM((n, width), BF), pltpu.VMEM((n, hd), BF)],
        (meta, step_mine, gains, shifts, wh, *blocks),
    )
    hold = []
    back = lax.all_to_all(heads, "ctx", 0, 0, tiled=True)
    if fast:
        far2 = over_ctx(tie(near2, heads), 1)
    att = back.reshape(units, rep, hd, rows)[:, 0].reshape(seqs, width, rows)

    enc_rows = nctx * encoder.shape[1]
    enc_all, kvt, w_keyval = call(
        encoder_kernel, "encoder_rows",
        [((seqs, enc_rows, width), BF), ((seqs, 2 * width, enc_rows), BF), ((width, 2 * width), BF)],
        [SM, ANY, ANY, ANY] + [VM] * nctx,
        [pltpu.SemaphoreType.DMA((5,))],
        (meta, own["keyval"], near2, far2, *blocks),
    )
    if fast:
        near4 = over_x(tie(packed[2], kvt))
        hold = [near4]

    tall = seqs * rows
    square = pltpu.VMEM((width, width), BF)
    hidden2, hidden1, q, crossed, shares = call(
        forward_kernel, "forward",
        [((tall, width), F32), ((tall, width), F32), ((tall, width), BF), ((seqs, width, rows), BF), ((units, rows, enc_rows), BF)],
        [SM] + [VM] * 6 + [ANY] * 5,
        [square] * 3 + [pltpu.SemaphoreType.DMA((9,))],
        (meta, tokens, steps, att, kvt, gains, shifts, own["out"], own["query"], own["cross"], near2, far2),
    )
    if fast:
        far3 = over_ctx(tie(near3, hidden2), 1)
    mixed, h2g, extra1, down_keep, down_send, up_keep, up_send = call(
        feed_kernel, "feed",
        [((seqs, rows, width), BF), ((tall, width), F32), ((extra_rows, width), F32)] + [((16, 64, width), BF)] * 4,
        [SM] + [VM] * 6 + [ANY] * 6,
        [pltpu.VMEM((width, ff), BF), pltpu.VMEM((ff, width), BF), pltpu.VMEM((ff, tall), BF),
         pltpu.VMEM((width, tall), BF), pltpu.VMEM((tall, ff), BF), pltpu.SemaphoreType.DMA((12,))],
        (meta, hidden2, gains, shifts, bias_u, bias_d, out_grad, own["up"], own["down"], near2, far2, near3, far3),
    )
    hold_far = []
    if fast:
        far4 = over_ctx(tie(near4, h2g), 1)
        hold_far = [far4]
        down_got, up_got = over_ctx(down_send, 1), over_ctx(up_send, 1)
    dq, part = call(
        cross_back_kernel, "cross_back",
        [((tall, width), BF), ((seqs, 2 * width, enc_rows), BF)],
        [SM] + [VM] * 4 + [ANY] * 3,
        [square, pltpu.VMEM((tall, width), BF), pltpu.SemaphoreType.DMA((3,))],
        (meta, h2g, q, shares, kvt, own["cross"], near2, far2),
    )
    hold = []
    if fast:
        down_x, down_kept, up_y, up_kept = sums(
            "reduce_1", [([[down_keep, down_got]], True), ([[up_keep, up_got]], True)], [dq])
        down_x1, up_y1 = over_x(down_x), over_ctx(up_y, 2)
        hold = [down_x]
    h1g, att_grad, extra2 = call(
        hidden_back_kernel, "hidden_back",
        [((tall, width), F32), ((seqs, width, rows), BF), ((extra_rows, width), F32)],
        [SM] + [VM] * 5 + [ANY] * 4,
        [square, square, pltpu.SemaphoreType.DMA((6,))],
        (meta, h2g, hidden1, dq, gains, extra1, own["out"], own["query"], near2, far2),
        after=hold,
    )
    by_unit = att_grad.reshape(units, 1, hd, rows)
    grads = lax.all_to_all(jnp.broadcast_to(by_unit, (units, rep, hd, rows)).reshape(nctx, hd, rows), "ctx", 0, 0, tiled=True)
    keep1, send1, keep0, send0, kv_keep, kv_send = call(
        weights_back_kernel, "weights_back",
        [((8, 80, width), BF)] * 4 + [((8, enc_rows // 4, width), BF)] * 2,
        [SM] + [VM] * 10,
        [pltpu.VMEM((width, tall), BF), pltpu.VMEM((seqs, width, enc_rows), BF), pltpu.VMEM((seqs, enc_rows, 2 * width), BF)],
        (meta, h2g, h1g, hidden1, crossed, att, dq, part, enc_all, gains, shifts), after=hold_far,
    )
    hold = []
    if fast:
        got1, got0, kv_0 = (over_ctx(tie(part, grads, down_x1, up_y1), 1) for part in (send1, send0, kv_send))

        down_y, down_kept, up_x, up_kept = sums(
            "reduce_2", [([[down_kept, down_x1]], True), ([[up_kept, up_y1]], True)], [grads, keep1],
        )
        down_y1, up_x1 = over_ctx(down_y, 2), over_x(up_x)
        hold = [down_y]

    head_scratch = [pltpu.VMEM((n // 2, hd), BF), pltpu.VMEM((n // 2, hd), BF), pltpu.VMEM((hd, n), BF)]
    query_acc, key_half = call(
        attend_back_first, "attend_back_1", [((hd, n), F32), ((2 * hd, n // 2), BF)], [VM] * 4, head_scratch,
        (joined, attended_full, stats, grads), after=hold,
    )
    hold = []
    if fast:
        feed_z, feed_kept, cross_x, cross_kept, kv_y, kv_kept = sums(
            "reduce_3",
            [([[down_kept, down_y1], [up_kept, up_x1]], True), ([[keep1, got1]], False), ([[keep0, got0]], False), ([[kv_keep, kv_0]], True)],
            [query_acc],
        )
        feed_z1, cross_x1, kv_1 = over_ctx(feed_z, 4), over_x(cross_x), over_ctx(kv_y, 2)
        hold = [feed_z]
    joined_grad, u_keep, u_send = call(
        attend_back_second, "attend_back_2",
        [((nctx, 3 * hd, rows), BF), ((3 * hd + extra_rows, width // 2), F32), ((3 * hd + extra_rows, width // 2), BF)],
        [SM] + [VM] * 11,
        head_scratch
        + [pltpu.VMEM((2 * hd, n // 2), BF), pltpu.VMEM((hd, n), F32), pltpu.VMEM((3 * hd + 16, n), BF),
           pltpu.VMEM((3 * hd + extra_rows, width), F32)],
        (meta, joined, attended_full, stats, grads, query_acc, key_half, xhat0, gains, shifts, wh, extra2),
        after=hold,
    )
    if fast:
        joined_grad, u_send = tie(joined_grad, feed_z1, kv_1), tie(u_send, feed_z1, kv_1)
        u_x1 = over_x(u_send)[None]
        feed_w, kv_z, kv_kept, cross_y, cross_kept = sums(
            "reduce_4", [([[feed_kept, feed_z1]], False), ([[kv_kept, kv_1]], True), ([[cross_kept, cross_x1]], True)], [u_send],
        )
        feed_w1, kv_2, cross_y1 = over_ctx(feed_w, 8), over_ctx(kv_z, 4), over_ctx(cross_y, 2)
        cross_z, cross_kept, u_sum = sums("reduce_5", [([[cross_kept, cross_y1]], True), ([[u_keep[None], u_x1]], False)])
        cross_z1, u_8 = over_ctx(cross_z, 4), over_ctx(u_sum, 8)
        (merged,) = call(
            merge_kernel, "reduce_6", [((1, 368, width), BF)], [VM] * 4, [], (feed_w, feed_w1, u_sum, u_8), after=[cross_z1, kv_2],
        )
        cross_w, kv_far, kv_near = sums("reduce_7", [([[cross_kept, cross_z1]], False), ([[kv_kept, kv_2]], True)], [merged])
        cross_w1, kv_got = over_ctx(cross_w, 8), over_ctx(kv_far, 8)
        merged = tie(merged, cross_w)
        spread_out = [over_ctx(merged, mask) for mask in (4, 2, 6)]
        hold = [cross_w]
    dj = lax.all_to_all(joined_grad, "ctx", 0, 0, tiled=True)
    dj = dj.reshape(units, rep, 3 * hd, rows)[:, 0].reshape(seqs, H, 3 * hd, rows)
    (tokens_grad,) = call(
        start_kernel, "start_grad",
        [((seqs, rows, width), F32)],
        [SM] + [VM] * 5 + [ANY] * 3,
        [pltpu.VMEM((width, 3 * width), BF), pltpu.VMEM((seqs, 3 * width, rows), BF), pltpu.SemaphoreType.DMA((7,))],
        (meta, dj, tokens, steps, gains, h1g, own["joined"], near4, far4),
        after=hold,
    )

    if fast:
        (cross_pair,) = call(
            pair_kernel, "reduce_8", [((2, 80, width), BF)], [VM] * 2, [], (cross_w, cross_w1), after=[kv_got, tokens_grad],
        )
        pieces = [tie(piece, cross_pair) for piece in [merged] + spread_out]
        pieces = pieces + [over_ctx(piece, 1) for piece in pieces]
        (enc_grad,) = call(
            encoder_back_kernel, "encoder_back", [(encoder.shape, F32)], [VM] * 3, [], (kv_near, kv_got, w_keyval), after=[cross_pair],
        )
        up_grad, down_grad, self_in_grad, gain_grad, shift_grad, table_grad, down_bias_grad, up_bias_grad = call(
            place_kernel, "place",
            [((width // 2, ff), F32), ((ff // 2, width), F32), ((width // 2, 3 * width), F32), ((3, width // 2), F32),
             ((3, width // 2), F32), ((steps_count, width // 2), F32), ((1, width // 2), F32), ((4, width // 2), F32)],
            [SM] + [VM] * 9, [pltpu.VMEM((3 * width, width // 2), F32)], (meta, all_ids, *pieces), after=[enc_grad],
        )
        down_bias_grad, up_bias_grad = down_bias_grad.reshape(-1), up_bias_grad.reshape(-1)
        cross_pieces = spread(cross_pair, [up_grad])
        out_g, query_g, cross_g, keyval_g = call(
            place_cross_kernel, "place_cross",
            [((width // 2, width), F32)] * 3 + [((width // 2, 2 * width), F32)],
            [SM] + [VM] * 8, [], (meta, *cross_pieces),
        )
    else:
        def scatter(g, axis=0):
            return lax.psum(lax.psum_scatter(g, "fsdp", scatter_dimension=axis, tiled=True), "ctx")

        down_all = jnp.stack([down_keep, down_send]).reshape(2, 2, 8, 64, width).transpose(1, 0, 2, 3, 4)
        up_all = jnp.stack([up_keep, up_send]).reshape(2, 2, 2, 4, 64, width).transpose(2, 3, 4, 0, 1, 5)
        down_grad, up_grad = scatter(down_all.reshape(ff, width).astype(F32)), scatter(up_all.reshape(width, ff).astype(F32))
        c_all = jnp.stack([jnp.stack([keep0, send0]), jnp.stack([keep1, send1])])
        out_g, query_g, cross_g = (scatter(c_all[:, :, :, k : k + 16].reshape(width, width).astype(F32)) for k in (0, 16, 32))
        keyval_g = scatter(c_all[:, :, :, 48:80].transpose(0, 2, 3, 1, 4).reshape(width, 2 * width).astype(F32))
        kv = jnp.stack([kv_keep, kv_send]).reshape(2, 2, 2, 2, seqs, 2, enc_rows // 16, width).transpose(4, 3, 2, 1, 0, 6, 5, 7)
        kv = lax.psum_scatter(kv.reshape(seqs, enc_rows, 2 * width), "ctx", scatter_dimension=1, tiled=True)
        enc_grad = jnp.einsum("sre,de->srd", kv, w_keyval, preferred_element_type=F32)
        u = jnp.concatenate([u_keep, u_send.astype(F32)], axis=1)
        every_u = lax.all_gather(lax.psum(u[: 3 * hd], "fsdp"), "ctx", axis=0, tiled=False)
        by_head = every_u.reshape(seqs, H, rep, 3, hd, width).sum(axis=(0, 2))
        joined_g = by_head.transpose(3, 1, 0, 2).reshape(width, 3 * width)
        self_in_grad = lax.dynamic_slice_in_dim(joined_g, x * self_in.shape[0], self_in.shape[0], 0)
        total = lax.psum(u[3 * hd :], ("ctx", "fsdp"))
        wide = norm_gain.shape[1]
        extra = lax.dynamic_slice_in_dim(total, x * wide, wide, 1)
        last = extra_rows - 10
        down_bias_grad = extra[last]
        up_bias_all = total[last + 1 : last + 5].reshape(4, 2, width // 2).transpose(1, 0, 2).reshape(-1)
        up_bias_grad = lax.dynamic_slice_in_dim(up_bias_all, x * up_bias.shape[0], up_bias.shape[0], 0)
        gain_grad = jnp.stack([extra[0], extra[last + 7], extra[last + 5]])
        shift_grad = jnp.stack([extra[1], extra[last + 8], extra[last + 6]])
        hot = (jnp.arange(steps_count, dtype=jnp.int32).astype(F32)[:, None, None] == all_ids[None, :, None]).astype(F32)
        table_grad = jnp.sum(hot * extra[None, 2 : 2 + slots, :], axis=1)

    return (
        mixed, tokens_grad, enc_grad, self_in_grad, out_g, query_g, keyval_g, cross_g, up_grad, up_bias_grad,
        down_grad, down_bias_grad, gain_grad, shift_grad, table_grad,
    )


def solution(mesh):
    tok = P("fsdp", "ctx", None)
    row, vec, col = P("fsdp", None), P("fsdp"), P(None, "fsdp")
    in_specs = (tok, tok, vec, tok, row, row, row, row, row, row, vec, row, vec, col, col, col)
    out_specs = (tok, tok, tok, row, row, row, row, row, row, vec, row, vec, col, col, col)
    return jax.shard_map(shards, mesh=mesh, in_specs=in_specs, out_specs=out_specs, check_vma=False)
```

```python
import functools
import math

import jax
import jax.numpy as jnp
from jax import lax
from jax.experimental import pallas as pl
from jax.experimental.pallas import tpu as pltpu
from jax.sharding import PartitionSpec as P

H = 8
EPS = 1e-05
F32 = jnp.float32
BF = jnp.bfloat16
LOG2E = 1.4426950408889634
LARGE, SMALL = 62, 32
ROOMY = ("split", "prepare", "pack", "unpack", "attend", "encoder_rows", "weights_back")


def limit_of(name):
    return (LARGE if name in ROOMY else SMALL) * 1024 * 1024


def nn(a, b):
    return lax.dot_general(a, b, (((1,), (0,)), ((), ())), preferred_element_type=F32)


def nt(a, b):
    return lax.dot_general(a, b, (((1,), (1,)), ((), ())), preferred_element_type=F32)


def flip(v):
    return jnp.transpose(v)


def normalise(v):
    centred = v - jnp.mean(v, axis=-1, keepdims=True)
    r = lax.rsqrt(jnp.mean(centred * centred, axis=-1, keepdims=True) + EPS)
    return centred * r, r


def norm_back(grad, gain, xhat, r):
    u = grad * gain
    return r * (u - jnp.mean(u, axis=-1, keepdims=True) - xhat * jnp.mean(u * xhat, axis=-1, keepdims=True))


def aligned(index, size):
    return pl.ds(pl.multiple_of(index, size), size)


VM = pl.BlockSpec(memory_space=pltpu.VMEM)
SM = pl.BlockSpec(memory_space=pltpu.SMEM)
ANY = pl.BlockSpec(memory_space=pl.ANY)


def call(kernel, name, outs, in_specs, scratch, args, out_specs=None, after=()):
    args = list(args)
    if after:
        args[0] = tie(args[0], *after)
    return pl.pallas_call(
        kernel,
        name=name,
        out_shape=[jax.ShapeDtypeStruct(s, d) for s, d in outs],
        in_specs=in_specs,
        out_specs=out_specs or [VM] * len(outs),
        scratch_shapes=scratch,
        compiler_params=pltpu.CompilerParams(vmem_limit_bytes=limit_of(name)),
        cost_estimate=pl.CostEstimate(flops=1000, bytes_accessed=1000, transcendentals=0),
    )(*args)


class Placer:
    def __init__(self, sems, x, c):
        self.sems, self.x, self.c, self.used = sems, x, c, 0

    def copy(self, src, dst):
        copy = pltpu.make_async_copy(src, dst, self.sems.at[self.used])
        self.used += 1
        copy.start()
        return copy

    def lay(self, own, near, far, dst, row0, blocks):
        rows = own.shape[0]
        half = rows // 2
        base = (1 - self.x) * rows
        copies = [self.copy(own, dst.at[aligned(self.x * rows, rows)])]
        for b in range(blocks):
            cols = pl.ds(b * 512, 512)
            part = pl.ds(row0 + b * half, half)
            copies.append(self.copy(near.at[part], dst.at[aligned(base + self.c * half, half), cols]))
            copies.append(self.copy(far.at[part], dst.at[aligned(base + (1 - self.c) * half, half), cols]))
        return copies


def wait(copies):
    for copy in copies:
        copy.wait()


def split_kernel(meta, tokens, encoder, mine, others):
    rows, span = tokens.shape[1], encoder.shape[1]
    for out, s in ((others, 1 - meta[9]), (mine, meta[9])):
        out[0:rows, :] = tokens[s]
        for k in range(encoder.shape[0]):
            out[rows + k * span : rows + (k + 1) * span, :] = encoder[k]


ORDER = (0, 4, 2, 6, 8, 12, 10, 14, 1, 5, 3, 7, 9, 13, 11, 15)


def attend_kernel(meta, step, gains, shifts, wh, *refs):
    blocks, (xhat_out, joined_out, heads_out, full_out, stats_out, normed, keys) = refs[:-7], refs[-7:]
    n, width = xhat_out.shape
    hd = joined_out.shape[0] // 3
    rows = heads_out.shape[2]
    stats_out[...] = jnp.zeros_like(stats_out)
    for k, block in enumerate(blocks):
        xhat, r = normalise(block[0:rows, :].astype(F32) + step[...])
        at = aligned((meta[7] ^ ORDER[k] if len(blocks) == 16 else k) * rows, rows)
        xhat_out[at, :] = xhat.astype(BF)
        normed[at, :] = (xhat * gains[0:1, :] + shifts[0:1, :]).astype(BF)
        stats_out[1:2, at] = flip(jnp.broadcast_to(r, (rows, 128)))[0:1, :]
    for b in range(n // 512):
        cols = pl.ds(b * 512, 512)
        joined_out[:, cols] = nt(wh[...], normed[cols, :]).astype(BF)
    keys[...] = flip(joined_out[hd : 2 * hd, :].astype(F32)).astype(BF)
    factor = LOG2E / math.sqrt(hd)
    wide = 1024

    def query_block(b, carry):
        cols = aligned(b * wide, wide)
        scores = nn(keys[...], joined_out[0:hd, cols]) * factor
        peak = jnp.max(scores, axis=0, keepdims=True)
        shares = jnp.exp2(scores - peak)
        total = jnp.sum(shares, axis=0, keepdims=True)
        out = nn(joined_out[2 * hd : 3 * hd, :], shares.astype(BF)) * (1.0 / total)
        full_out[:, cols] = out
        stats_out[0:1, cols] = peak + jnp.log2(total)
        for part in range(wide // rows):
            heads_out[b * (wide // rows) + part] = out[:, part * rows : (part + 1) * rows].astype(BF)
        return carry

    lax.fori_loop(0, n // wide, query_block, 0)


def key_blocks(first, joined, full, stats, grads, keys, values, gout, key_grads, query_acc):
    n = full.shape[1]
    hd = joined.shape[0] // 3
    rows = grads.shape[2]
    span = keys.shape[0]
    scale = 1.0 / math.sqrt(hd)
    factor = LOG2E * scale
    for j in range(grads.shape[0]):
        gout[:, j * rows : (j + 1) * rows] = grads[j]
    mine = pl.ds(first, span)
    keys[...] = flip(joined[hd : 2 * hd, mine].astype(F32)).astype(BF)
    values[...] = flip(joined[2 * hd : 3 * hd, mine].astype(F32)).astype(BF)
    delta = jnp.sum(gout[...].astype(F32) * full[...], axis=0, keepdims=True)
    lse = stats[0:1, :]
    wide = 256

    def key_block(b, carry):
        at = aligned(b * wide, wide)
        queries = joined[0:hd, :]
        shares = jnp.exp2(nn(keys[at, :], queries) * factor - lse)
        share_grad = nn(values[at, :], gout[...])
        score_grad = (shares * (share_grad - delta)).astype(BF)
        key_grads[0:hd, at] = (nt(queries, score_grad) * scale).astype(BF)
        key_grads[hd : 2 * hd, at] = nt(gout[...], shares.astype(BF)).astype(BF)
        query_acc[...] += nn(joined[hd : 2 * hd, aligned(first + b * wide, wide)], score_grad)
        return carry

    lax.fori_loop(0, span // wide, key_block, 0)


def attend_back_first(joined, full, stats, grads, query_out, key_out, keys, values, gout):
    query_out[...] = jnp.zeros_like(query_out)
    key_blocks(0, joined, full, stats, grads, keys, values, gout, key_out, query_out)


def attend_back_second(
    meta, joined, full, stats, grads, query_in, key_in, xhat, gains, shifts, wh, extra, joined_grad_out, keep_out, send_out,
    keys, values, gout, key_grads, query_acc, lhs, whole,
):
    x, active, slot = meta[0], meta[3], meta[4]
    n, width = xhat.shape
    hd = joined.shape[0] // 3
    half = width // 2
    rows = grads.shape[2]
    scale = 1.0 / math.sqrt(hd)
    query_acc[...] = query_in[...]
    key_blocks(n // 2, joined, full, stats, grads, keys, values, gout, key_grads, query_acc)
    lhs[0:hd, :] = (query_acc[...] * scale).astype(BF)
    lhs[hd : 3 * hd, 0 : n // 2] = key_in[...]
    lhs[hd : 3 * hd, n // 2 :] = key_grads[...]
    for j in range(joined_grad_out.shape[0]):
        joined_grad_out[j] = lhs[0 : 3 * hd, j * rows : (j + 1) * rows]

    gain, shift = gains[0:1, :], shifts[0:1, :]
    grad = lhs[0 : 3 * hd, :].astype(F32)
    r = stats[1:2, :]
    weight = wh[...].astype(F32)
    bias = jnp.sum(weight * shift, axis=1, keepdims=True)
    mixed_mean = jnp.sum(grad * (joined[...].astype(F32) - bias), axis=0, keepdims=True) * (1.0 / width)
    tail = lhs.shape[0] - 3 * hd
    first = lax.broadcasted_iota(jnp.int32, (tail, n), 0) == 0
    lhs[3 * hd :, :] = jnp.where(first, mixed_mean * r, 0.0).astype(BF)
    product = nn(lhs[...], xhat[...])
    m = product[0 : 3 * hd]
    sums = jnp.sum(grad, axis=1, keepdims=True)
    scaled_sums = jnp.sum(grad * r, axis=1, keepdims=True)
    lead = gain * jnp.sum(weight * scaled_sums, axis=0, keepdims=True)
    start_sum = lead - jnp.mean(lead, axis=1, keepdims=True) - product[3 * hd : 3 * hd + 1]
    on = active.astype(F32)
    whole[0 : 3 * hd, :] = (m * gain + sums * shift) * on
    gain_grad = jnp.sum(weight * m, axis=0, keepdims=True) * on
    shift_grad = jnp.sum(weight * sums, axis=0, keepdims=True) * on
    row = lax.broadcasted_iota(jnp.int32, extra.shape, 0)
    more = jnp.where(row == 0, gain_grad, 0.0) + jnp.where(row == 1, shift_grad, 0.0)
    more = more + jnp.where(row == 2 + slot, start_sum * on, 0.0)
    whole[3 * hd :, :] = extra[...] + more
    keep_out[...] = whole[:, aligned(x * half, half)]
    send_out[...] = whole[:, aligned((1 - x) * half, half)].astype(BF)


def prepare_kernel(meta, ids, weight, gain, shift, table, down_bias, up_bias, out, turned, small):
    width = weight.shape[1] // 3
    hd = width // H
    pair, odd = meta[8] // 2, meta[8] % 2
    for j in range(3):
        turned[...] = flip(weight[:, aligned(j * width + pair * 2 * hd, 2 * hd)])
        out[j * hd : (j + 1) * hd, :] = turned[aligned(odd * hd, hd), :]
    small[...] = jnp.zeros_like(small)
    at = 0
    for part in (gain, shift, table):
        small[at : at + part.shape[0], :] = part[...].astype(F32)
        at += part.shape[0]
    half = small.shape[1]
    for part in (down_bias, up_bias):
        for q in range(part.shape[0] // half):
            small[at : at + 1, :] = part[q * half : (q + 1) * half].astype(F32).reshape(1, half)
            at += 1
    lane = lax.broadcasted_iota(jnp.int32, (1, small.shape[1]), 1)
    line = jnp.zeros((1, small.shape[1]), F32)
    for s in range(2):
        line = line + jnp.where(lane == s, ids[s].astype(F32), 0.0)
    small[at : at + 1, :] = line
    out[3 * hd :, :] = small[...].astype(BF)


def unpack_kernel(
    meta, ids, mine, other, wh_out, gains_out, shifts_out, steps_out, step_out, up_out, down_out, ids_out, both,
):
    x = meta[0]
    rows, half = mine.shape
    head_rows = wh_out.shape[0]
    count = rows - head_rows
    for part, at in ((mine, x), (other, 1 - x)):
        lanes = aligned(at * half, half)
        wh_out[:, lanes] = part[0:head_rows, :]
        both[:, lanes] = part[head_rows:, :].astype(F32)
    gains_out[...] = both[0:3, :]
    shifts_out[...] = both[3:6, :]
    for s in range(2):
        steps_out[s : s + 1, :] = both[pl.ds(6 + ids[s], 1), :]
    step_out[...] = both[pl.ds(6 + ids[meta[9]], 1), :]
    last = count - 8
    down_out[...] = both[last : last + 1, :]
    for q in range(4):
        line = both[last + 1 + q : last + 2 + q, :]
        up_out[:, q * half : (q + 1) * half] = line[:, 0:half]
        up_out[:, (4 + q) * half : (5 + q) * half] = line[:, half:]
    ids_out[...] = both[last + 5 : last + 6, :]


def encoder_kernel(meta, own, near, far, *refs):
    blocks, (enc_out, kvt_out, weight_out, sems) = refs[:-4], refs[-4:]
    put = Placer(sems, meta[0], meta[1])
    copies = put.lay(own, near, far, weight_out, 0, 2)
    rows = enc_out.shape[1] // len(blocks)
    first = blocks[0].shape[0] - enc_out.shape[0] * rows
    for k, block in enumerate(blocks):
        at = aligned((meta[7] ^ ORDER[k] if len(blocks) == 16 else k) * rows, rows)
        for s in range(enc_out.shape[0]):
            enc_out[s, at, :] = block[first + s * rows : first + (s + 1) * rows, :]
    wait(copies)
    for s in range(enc_out.shape[0]):
        for b in range(2):
            kv = nn(enc_out[s], weight_out[:, b * 512 : (b + 1) * 512])
            kvt_out[s, b * 512 : (b + 1) * 512, :] = flip(kv).astype(BF)


def pack_kernel(counts, meta, *refs):
    total = sum(counts)
    weights, outs, sems = refs[:total], refs[total:-1], refs[-1]
    copies = []
    index = 0
    for out, count in zip(outs, counts):
        at = 0
        for weight in weights[index : index + count]:
            half = weight.shape[0] // 2
            for b in range(weight.shape[1] // 512):
                src = weight.at[aligned(meta[1] * half, half), pl.ds(b * 512, 512)]
                copies.append(pltpu.make_async_copy(src, out.at[pl.ds(at, half)], sems.at[len(copies)]))
                copies[-1].start()
                at += half
        index += count
    wait(copies)


GROUPS = (("keyval", "out", "query", "cross", "up"), ("down",), ("joined",))


def chunk_at(meta, k, xr):
    x, c = meta[0], meta[1]
    return x ^ xr, c ^ k


def forward_kernel(
    meta, tokens, steps, att, kvt, gains, shifts, own_out, own_query, own_cross, near2, far2,
    h2_out, h1_out, q_out, crossed_out, shares_out, w_out, w_query, w_cross, sems,
):
    seqs, rows, width = tokens.shape
    hd = width // H
    put = Placer(sems, meta[0], meta[1])
    half = own_out.shape[0] // 2
    c_out = put.lay(own_out, near2, far2, w_out, 2 * half, 1)
    c_query = put.lay(own_query, near2, far2, w_query, 3 * half, 1)
    c_cross = put.lay(own_cross, near2, far2, w_cross, 4 * half, 1)
    factor = LOG2E / math.sqrt(hd)

    wait(c_out)
    for s in range(seqs):
        at = pl.ds(s * rows, rows)
        start = tokens[s].astype(F32) + steps[s : s + 1, :]
        h1_out[at, :] = start + nn(flip(att[s]), w_out[...])
    hidden1 = h1_out[...]
    xhat1, unused = normalise(hidden1)
    wait(c_query)
    q_out[...] = nn((xhat1 * gains[1:2, :] + shifts[1:2, :]).astype(BF), w_query[...]).astype(BF)
    for s in range(seqs):
        for first in range(0, H, TOGETHER):
            heads = range(first, first + TOGETHER)
            scores = [
                nn(q_out[s * rows : (s + 1) * rows, h * hd : (h + 1) * hd], kvt[s, h * hd : (h + 1) * hd, :]) * factor for h in heads
            ]
            peaks = [jnp.max(score, axis=1, keepdims=True) for score in scores]
            shares = [jnp.exp2(score - peak) for score, peak in zip(scores, peaks)]
            totals = [jnp.sum(share, axis=1, keepdims=True) for share in shares]
            lows = [(share * (1.0 / total)).astype(BF) for share, total in zip(shares, totals)]
            got = [nt(kvt[s, width + h * hd : width + (h + 1) * hd, :], low) for h, low in zip(heads, lows)]
            for k, h in enumerate(heads):
                shares_out[s * H + h] = lows[k]
                crossed_out[s, h * hd : (h + 1) * hd, :] = got[k].astype(BF)
    wait(c_cross)
    for s in range(seqs):
        at = pl.ds(s * rows, rows)
        h2_out[at, :] = h1_out[at, :] + nn(flip(crossed_out[s]), w_cross[...])


TOGETHER = 8


def feed_kernel(
    meta, hidden2_in, gains, shifts, up_bias, down_bias, out_grad, own_up, own_down, near2, far2, near3, far3,
    mixed_out, h2g_out, extra_out, down_keep, down_send, up_keep, up_send, w_up, w_down, act_t, n2_t, pre_low, sems,
):
    seqs, rows, width = out_grad.shape
    ff = w_down.shape[0]
    slots = extra_out.shape[0]
    put = Placer(sems, meta[0], meta[1])
    c_up = put.lay(own_up, near2, far2, w_up, 5 * (own_up.shape[0] // 2), 4)
    c_down = put.lay(own_down, near3, far3, w_down, 0, 1)
    hidden2 = hidden2_in[...]
    xhat2, r2 = normalise(hidden2)
    n2 = (xhat2 * gains[2:3, :] + shifts[2:3, :]).astype(BF)
    n2_t[...] = flip(n2)
    grad = jnp.concatenate([out_grad[s] for s in range(seqs)], axis=0)
    top = grad.astype(F32)
    wait(c_up)
    wait(c_down)
    mixed = hidden2 + down_bias[...]
    n2_grad = jnp.zeros_like(hidden2)
    extra_out[...] = jnp.zeros_like(extra_out)
    root = math.sqrt(2.0 / math.pi)
    bias_row = slots - 10
    for b in range(ff // 512):
        cols = pl.ds(b * 512, 512)
        pre = nn(n2, w_up[:, cols]) + up_bias[:, cols]
        square = pre * pre
        bent = jnp.tanh(root * pre * (1.0 + 0.044715 * square))
        act = (0.5 * pre * (1.0 + bent)).astype(BF)
        slope = 0.5 * (1.0 + bent) + 0.5 * root * pre * (1.0 - bent * bent) * (1.0 + 3.0 * 0.044715 * square)
        mixed = mixed + nn(act, w_down[cols, :])
        act_t[cols, :] = flip(act)
        low = (nt(grad, w_down[cols, :]) * slope).astype(BF)
        pre_low[:, cols] = low
        n2_grad = n2_grad + nt(low, w_up[:, cols])
        sums = jnp.sum(low.astype(F32), axis=0, keepdims=True)
        per_half = ff // 512 // 2
        lanes = pl.ds((b // per_half) * 256, 256)
        for piece in range(2):
            row = bias_row + 1 + (b % per_half) * 2 + piece
            extra_out[row : row + 1, lanes] = sums[:, piece * 256 : (piece + 1) * 256]
    for s in range(seqs):
        mixed_out[s] = mixed[s * rows : (s + 1) * rows].astype(BF)
    h2g_out[...] = top + norm_back(n2_grad, gains[2:3, :], xhat2, r2)
    extra_out[bias_row : bias_row + 1, :] = jnp.sum(top, axis=0, keepdims=True)
    extra_out[bias_row + 5 : bias_row + 6, :] = jnp.sum(n2_grad * xhat2, axis=0, keepdims=True)
    extra_out[bias_row + 6 : bias_row + 7, :] = jnp.sum(n2_grad, axis=0, keepdims=True)

    me = meta[2]
    for k in (1, 0):
        down_out, up_out = (down_send, up_send) if k else (down_keep, up_keep)
        for xr in (1, 0):
            xa, ca = chunk_at(meta, k, xr)
            down = nn(act_t[aligned(xa * (ff // 2) + ca * (ff // 4), ff // 4), :], grad).astype(BF)
            up = nn(n2_t[aligned(xa * (width // 2), width // 2), :], pre_low[:, aligned(ca * (ff // 2), ff // 2)])
            up = up.astype(BF)
            for a in range(8):
                at = a ^ me
                down_out[xr * 8 + at] = down[a * 64 : (a + 1) * 64]
                up_out[(at // 4) * 8 + xr * 4 + at % 4] = up[(a % 4) * 64 : (a % 4 + 1) * 64, (a // 4) * 512 : (a // 4 + 1) * 512]


def cross_back_kernel(meta, h2g, q, shares, kvt, own_cross, near2, far2, dq_out, part_out, w_cross, dc, sems):
    width = h2g.shape[1]
    seqs, unused, enc_rows = kvt.shape
    rows = h2g.shape[0] // seqs
    hd = width // H
    scale = 1.0 / math.sqrt(hd)
    put = Placer(sems, meta[0], meta[1])
    half = own_cross.shape[0] // 2
    wait(put.lay(own_cross, near2, far2, w_cross, 4 * half, 1))
    dc[...] = nt(h2g[...].astype(BF), w_cross[...]).astype(BF)
    for s in range(seqs):
        at = slice(s * rows, (s + 1) * rows)
        q_t = flip(q[at, :])
        dc_t = flip(dc[at, :])
        for first in range(0, H, TOGETHER):
            heads = range(first, first + TOGETHER)
            lows = [shares[s * H + h] for h in heads]
            wides = [low.astype(F32) for low in lows]
            share_grads = [nn(dc[at, h * hd : (h + 1) * hd], kvt[s, width + h * hd : width + (h + 1) * hd, :]) for h in heads]
            means = [jnp.sum(wide * grad, axis=1, keepdims=True) for wide, grad in zip(wides, share_grads)]
            score_grads = [(wide * (grad - mean)).astype(BF) for wide, grad, mean in zip(wides, share_grads, means)]
            q_grads = [nt(grad, kvt[s, h * hd : (h + 1) * hd, :]) for h, grad in zip(heads, score_grads)]
            k_grads = [nn(q_t[h * hd : (h + 1) * hd], grad) for h, grad in zip(heads, score_grads)]
            v_grads = [nn(dc_t[h * hd : (h + 1) * hd], low) for h, low in zip(heads, lows)]
            for k, h in enumerate(heads):
                head = slice(h * hd, (h + 1) * hd)
                dq_out[at, head] = (q_grads[k] * scale).astype(BF)
                part_out[s, head, :] = (k_grads[k] * scale).astype(BF)
                part_out[s, width + h * hd : width + (h + 1) * hd, :] = v_grads[k].astype(BF)


def hidden_back_kernel(
    meta, h2g, hidden1, dq, gains, extra_in, own_out, own_query, near2, far2, h1g_out, att_grad_out, extra_out,
    w_out, w_query, sems,
):
    width = h2g.shape[1]
    seqs, unused, rows = att_grad_out.shape
    put = Placer(sems, meta[0], meta[1])
    half = own_out.shape[0] // 2
    c_query = put.lay(own_query, near2, far2, w_query, 3 * half, 1)
    c_out = put.lay(own_out, near2, far2, w_out, 2 * half, 1)
    xhat1, r1 = normalise(hidden1[...])
    wait(c_query)
    n1_grad = nt(dq[...], w_query[...])
    grad1 = h2g[...] + norm_back(n1_grad, gains[1:2, :], xhat1, r1)
    h1g_out[...] = grad1
    low1 = grad1.astype(BF)
    wait(c_out)
    for s in range(seqs):
        att_grad_out[s] = nt(w_out[...], low1[s * rows : (s + 1) * rows]).astype(BF)
    last = extra_out.shape[0] - 10
    row = lax.broadcasted_iota(jnp.int32, extra_out.shape, 0)
    more = jnp.where(row == last + 7, jnp.sum(n1_grad * xhat1, axis=0, keepdims=True), 0.0)
    more = more + jnp.where(row == last + 8, jnp.sum(n1_grad, axis=0, keepdims=True), 0.0)
    for s in range(seqs):
        token_sum = jnp.sum(grad1[s * rows : (s + 1) * rows], axis=0, keepdims=True)
        more = more + jnp.where(row == 2 + meta[5] + s, token_sum, 0.0)
    extra_out[...] = extra_in[...] + more


def weights_back_kernel(
    meta, h2g, h1g, hidden1, crossed, att, dq, part, enc, gains, shifts, keep1, send1, keep0, send0, kv_keep, kv_send,
    n1_t, enc_t, part_t,
):
    width = h2g.shape[1]
    seqs, unused, rows = att.shape
    xhat1, unused = normalise(hidden1[...])
    n1_t[...] = flip((xhat1 * gains[1:2, :] + shifts[1:2, :]).astype(BF))
    low2, low1 = h2g[...].astype(BF), h1g[...].astype(BF)
    enc_rows = enc.shape[1]
    span = enc_rows // 16
    for s in range(seqs):
        enc_t[s] = flip(enc[s])
        part_t[s] = flip(part[s])
    for k in (1, 0):
        out = kv_send if k else kv_keep
        for at in range(8):
            a = at ^ meta[2]
            first = aligned(((a & 1) * 8 + (a & 2) * 2 + (a & 4) // 2 + (meta[1] ^ k)) * span, span)
            for s in range(seqs):
                for j in range(2):
                    row = (s * 2 + j) * span
                    out[at, row : row + span, :] = part_t[s, first, j * width : (j + 1) * width]
    me = meta[2]
    for k in (1, 0):
        for xr in (1, 0):
            out = ((keep0, keep1), (send0, send1))[k][xr]
            xa, ca = chunk_at(meta, k, xr)
            at = aligned(xa * (width // 2) + ca * (width // 4), width // 4)
            outer = jnp.zeros((width // 4, width), F32)
            cross = jnp.zeros((width // 4, width), F32)
            keyval = jnp.zeros((width // 2, width), F32)
            for s in range(seqs):
                mine = slice(s * rows, (s + 1) * rows)
                outer = outer + nn(att[s, at, :], low1[mine])
                cross = cross + nn(crossed[s, at, :], low2[mine])
                keyval = keyval + nt(enc_t[s, aligned(xa * (width // 2), width // 2), :], part[s, aligned(ca * width, width), :])
            query = nn(n1_t[at, :], dq[...]).astype(BF)
            outer, cross, keyval = outer.astype(BF), cross.astype(BF), keyval.astype(BF)
            for a in range(8):
                out[a ^ me, 0:16, :] = outer[a * 16 : (a + 1) * 16]
                out[a ^ me, 16:32, :] = query[a * 16 : (a + 1) * 16]
                out[a ^ me, 32:48, :] = cross[a * 16 : (a + 1) * 16]
                out[a ^ me, 48:80, :] = keyval[a * 32 : (a + 1) * 32]


def start_kernel(meta, grads, tokens, steps, gains, h1g, own, near, far, grad_out, weight, turned, sems):
    seqs, rows, width = tokens.shape
    hd = width // H
    put = Placer(sems, meta[0], meta[1])
    copies = put.lay(own, near, far, weight, 0, 3)
    for s in range(seqs):
        for h in range(H):
            for j in range(3):
                turned[s, j * width + h * hd : j * width + (h + 1) * hd, :] = grads[s, h, j * hd : (j + 1) * hd, :]
    wait(copies)
    for s in range(seqs):
        xhat, r = normalise(tokens[s].astype(F32) + steps[s : s + 1, :])
        grad = nt(flip(turned[s]), weight[...])
        grad_out[s] = h1g[s * rows : (s + 1) * rows, :] + norm_back(grad, gains[0:1, :], xhat, r)


PIECES = [(core, mask + far, far) for core in (0, 1) for mask in (0, 2, 4, 6) for far in (0, 1)]


def place_cross_kernel(meta, *refs):
    pieces, (out_out, query_out, cross_out, keyval_out) = refs[:-4], refs[-4:]
    c, me = meta[1], meta[2]
    for k, (core, mask, index) in enumerate(PIECES):
        block = pieces[k // 2][index].astype(F32)
        a = me ^ mask
        ca = c ^ core
        at = aligned(ca * 128 + a * 16, 16)
        out_out[at, :] = block[0:16]
        query_out[at, :] = block[16:32]
        cross_out[at, :] = block[32:48]
        keyval_out[aligned(a * 32, 32), aligned(ca * 512, 512)] = block[48:80]


def encoder_back_kernel(kv, got, weight, out):
    seqs, span, width = out.shape
    total = (kv[0].astype(F32) + got[0].astype(F32)).astype(BF)
    for s in range(seqs):
        first = s * 2 * span
        keys = nt(total[first : first + span], weight[:, 0:width])
        out[s] = keys + nt(total[first + span : first + 2 * span], weight[:, width:])


def merge_kernel(feed, feed_got, heads, heads_got, out):
    rows = feed.shape[1]
    for k in range(2):
        total = feed[k].astype(F32) + feed_got[1 - k].astype(F32)
        out[0, k * rows : (k + 1) * rows, :] = total.astype(BF)
    total = heads[0].astype(F32) + heads_got[0].astype(F32)
    count, half = total.shape
    split = out.shape[1] - 2 * rows
    out[0, 2 * rows :, 0:half] = total[0:split].astype(BF)
    rest = jnp.concatenate([total[split:], jnp.zeros((2 * split - count, half), F32)], axis=0)
    out[0, 2 * rows :, half:] = rest.astype(BF)


def place_kernel(meta, ids, *refs):
    pieces = refs[:8]
    feed_up, feed_down, grad_out, gain_out, shift_out, table_out, down_out, up_out, stacked = refs[8:]
    c, me, low = meta[1], meta[2], meta[6]
    for k, (core, mask, index) in enumerate(PIECES):
        block = pieces[k // 2][0, index * 128 : (index + 1) * 128, :].astype(F32)
        a = me ^ mask
        ca = c ^ core
        feed_down[aligned(ca * 512 + a * 64, 64), :] = block[0:64]
        feed_up[aligned((a % 4) * 64, 64), aligned(ca * 1024 + (a // 4) * 512, 512)] = block[64:128]
    hd = 64
    half = grad_out.shape[0]
    total = jnp.zeros((16, half), F32)
    for k, mask in enumerate((0, 4, 2, 6, 1, 5, 3, 7)):
        wide = pieces[k][0, 256:368, :].astype(F32)
        block = jnp.concatenate([wide[:, 0:half], wide[0:96, half:]], axis=0)
        head = low ^ mask
        for j in range(3):
            stacked[aligned(j * H * hd + head * hd, hd), :] = block[j * hd : (j + 1) * hd]
        total = total + block[3 * hd :]
    for b in range(3):
        grad_out[:, b * 512 : (b + 1) * 512] = flip(stacked[b * 512 : (b + 1) * 512, :])
    last = total.shape[0] - 10
    for row, (g, b) in enumerate(((0, 1), (last + 7, last + 8), (last + 5, last + 6))):
        gain_out[row : row + 1, :] = total[g : g + 1]
        shift_out[row : row + 1, :] = total[b : b + 1]
    down_out[...] = total[last : last + 1]
    up_out[...] = total[last + 1 : last + 5]
    step = lax.broadcasted_iota(jnp.int32, table_out.shape, 0).astype(F32)
    table = jnp.zeros(table_out.shape, F32)
    for k in range(4):
        lane = (k // 2) * half + k % 2
        table = table + jnp.where(step == ids[:, lane : lane + 1], total[2 + k : 3 + k], 0.0)
    table_out[...] = table


def sums(name, jobs, after=()):
    arrays, plan, outs = [], [], []
    for groups, split in jobs:
        steps, row = [], 0
        for group in groups:
            steps.append((row, range(len(arrays), len(arrays) + len(group))))
            row += group[0].shape[1]
            arrays += group
        blocks, width = groups[0][0].shape[0], groups[0][0].shape[2]
        plan.append((len(outs), blocks, split, steps))
        outs += [((blocks // 2, row, width), BF)] * 2 if split else [((blocks, row, width), BF)]
    count = len(arrays)

    def kernel(*refs):
        results = refs[count:]
        for first, blocks, split, steps in plan:
            for row, which in steps:
                total = refs[which[0]][...].astype(F32)
                for k in which[1:]:
                    total = total + refs[k][...].astype(F32)
                total = total.astype(BF)
                rows = pl.ds(row, total.shape[1])
                if split:
                    results[first][:, rows, :] = total[blocks // 2 :]
                    results[first + 1][:, rows, :] = total[: blocks // 2]
                else:
                    results[first][:, rows, :] = total

    return call(kernel, name, outs, [VM] * count, [], arrays, after=after)


def pair_kernel(mine, got, out):
    for k in range(2):
        out[k] = (mine[k].astype(F32) + got[1 - k].astype(F32)).astype(BF)


def tie(value, *others):
    return lax.optimization_barrier((value,) + others)[0]


def over_ctx(value, mask):
    return lax.ppermute(value, "ctx", [(i, i ^ mask) for i in range(16)])


def over_x(value):
    return lax.ppermute(value, "fsdp", [(0, 1), (1, 0)])


def spread(piece, first=()):
    pieces = [piece] + [over_ctx(piece, mask) for mask in (4, 2, 6)]
    pieces = [tie(p, *first) for p in pieces]
    return pieces + [over_ctx(p, 1) for p in pieces]


def shards(
    tokens, encoder, step_ids, out_grad, self_in, self_out, cross_query, cross_keyval, cross_out,
    ffn_up, up_bias, ffn_down, down_bias, norm_gain, norm_shift, step_table,
):
    nctx, nx = lax.axis_size("ctx"), lax.axis_size("fsdp")
    i, x = lax.axis_index("ctx"), lax.axis_index("fsdp")
    seqs, rows, width = tokens.shape
    hd = width // H
    units = seqs * H
    rep = nctx // units
    unit = i // rep
    s_mine, head = unit // H, unit % H
    n = rows * nctx
    ff = 2048
    fast = nctx == 16 and nx == 2
    steps_count = step_table.shape[0]
    slots = seqs * nx
    extra_rows = -(-(slots + 12) // 16) * 16
    zero = jnp.int32(0)

    xk, c, me = zero, zero, zero
    if fast:
        xk, c, me = x, i & 1, ((i >> 1) & 1) * 4 + ((i >> 2) & 1) * 2 + ((i >> 3) & 1)
    active = (i % rep == 0).astype(jnp.int32)
    meta = jnp.stack([xk, c, me, active, seqs * x + s_mine, seqs * x, i & 7, i, head, s_mine]).astype(jnp.int32)

    if fast:
        mine, others = call(
            split_kernel, "split", [((rows + seqs * encoder.shape[1], width), BF)] * 2, [SM, VM, VM], [], (meta, tokens, encoder),
        )
        got = over_ctx(others, 8)
        blocks = [mine] + [over_ctx(mine, mask) for mask in (4, 2, 6)]
        blocks += [got] + [over_ctx(got, mask) for mask in (4, 2, 6)]

        (small,) = call(
            prepare_kernel, "prepare", [((256, width // 2), BF)], [SM, SM] + [VM] * 6,
            [pltpu.VMEM((2 * hd, width // 2), BF), pltpu.VMEM((64, width // 2), F32)],
            (meta, step_ids, self_in, norm_gain, norm_shift, step_table, down_bias, up_bias),
            after=[mine],
        )
        own = dict(keyval=cross_keyval, out=self_out, query=cross_query, cross=cross_out, up=ffn_up, down=ffn_down, joined=self_in)

        weights = [own[name] for group in GROUPS for name in group]
        sizes = [sum(own[name].size for name in group) // 1024 for group in GROUPS]
        packed = call(
            functools.partial(pack_kernel, [len(group) for group in GROUPS]), "pack", [((size, 512), BF) for size in sizes],
            [SM] + [ANY] * len(weights), [pltpu.SemaphoreType.DMA((13,))], (meta, *weights), after=[small],
        )
        other_small = over_x(small)
        near2, near3 = (over_x(tie(p, other_small, *blocks[1:5])) for p in packed[:2])
        wh, gains, shifts, steps, step_mine, bias_u, bias_d, all_ids = call(
            unpack_kernel, "unpack",
            [((3 * hd, width), BF), ((3, width), F32), ((3, width), F32), ((seqs, width), F32), ((1, width), F32),
             ((1, ff), F32), ((1, width), F32), ((1, width), F32)],
            [SM, SM, VM, VM], [pltpu.VMEM((64, width), F32)], (meta, step_ids, small, other_small), after=[packed[0]],
        )
        blocks += [over_ctx(tie(block, wh), 1) for block in blocks]
    else:
        def gather(w, axis=0):
            return lax.all_gather(w, "fsdp", axis=axis, tiled=True)

        gains, shifts = gather(norm_gain, 1).astype(F32), gather(norm_shift, 1).astype(F32)
        table = gather(step_table, 1)
        bias_d, bias_u = gather(down_bias)[None, :].astype(F32), gather(up_bias)[None, :].astype(F32)
        all_ids = gather(step_ids.astype(BF)).astype(F32)
        full = dict(keyval=gather(cross_keyval), out=gather(self_out), query=gather(cross_query), cross=gather(cross_out),
                    up=gather(ffn_up), down=gather(ffn_down), joined=gather(self_in))
        half_of = {name: w.shape[0] // 2 for name, w in full.items()}
        own = {name: w[: half_of[name]] for name, w in full.items()}

        def group(names, which):
            parts = []
            for name in names:
                rest = full[name][half_of[name] :]
                quarter = half_of[name] // 2
                part = rest[which * quarter : (which + 1) * quarter]
                parts += [part[:, b : b + 512] for b in range(0, part.shape[1], 512)]
            return jnp.concatenate(parts, axis=0)

        (near2, far2), (near3, far3), (near4, far4) = ([group(names, w) for w in (0, 1)] for names in GROUPS)
        by_head = full["joined"].reshape(width, 3, H, hd)
        wh = lax.dynamic_index_in_dim(by_head, head, 2, False).reshape(width, 3 * hd).T
        onehot = (jnp.arange(steps_count, dtype=jnp.int32)[None, :] == step_ids[:, None]).astype(BF)
        steps = jnp.dot(onehot, table, preferred_element_type=F32)
        step_mine = lax.dynamic_index_in_dim(steps, s_mine, 0, True)
        every = lax.all_gather(tokens, "ctx", axis=0, tiled=False)
        chosen = lax.dynamic_index_in_dim(every, s_mine, 1, False)
        encs = lax.all_gather(encoder, "ctx", axis=0, tiled=False)
        blocks = [jnp.concatenate([chosen[j], encs[j].reshape(-1, width)], axis=0) for j in range(nctx)]
    xhat0, joined, heads, attended_full, stats = call(
        attend_kernel, "attend",
        [((n, width), BF), ((3 * hd, n), BF), ((nctx, hd, rows), BF), ((hd, n), F32), ((8, n), F32)],
        [SM] + [VM] * (4 + nctx),
        [pltpu.VMEM((n, width), BF), pltpu.VMEM((n, hd), BF)],
        (meta, step_mine, gains, shifts, wh, *blocks),
    )
    hold = []
    back = lax.all_to_all(heads, "ctx", 0, 0, tiled=True)
    if fast:
        far2 = over_ctx(tie(near2, heads), 1)
    att = back.reshape(units, rep, hd, rows)[:, 0].reshape(seqs, width, rows)

    enc_rows = nctx * encoder.shape[1]
    enc_all, kvt, w_keyval = call(
        encoder_kernel, "encoder_rows",
        [((seqs, enc_rows, width), BF), ((seqs, 2 * width, enc_rows), BF), ((width, 2 * width), BF)],
        [SM, ANY, ANY, ANY] + [VM] * nctx,
        [pltpu.SemaphoreType.DMA((5,))],
        (meta, own["keyval"], near2, far2, *blocks),
    )
    if fast:
        near4 = over_x(tie(packed[2], kvt))
        hold = [near4]

    tall = seqs * rows
    square = pltpu.VMEM((width, width), BF)
    hidden2, hidden1, q, crossed, shares = call(
        forward_kernel, "forward",
        [((tall, width), F32), ((tall, width), F32), ((tall, width), BF), ((seqs, width, rows), BF), ((units, rows, enc_rows), BF)],
        [SM] + [VM] * 6 + [ANY] * 5,
        [square] * 3 + [pltpu.SemaphoreType.DMA((9,))],
        (meta, tokens, steps, att, kvt, gains, shifts, own["out"], own["query"], own["cross"], near2, far2),
    )
    if fast:
        far3 = over_ctx(tie(near3, hidden2), 1)
    mixed, h2g, extra1, down_keep, down_send, up_keep, up_send = call(
        feed_kernel, "feed",
        [((seqs, rows, width), BF), ((tall, width), F32), ((extra_rows, width), F32)] + [((16, 64, width), BF)] * 4,
        [SM] + [VM] * 6 + [ANY] * 6,
        [pltpu.VMEM((width, ff), BF), pltpu.VMEM((ff, width), BF), pltpu.VMEM((ff, tall), BF),
         pltpu.VMEM((width, tall), BF), pltpu.VMEM((tall, ff), BF), pltpu.SemaphoreType.DMA((12,))],
        (meta, hidden2, gains, shifts, bias_u, bias_d, out_grad, own["up"], own["down"], near2, far2, near3, far3),
    )
    hold_far = []
    if fast:
        far4 = over_ctx(tie(near4, h2g), 1)
        hold_far = [far4]
        down_got, up_got = over_ctx(down_send, 1), over_ctx(up_send, 1)
    dq, part = call(
        cross_back_kernel, "cross_back",
        [((tall, width), BF), ((seqs, 2 * width, enc_rows), BF)],
        [SM] + [VM] * 4 + [ANY] * 3,
        [square, pltpu.VMEM((tall, width), BF), pltpu.SemaphoreType.DMA((3,))],
        (meta, h2g, q, shares, kvt, own["cross"], near2, far2),
    )
    hold = []
    if fast:
        down_x, down_kept, up_y, up_kept = sums(
            "reduce_1", [([[down_keep, down_got]], True), ([[up_keep, up_got]], True)], [dq])
        down_x1, up_y1 = over_x(down_x), over_ctx(up_y, 2)
        hold = [down_x]
    h1g, att_grad, extra2 = call(
        hidden_back_kernel, "hidden_back",
        [((tall, width), F32), ((seqs, width, rows), BF), ((extra_rows, width), F32)],
        [SM] + [VM] * 5 + [ANY] * 4,
        [square, square, pltpu.SemaphoreType.DMA((6,))],
        (meta, h2g, hidden1, dq, gains, extra1, own["out"], own["query"], near2, far2),
        after=hold,
    )
    by_unit = att_grad.reshape(units, 1, hd, rows)
    grads = lax.all_to_all(jnp.broadcast_to(by_unit, (units, rep, hd, rows)).reshape(nctx, hd, rows), "ctx", 0, 0, tiled=True)
    keep1, send1, keep0, send0, kv_keep, kv_send = call(
        weights_back_kernel, "weights_back",
        [((8, 80, width), BF)] * 4 + [((8, enc_rows // 4, width), BF)] * 2,
        [SM] + [VM] * 10,
        [pltpu.VMEM((width, tall), BF), pltpu.VMEM((seqs, width, enc_rows), BF), pltpu.VMEM((seqs, enc_rows, 2 * width), BF)],
        (meta, h2g, h1g, hidden1, crossed, att, dq, part, enc_all, gains, shifts), after=hold_far,
    )
    hold = []
    if fast:
        got1, got0, kv_0 = (over_ctx(tie(part, grads, down_x1, up_y1), 1) for part in (send1, send0, kv_send))

        down_y, down_kept, up_x, up_kept = sums(
            "reduce_2", [([[down_kept, down_x1]], True), ([[up_kept, up_y1]], True)], [grads, keep1],
        )
        down_y1, up_x1 = over_ctx(down_y, 2), over_x(up_x)
        hold = [down_y]

    head_scratch = [pltpu.VMEM((n // 2, hd), BF), pltpu.VMEM((n // 2, hd), BF), pltpu.VMEM((hd, n), BF)]
    query_acc, key_half = call(
        attend_back_first, "attend_back_1", [((hd, n), F32), ((2 * hd, n // 2), BF)], [VM] * 4, head_scratch,
        (joined, attended_full, stats, grads), after=hold,
    )
    hold = []
    if fast:
        feed_z, feed_kept, cross_x, cross_kept, kv_y, kv_kept = sums(
            "reduce_3",
            [([[down_kept, down_y1], [up_kept, up_x1]], True), ([[keep1, got1]], False), ([[keep0, got0]], False), ([[kv_keep, kv_0]], True)],
            [query_acc],
        )
        feed_z1, cross_x1, kv_1 = over_ctx(feed_z, 4), over_x(cross_x), over_ctx(kv_y, 2)
        hold = [feed_z]
    joined_grad, u_keep, u_send = call(
        attend_back_second, "attend_back_2",
        [((nctx, 3 * hd, rows), BF), ((3 * hd + extra_rows, width // 2), F32), ((3 * hd + extra_rows, width // 2), BF)],
        [SM] + [VM] * 11,
        head_scratch
        + [pltpu.VMEM((2 * hd, n // 2), BF), pltpu.VMEM((hd, n), F32), pltpu.VMEM((3 * hd + 16, n), BF),
           pltpu.VMEM((3 * hd + extra_rows, width), F32)],
        (meta, joined, attended_full, stats, grads, query_acc, key_half, xhat0, gains, shifts, wh, extra2),
        after=hold,
    )
    if fast:
        joined_grad, u_send = tie(joined_grad, feed_z1, kv_1), tie(u_send, feed_z1, kv_1)
        u_x1 = over_x(u_send)[None]
        feed_w, kv_z, kv_kept, cross_y, cross_kept = sums(
            "reduce_4", [([[feed_kept, feed_z1]], False), ([[kv_kept, kv_1]], True), ([[cross_kept, cross_x1]], True)], [u_send],
        )
        feed_w1, kv_2, cross_y1 = over_ctx(feed_w, 8), over_ctx(kv_z, 4), over_ctx(cross_y, 2)
        cross_z, cross_kept, u_sum = sums("reduce_5", [([[cross_kept, cross_y1]], True), ([[u_keep[None], u_x1]], False)])
        cross_z1, u_8 = over_ctx(cross_z, 4), over_ctx(u_sum, 8)
        (merged,) = call(
            merge_kernel, "reduce_6", [((1, 368, width), BF)], [VM] * 4, [], (feed_w, feed_w1, u_sum, u_8), after=[cross_z1, kv_2],
        )
        cross_w, kv_far, kv_near = sums("reduce_7", [([[cross_kept, cross_z1]], False), ([[kv_kept, kv_2]], True)], [merged])
        cross_w1, kv_got = over_ctx(cross_w, 8), over_ctx(kv_far, 8)
        merged = tie(merged, cross_w)
        spread_out = [over_ctx(merged, mask) for mask in (4, 2, 6)]
        hold = [cross_w]
    dj = lax.all_to_all(joined_grad, "ctx", 0, 0, tiled=True)
    dj = dj.reshape(units, rep, 3 * hd, rows)[:, 0].reshape(seqs, H, 3 * hd, rows)
    (tokens_grad,) = call(
        start_kernel, "start_grad",
        [((seqs, rows, width), F32)],
        [SM] + [VM] * 5 + [ANY] * 3,
        [pltpu.VMEM((width, 3 * width), BF), pltpu.VMEM((seqs, 3 * width, rows), BF), pltpu.SemaphoreType.DMA((7,))],
        (meta, dj, tokens, steps, gains, h1g, own["joined"], near4, far4),
        after=hold,
    )

    if fast:
        (cross_pair,) = call(
            pair_kernel, "reduce_8", [((2, 80, width), BF)], [VM] * 2, [], (cross_w, cross_w1), after=[kv_got, tokens_grad],
        )
        pieces = [tie(piece, cross_pair) for piece in [merged] + spread_out]
        pieces = pieces + [over_ctx(piece, 1) for piece in pieces]
        (enc_grad,) = call(
            encoder_back_kernel, "encoder_back", [(encoder.shape, F32)], [VM] * 3, [], (kv_near, kv_got, w_keyval), after=[cross_pair],
        )
        up_grad, down_grad, self_in_grad, gain_grad, shift_grad, table_grad, down_bias_grad, up_bias_grad = call(
            place_kernel, "place",
            [((width // 2, ff), F32), ((ff // 2, width), F32), ((width // 2, 3 * width), F32), ((3, width // 2), F32),
             ((3, width // 2), F32), ((steps_count, width // 2), F32), ((1, width // 2), F32), ((4, width // 2), F32)],
            [SM] + [VM] * 9, [pltpu.VMEM((3 * width, width // 2), F32)], (meta, all_ids, *pieces), after=[enc_grad],
        )
        down_bias_grad, up_bias_grad = down_bias_grad.reshape(-1), up_bias_grad.reshape(-1)
        cross_pieces = spread(cross_pair, [up_grad])
        out_g, query_g, cross_g, keyval_g = call(
            place_cross_kernel, "place_cross",
            [((width // 2, width), F32)] * 3 + [((width // 2, 2 * width), F32)],
            [SM] + [VM] * 8, [], (meta, *cross_pieces),
        )
    else:
        def scatter(g, axis=0):
            return lax.psum(lax.psum_scatter(g, "fsdp", scatter_dimension=axis, tiled=True), "ctx")

        down_all = jnp.stack([down_keep, down_send]).reshape(2, 2, 8, 64, width).transpose(1, 0, 2, 3, 4)
        up_all = jnp.stack([up_keep, up_send]).reshape(2, 2, 2, 4, 64, width).transpose(2, 3, 4, 0, 1, 5)
        down_grad, up_grad = scatter(down_all.reshape(ff, width).astype(F32)), scatter(up_all.reshape(width, ff).astype(F32))
        c_all = jnp.stack([jnp.stack([keep0, send0]), jnp.stack([keep1, send1])])
        out_g, query_g, cross_g = (scatter(c_all[:, :, :, k : k + 16].reshape(width, width).astype(F32)) for k in (0, 16, 32))
        keyval_g = scatter(c_all[:, :, :, 48:80].transpose(0, 2, 3, 1, 4).reshape(width, 2 * width).astype(F32))
        kv = jnp.stack([kv_keep, kv_send]).reshape(2, 2, 2, 2, seqs, 2, enc_rows // 16, width).transpose(4, 3, 2, 1, 0, 6, 5, 7)
        kv = lax.psum_scatter(kv.reshape(seqs, enc_rows, 2 * width), "ctx", scatter_dimension=1, tiled=True)
        enc_grad = jnp.einsum("sre,de->srd", kv, w_keyval, preferred_element_type=F32)
        u = jnp.concatenate([u_keep, u_send.astype(F32)], axis=1)
        every_u = lax.all_gather(lax.psum(u[: 3 * hd], "fsdp"), "ctx", axis=0, tiled=False)
        by_head = every_u.reshape(seqs, H, rep, 3, hd, width).sum(axis=(0, 2))
        joined_g = by_head.transpose(3, 1, 0, 2).reshape(width, 3 * width)
        self_in_grad = lax.dynamic_slice_in_dim(joined_g, x * self_in.shape[0], self_in.shape[0], 0)
        total = lax.psum(u[3 * hd :], ("ctx", "fsdp"))
        wide = norm_gain.shape[1]
        extra = lax.dynamic_slice_in_dim(total, x * wide, wide, 1)
        last = extra_rows - 10
        down_bias_grad = extra[last]
        up_bias_all = total[last + 1 : last + 5].reshape(4, 2, width // 2).transpose(1, 0, 2).reshape(-1)
        up_bias_grad = lax.dynamic_slice_in_dim(up_bias_all, x * up_bias.shape[0], up_bias.shape[0], 0)
        gain_grad = jnp.stack([extra[0], extra[last + 7], extra[last + 5]])
        shift_grad = jnp.stack([extra[1], extra[last + 8], extra[last + 6]])
        hot = (jnp.arange(steps_count, dtype=jnp.int32).astype(F32)[:, None, None] == all_ids[None, :, None]).astype(F32)
        table_grad = jnp.sum(hot * extra[None, 2 : 2 + slots, :], axis=1)

    return (
        mixed, tokens_grad, enc_grad, self_in_grad, out_g, query_g, keyval_g, cross_g, up_grad, up_bias_grad,
        down_grad, down_bias_grad, gain_grad, shift_grad, table_grad,
    )


def solution(mesh):
    tok = P("fsdp", "ctx", None)
    row, vec, col = P("fsdp", None), P("fsdp"), P(None, "fsdp")
    in_specs = (tok, tok, vec, tok, row, row, row, row, row, row, vec, row, vec, col, col, col)
    out_specs = (tok, tok, tok, row, row, row, row, row, row, vec, row, vec, col, col, col)
    return jax.shard_map(shards, mesh=mesh, in_specs=in_specs, out_specs=out_specs, check_vma=False)
```

```python
import functools
import math

import jax
import jax.numpy as jnp
from jax import lax
from jax.experimental import pallas as pl
from jax.experimental.pallas import tpu as pltpu
from jax.sharding import PartitionSpec as P

H = 8
EPS = 1e-05
F32 = jnp.float32
BF = jnp.bfloat16
LOG2E = 1.4426950408889634
LARGE, SMALL = 62, 32
ROOMY = ("split", "prepare", "pack", "unpack", "attend", "encoder_rows", "weights_back")


def limit_of(name):
    return (LARGE if name in ROOMY else SMALL) * 1024 * 1024


def nn(a, b):
    return lax.dot_general(a, b, (((1,), (0,)), ((), ())), preferred_element_type=F32)


def nt(a, b):
    return lax.dot_general(a, b, (((1,), (1,)), ((), ())), preferred_element_type=F32)


def flip(v):
    return jnp.transpose(v)


def normalise(v):
    centred = v - jnp.mean(v, axis=-1, keepdims=True)
    r = lax.rsqrt(jnp.mean(centred * centred, axis=-1, keepdims=True) + EPS)
    return centred * r, r


def norm_back(grad, gain, xhat, r):
    u = grad * gain
    return r * (u - jnp.mean(u, axis=-1, keepdims=True) - xhat * jnp.mean(u * xhat, axis=-1, keepdims=True))


def aligned(index, size):
    return pl.ds(pl.multiple_of(index, size), size)


VM = pl.BlockSpec(memory_space=pltpu.VMEM)
SM = pl.BlockSpec(memory_space=pltpu.SMEM)
ANY = pl.BlockSpec(memory_space=pl.ANY)


def call(kernel, name, outs, in_specs, scratch, args, out_specs=None, after=()):
    args = list(args)
    if after:
        args[0] = tie(args[0], *after)
    return pl.pallas_call(
        kernel,
        name=name,
        out_shape=[jax.ShapeDtypeStruct(s, d) for s, d in outs],
        in_specs=in_specs,
        out_specs=out_specs or [VM] * len(outs),
        scratch_shapes=scratch,
        compiler_params=pltpu.CompilerParams(vmem_limit_bytes=limit_of(name)),
        cost_estimate=pl.CostEstimate(flops=1000, bytes_accessed=1000, transcendentals=0),
    )(*args)


class Placer:
    def __init__(self, sems, x, c):
        self.sems, self.x, self.c, self.used = sems, x, c, 0

    def copy(self, src, dst):
        copy = pltpu.make_async_copy(src, dst, self.sems.at[self.used])
        self.used += 1
        copy.start()
        return copy

    def lay(self, own, near, far, dst, row0, blocks):
        rows = own.shape[0]
        half = rows // 2
        base = (1 - self.x) * rows
        copies = [self.copy(own, dst.at[aligned(self.x * rows, rows)])]
        for b in range(blocks):
            cols = pl.ds(b * 512, 512)
            part = pl.ds(row0 + b * half, half)
            copies.append(self.copy(near.at[part], dst.at[aligned(base + self.c * half, half), cols]))
            copies.append(self.copy(far.at[part], dst.at[aligned(base + (1 - self.c) * half, half), cols]))
        return copies


def wait(copies):
    for copy in copies:
        copy.wait()


def split_kernel(meta, tokens, encoder, mine, others):
    rows, span = tokens.shape[1], encoder.shape[1]
    for out, s in ((others, 1 - meta[9]), (mine, meta[9])):
        out[0:rows, :] = tokens[s]
        for k in range(encoder.shape[0]):
            out[rows + k * span : rows + (k + 1) * span, :] = encoder[k]


ORDER = (0, 4, 2, 6, 8, 12, 10, 14, 1, 5, 3, 7, 9, 13, 11, 15)


def attend_kernel(meta, step, gains, shifts, wh, *refs):
    blocks, (xhat_out, joined_out, heads_out, full_out, stats_out, normed, keys) = refs[:-7], refs[-7:]
    n, width = xhat_out.shape
    hd = joined_out.shape[0] // 3
    rows = heads_out.shape[2]
    stats_out[...] = jnp.zeros_like(stats_out)
    for k, block in enumerate(blocks):
        xhat, r = normalise(block[0:rows, :].astype(F32) + step[...])
        at = aligned((meta[7] ^ ORDER[k] if len(blocks) == 16 else k) * rows, rows)
        xhat_out[at, :] = xhat.astype(BF)
        normed[at, :] = (xhat * gains[0:1, :] + shifts[0:1, :]).astype(BF)
        stats_out[1:2, at] = flip(jnp.broadcast_to(r, (rows, 128)))[0:1, :]
    for b in range(n // 512):
        cols = pl.ds(b * 512, 512)
        joined_out[:, cols] = nt(wh[...], normed[cols, :]).astype(BF)
    keys[...] = flip(joined_out[hd : 2 * hd, :].astype(F32)).astype(BF)
    factor = LOG2E / math.sqrt(hd)
    wide = 1024

    def query_block(b, carry):
        cols = aligned(b * wide, wide)
        scores = nn(keys[...], joined_out[0:hd, cols]) * factor
        peak = jnp.max(scores, axis=0, keepdims=True)
        shares = jnp.exp2(scores - peak)
        total = jnp.sum(shares, axis=0, keepdims=True)
        out = nn(joined_out[2 * hd : 3 * hd, :], shares.astype(BF)) * (1.0 / total)
        full_out[:, cols] = out
        stats_out[0:1, cols] = peak + jnp.log2(total)
        for part in range(wide // rows):
            heads_out[b * (wide // rows) + part] = out[:, part * rows : (part + 1) * rows].astype(BF)
        return carry

    lax.fori_loop(0, n // wide, query_block, 0)


def key_blocks(first, joined, full, stats, grads, keys, values, gout, key_grads, query_acc):
    n = full.shape[1]
    hd = joined.shape[0] // 3
    rows = grads.shape[2]
    span = keys.shape[0]
    scale = 1.0 / math.sqrt(hd)
    factor = LOG2E * scale
    for j in range(grads.shape[0]):
        gout[:, j * rows : (j + 1) * rows] = grads[j]
    mine = pl.ds(first, span)
    keys[...] = flip(joined[hd : 2 * hd, mine].astype(F32)).astype(BF)
    values[...] = flip(joined[2 * hd : 3 * hd, mine].astype(F32)).astype(BF)
    delta = jnp.sum(gout[...].astype(F32) * full[...], axis=0, keepdims=True)
    lse = stats[0:1, :]
    wide = 256

    def key_block(b, carry):
        at = aligned(b * wide, wide)
        queries = joined[0:hd, :]
        shares = jnp.exp2(nn(keys[at, :], queries) * factor - lse)
        share_grad = nn(values[at, :], gout[...])
        score_grad = (shares * (share_grad - delta)).astype(BF)
        key_grads[0:hd, at] = (nt(queries, score_grad) * scale).astype(BF)
        key_grads[hd : 2 * hd, at] = nt(gout[...], shares.astype(BF)).astype(BF)
        query_acc[...] += nn(joined[hd : 2 * hd, aligned(first + b * wide, wide)], score_grad)
        return carry

    lax.fori_loop(0, span // wide, key_block, 0)


def attend_back_first(joined, full, stats, grads, query_out, key_out, keys, values, gout):
    query_out[...] = jnp.zeros_like(query_out)
    key_blocks(0, joined, full, stats, grads, keys, values, gout, key_out, query_out)


def attend_back_second(
    meta, joined, full, stats, grads, query_in, key_in, xhat, gains, shifts, wh, extra, joined_grad_out, keep_out, send_out,
    keys, values, gout, key_grads, query_acc, lhs, whole,
):
    x, active, slot = meta[0], meta[3], meta[4]
    n, width = xhat.shape
    hd = joined.shape[0] // 3
    half = width // 2
    rows = grads.shape[2]
    scale = 1.0 / math.sqrt(hd)
    query_acc[...] = query_in[...]
    key_blocks(n // 2, joined, full, stats, grads, keys, values, gout, key_grads, query_acc)
    lhs[0:hd, :] = (query_acc[...] * scale).astype(BF)
    lhs[hd : 3 * hd, 0 : n // 2] = key_in[...]
    lhs[hd : 3 * hd, n // 2 :] = key_grads[...]
    for j in range(joined_grad_out.shape[0]):
        joined_grad_out[j] = lhs[0 : 3 * hd, j * rows : (j + 1) * rows]

    gain, shift = gains[0:1, :], shifts[0:1, :]
    grad = lhs[0 : 3 * hd, :].astype(F32)
    r = stats[1:2, :]
    weight = wh[...].astype(F32)
    bias = jnp.sum(weight * shift, axis=1, keepdims=True)
    mixed_mean = jnp.sum(grad * (joined[...].astype(F32) - bias), axis=0, keepdims=True) * (1.0 / width)
    tail = lhs.shape[0] - 3 * hd
    first = lax.broadcasted_iota(jnp.int32, (tail, n), 0) == 0
    lhs[3 * hd :, :] = jnp.where(first, mixed_mean * r, 0.0).astype(BF)
    product = nn(lhs[...], xhat[...])
    m = product[0 : 3 * hd]
    sums = jnp.sum(grad, axis=1, keepdims=True)
    scaled_sums = jnp.sum(grad * r, axis=1, keepdims=True)
    lead = gain * jnp.sum(weight * scaled_sums, axis=0, keepdims=True)
    start_sum = lead - jnp.mean(lead, axis=1, keepdims=True) - product[3 * hd : 3 * hd + 1]
    on = active.astype(F32)
    whole[0 : 3 * hd, :] = (m * gain + sums * shift) * on
    gain_grad = jnp.sum(weight * m, axis=0, keepdims=True) * on
    shift_grad = jnp.sum(weight * sums, axis=0, keepdims=True) * on
    row = lax.broadcasted_iota(jnp.int32, extra.shape, 0)
    more = jnp.where(row == 0, gain_grad, 0.0) + jnp.where(row == 1, shift_grad, 0.0)
    more = more + jnp.where(row == 2 + slot, start_sum * on, 0.0)
    whole[3 * hd :, :] = extra[...] + more
    keep_out[...] = whole[:, aligned(x * half, half)]
    send_out[...] = whole[:, aligned((1 - x) * half, half)].astype(BF)


def prepare_kernel(meta, ids, weight, gain, shift, table, down_bias, up_bias, out, turned, small):
    width = weight.shape[1] // 3
    hd = width // H
    pair, odd = meta[8] // 2, meta[8] % 2
    for j in range(3):
        turned[...] = flip(weight[:, aligned(j * width + pair * 2 * hd, 2 * hd)])
        out[j * hd : (j + 1) * hd, :] = turned[aligned(odd * hd, hd), :]
    small[...] = jnp.zeros_like(small)
    at = 0
    for part in (gain, shift, table):
        small[at : at + part.shape[0], :] = part[...].astype(F32)
        at += part.shape[0]
    half = small.shape[1]
    for part in (down_bias, up_bias):
        for q in range(part.shape[0] // half):
            small[at : at + 1, :] = part[q * half : (q + 1) * half].astype(F32).reshape(1, half)
            at += 1
    lane = lax.broadcasted_iota(jnp.int32, (1, small.shape[1]), 1)
    line = jnp.zeros((1, small.shape[1]), F32)
    for s in range(2):
        line = line + jnp.where(lane == s, ids[s].astype(F32), 0.0)
    small[at : at + 1, :] = line
    out[3 * hd :, :] = small[...].astype(BF)


def unpack_kernel(
    meta, ids, mine, other, wh_out, gains_out, shifts_out, steps_out, step_out, up_out, down_out, ids_out, both,
):
    x = meta[0]
    rows, half = mine.shape
    head_rows = wh_out.shape[0]
    count = rows - head_rows
    for part, at in ((mine, x), (other, 1 - x)):
        lanes = aligned(at * half, half)
        wh_out[:, lanes] = part[0:head_rows, :]
        both[:, lanes] = part[head_rows:, :].astype(F32)
    gains_out[...] = both[0:3, :]
    shifts_out[...] = both[3:6, :]
    for s in range(2):
        steps_out[s : s + 1, :] = both[pl.ds(6 + ids[s], 1), :]
    step_out[...] = both[pl.ds(6 + ids[meta[9]], 1), :]
    last = count - 8
    down_out[...] = both[last : last + 1, :]
    for q in range(4):
        line = both[last + 1 + q : last + 2 + q, :]
        up_out[:, q * half : (q + 1) * half] = line[:, 0:half]
        up_out[:, (4 + q) * half : (5 + q) * half] = line[:, half:]
    ids_out[...] = both[last + 5 : last + 6, :]


def encoder_kernel(meta, own, near, far, *refs):
    blocks, (enc_out, kvt_out, weight_out, sems) = refs[:-4], refs[-4:]
    put = Placer(sems, meta[0], meta[1])
    copies = put.lay(own, near, far, weight_out, 0, 2)
    rows = enc_out.shape[1] // len(blocks)
    first = blocks[0].shape[0] - enc_out.shape[0] * rows
    for k, block in enumerate(blocks):
        at = aligned((meta[7] ^ ORDER[k] if len(blocks) == 16 else k) * rows, rows)
        for s in range(enc_out.shape[0]):
            enc_out[s, at, :] = block[first + s * rows : first + (s + 1) * rows, :]
    wait(copies)
    for s in range(enc_out.shape[0]):
        for b in range(2):
            kv = nn(enc_out[s], weight_out[:, b * 512 : (b + 1) * 512])
            kvt_out[s, b * 512 : (b + 1) * 512, :] = flip(kv).astype(BF)


def pack_kernel(counts, meta, *refs):
    total = sum(counts)
    weights, outs, sems = refs[:total], refs[total:-1], refs[-1]
    copies = []
    index = 0
    for out, count in zip(outs, counts):
        at = 0
        for weight in weights[index : index + count]:
            half = weight.shape[0] // 2
            for b in range(weight.shape[1] // 512):
                src = weight.at[aligned(meta[1] * half, half), pl.ds(b * 512, 512)]
                copies.append(pltpu.make_async_copy(src, out.at[pl.ds(at, half)], sems.at[len(copies)]))
                copies[-1].start()
                at += half
        index += count
    wait(copies)


GROUPS = (("keyval", "out", "query", "cross", "up"), ("down",), ("joined",))


def chunk_at(meta, k, xr):
    x, c = meta[0], meta[1]
    return x ^ xr, c ^ k


def forward_kernel(
    meta, tokens, steps, att, kvt, gains, shifts, own_out, own_query, own_cross, near2, far2,
    h2_out, h1_out, q_out, crossed_out, shares_out, w_out, w_query, w_cross, sems,
):
    seqs, rows, width = tokens.shape
    hd = width // H
    put = Placer(sems, meta[0], meta[1])
    half = own_out.shape[0] // 2
    c_out = put.lay(own_out, near2, far2, w_out, 2 * half, 1)
    c_query = put.lay(own_query, near2, far2, w_query, 3 * half, 1)
    c_cross = put.lay(own_cross, near2, far2, w_cross, 4 * half, 1)
    factor = LOG2E / math.sqrt(hd)

    wait(c_out)
    for s in range(seqs):
        at = pl.ds(s * rows, rows)
        start = tokens[s].astype(F32) + steps[s : s + 1, :]
        h1_out[at, :] = start + nn(flip(att[s]), w_out[...])
    hidden1 = h1_out[...]
    xhat1, unused = normalise(hidden1)
    wait(c_query)
    q_out[...] = nn((xhat1 * gains[1:2, :] + shifts[1:2, :]).astype(BF), w_query[...]).astype(BF)
    for s in range(seqs):
        for first in range(0, H, TOGETHER):
            heads = range(first, first + TOGETHER)
            scores = [
                nn(q_out[s * rows : (s + 1) * rows, h * hd : (h + 1) * hd], kvt[s, h * hd : (h + 1) * hd, :]) * factor for h in heads
            ]
            peaks = [jnp.max(score, axis=1, keepdims=True) for score in scores]
            shares = [jnp.exp2(score - peak) for score, peak in zip(scores, peaks)]
            totals = [jnp.sum(share, axis=1, keepdims=True) for share in shares]
            lows = [(share * (1.0 / total)).astype(BF) for share, total in zip(shares, totals)]
            got = [nt(kvt[s, width + h * hd : width + (h + 1) * hd, :], low) for h, low in zip(heads, lows)]
            for k, h in enumerate(heads):
                shares_out[s * H + h] = lows[k]
                crossed_out[s, h * hd : (h + 1) * hd, :] = got[k].astype(BF)
    wait(c_cross)
    for s in range(seqs):
        at = pl.ds(s * rows, rows)
        h2_out[at, :] = h1_out[at, :] + nn(flip(crossed_out[s]), w_cross[...])


TOGETHER = 8


def feed_kernel(
    meta, hidden2_in, gains, shifts, up_bias, down_bias, out_grad, own_up, own_down, near2, far2, near3, far3,
    mixed_out, h2g_out, extra_out, down_keep, down_send, up_keep, up_send, w_up, w_down, act_t, n2_t, pre_low, sems,
):
    seqs, rows, width = out_grad.shape
    ff = w_down.shape[0]
    slots = extra_out.shape[0]
    put = Placer(sems, meta[0], meta[1])
    c_up = put.lay(own_up, near2, far2, w_up, 5 * (own_up.shape[0] // 2), 4)
    c_down = put.lay(own_down, near3, far3, w_down, 0, 1)
    hidden2 = hidden2_in[...]
    xhat2, r2 = normalise(hidden2)
    n2 = (xhat2 * gains[2:3, :] + shifts[2:3, :]).astype(BF)
    n2_t[...] = flip(n2)
    grad = jnp.concatenate([out_grad[s] for s in range(seqs)], axis=0)
    top = grad.astype(F32)
    wait(c_up)
    wait(c_down)
    mixed = hidden2 + down_bias[...]
    n2_grad = jnp.zeros_like(hidden2)
    extra_out[...] = jnp.zeros_like(extra_out)
    root = math.sqrt(2.0 / math.pi)
    bias_row = slots - 10
    for b in range(ff // 512):
        cols = pl.ds(b * 512, 512)
        pre = nn(n2, w_up[:, cols]) + up_bias[:, cols]
        square = pre * pre
        bent = jnp.tanh(root * pre * (1.0 + 0.044715 * square))
        act = (0.5 * pre * (1.0 + bent)).astype(BF)
        slope = 0.5 * (1.0 + bent) + 0.5 * root * pre * (1.0 - bent * bent) * (1.0 + 3.0 * 0.044715 * square)
        mixed = mixed + nn(act, w_down[cols, :])
        act_t[cols, :] = flip(act)
        low = (nt(grad, w_down[cols, :]) * slope).astype(BF)
        pre_low[:, cols] = low
        n2_grad = n2_grad + nt(low, w_up[:, cols])
        sums = jnp.sum(low.astype(F32), axis=0, keepdims=True)
        per_half = ff // 512 // 2
        lanes = pl.ds((b // per_half) * 256, 256)
        for piece in range(2):
            row = bias_row + 1 + (b % per_half) * 2 + piece
            extra_out[row : row + 1, lanes] = sums[:, piece * 256 : (piece + 1) * 256]
    for s in range(seqs):
        mixed_out[s] = mixed[s * rows : (s + 1) * rows].astype(BF)
    h2g_out[...] = top + norm_back(n2_grad, gains[2:3, :], xhat2, r2)
    extra_out[bias_row : bias_row + 1, :] = jnp.sum(top, axis=0, keepdims=True)
    extra_out[bias_row + 5 : bias_row + 6, :] = jnp.sum(n2_grad * xhat2, axis=0, keepdims=True)
    extra_out[bias_row + 6 : bias_row + 7, :] = jnp.sum(n2_grad, axis=0, keepdims=True)

    me = meta[2]
    for k in (1, 0):
        down_out, up_out = (down_send, up_send) if k else (down_keep, up_keep)
        for xr in (1, 0):
            xa, ca = chunk_at(meta, k, xr)
            down = nn(act_t[aligned(xa * (ff // 2) + ca * (ff // 4), ff // 4), :], grad).astype(BF)
            up = nn(n2_t[aligned(xa * (width // 2), width // 2), :], pre_low[:, aligned(ca * (ff // 2), ff // 2)])
            up = up.astype(BF)
            for a in range(8):
                at = a ^ me
                down_out[xr * 8 + at] = down[a * 64 : (a + 1) * 64]
                up_out[(at // 4) * 8 + xr * 4 + at % 4] = up[(a % 4) * 64 : (a % 4 + 1) * 64, (a // 4) * 512 : (a // 4 + 1) * 512]


def cross_back_kernel(meta, h2g, q, shares, kvt, own_cross, near2, far2, dq_out, part_out, w_cross, dc, sems):
    width = h2g.shape[1]
    seqs, unused, enc_rows = kvt.shape
    rows = h2g.shape[0] // seqs
    hd = width // H
    scale = 1.0 / math.sqrt(hd)
    put = Placer(sems, meta[0], meta[1])
    half = own_cross.shape[0] // 2
    wait(put.lay(own_cross, near2, far2, w_cross, 4 * half, 1))
    dc[...] = nt(h2g[...].astype(BF), w_cross[...]).astype(BF)
    for s in range(seqs):
        at = slice(s * rows, (s + 1) * rows)
        q_t = flip(q[at, :])
        dc_t = flip(dc[at, :])
        for first in range(0, H, TOGETHER):
            heads = range(first, first + TOGETHER)
            lows = [shares[s * H + h] for h in heads]
            wides = [low.astype(F32) for low in lows]
            share_grads = [nn(dc[at, h * hd : (h + 1) * hd], kvt[s, width + h * hd : width + (h + 1) * hd, :]) for h in heads]
            means = [jnp.sum(wide * grad, axis=1, keepdims=True) for wide, grad in zip(wides, share_grads)]
            score_grads = [(wide * (grad - mean)).astype(BF) for wide, grad, mean in zip(wides, share_grads, means)]
            q_grads = [nt(grad, kvt[s, h * hd : (h + 1) * hd, :]) for h, grad in zip(heads, score_grads)]
            k_grads = [nn(q_t[h * hd : (h + 1) * hd], grad) for h, grad in zip(heads, score_grads)]
            v_grads = [nn(dc_t[h * hd : (h + 1) * hd], low) for h, low in zip(heads, lows)]
            for k, h in enumerate(heads):
                head = slice(h * hd, (h + 1) * hd)
                dq_out[at, head] = (q_grads[k] * scale).astype(BF)
                part_out[s, head, :] = (k_grads[k] * scale).astype(BF)
                part_out[s, width + h * hd : width + (h + 1) * hd, :] = v_grads[k].astype(BF)


def hidden_back_kernel(
    meta, h2g, hidden1, dq, gains, extra_in, own_out, own_query, near2, far2, h1g_out, att_grad_out, extra_out,
    w_out, w_query, sems,
):
    width = h2g.shape[1]
    seqs, unused, rows = att_grad_out.shape
    put = Placer(sems, meta[0], meta[1])
    half = own_out.shape[0] // 2
    c_query = put.lay(own_query, near2, far2, w_query, 3 * half, 1)
    c_out = put.lay(own_out, near2, far2, w_out, 2 * half, 1)
    xhat1, r1 = normalise(hidden1[...])
    wait(c_query)
    n1_grad = nt(dq[...], w_query[...])
    grad1 = h2g[...] + norm_back(n1_grad, gains[1:2, :], xhat1, r1)
    h1g_out[...] = grad1
    low1 = grad1.astype(BF)
    wait(c_out)
    for s in range(seqs):
        att_grad_out[s] = nt(w_out[...], low1[s * rows : (s + 1) * rows]).astype(BF)
    last = extra_out.shape[0] - 10
    row = lax.broadcasted_iota(jnp.int32, extra_out.shape, 0)
    more = jnp.where(row == last + 7, jnp.sum(n1_grad * xhat1, axis=0, keepdims=True), 0.0)
    more = more + jnp.where(row == last + 8, jnp.sum(n1_grad, axis=0, keepdims=True), 0.0)
    for s in range(seqs):
        token_sum = jnp.sum(grad1[s * rows : (s + 1) * rows], axis=0, keepdims=True)
        more = more + jnp.where(row == 2 + meta[5] + s, token_sum, 0.0)
    extra_out[...] = extra_in[...] + more


def weights_back_kernel(
    meta, h2g, h1g, hidden1, crossed, att, dq, part, enc, gains, shifts, keep1, send1, keep0, send0, kv_keep, kv_send,
    n1_t, enc_t, part_t,
):
    width = h2g.shape[1]
    seqs, unused, rows = att.shape
    xhat1, unused = normalise(hidden1[...])
    n1_t[...] = flip((xhat1 * gains[1:2, :] + shifts[1:2, :]).astype(BF))
    low2, low1 = h2g[...].astype(BF), h1g[...].astype(BF)
    enc_rows = enc.shape[1]
    span = enc_rows // 16
    for s in range(seqs):
        enc_t[s] = flip(enc[s])
        part_t[s] = flip(part[s])
    for k in (1, 0):
        out = kv_send if k else kv_keep
        for at in range(8):
            a = at ^ meta[2]
            first = aligned(((a & 1) * 8 + (a & 2) * 2 + (a & 4) // 2 + (meta[1] ^ k)) * span, span)
            for s in range(seqs):
                for j in range(2):
                    row = (s * 2 + j) * span
                    out[at, row : row + span, :] = part_t[s, first, j * width : (j + 1) * width]
    me = meta[2]
    for k in (1, 0):
        for xr in (1, 0):
            out = ((keep0, keep1), (send0, send1))[k][xr]
            xa, ca = chunk_at(meta, k, xr)
            at = aligned(xa * (width // 2) + ca * (width // 4), width // 4)
            outer = jnp.zeros((width // 4, width), F32)
            cross = jnp.zeros((width // 4, width), F32)
            keyval = jnp.zeros((width // 2, width), F32)
            for s in range(seqs):
                mine = slice(s * rows, (s + 1) * rows)
                outer = outer + nn(att[s, at, :], low1[mine])
                cross = cross + nn(crossed[s, at, :], low2[mine])
                keyval = keyval + nt(enc_t[s, aligned(xa * (width // 2), width // 2), :], part[s, aligned(ca * width, width), :])
            query = nn(n1_t[at, :], dq[...]).astype(BF)
            outer, cross, keyval = outer.astype(BF), cross.astype(BF), keyval.astype(BF)
            for a in range(8):
                out[a ^ me, 0:16, :] = outer[a * 16 : (a + 1) * 16]
                out[a ^ me, 16:32, :] = query[a * 16 : (a + 1) * 16]
                out[a ^ me, 32:48, :] = cross[a * 16 : (a + 1) * 16]
                out[a ^ me, 48:80, :] = keyval[a * 32 : (a + 1) * 32]


def start_kernel(meta, grads, tokens, steps, gains, h1g, own, near, far, grad_out, weight, turned, sems):
    seqs, rows, width = tokens.shape
    hd = width // H
    put = Placer(sems, meta[0], meta[1])
    copies = put.lay(own, near, far, weight, 0, 3)
    for s in range(seqs):
        for h in range(H):
            for j in range(3):
                turned[s, j * width + h * hd : j * width + (h + 1) * hd, :] = grads[s, h, j * hd : (j + 1) * hd, :]
    wait(copies)
    for s in range(seqs):
        xhat, r = normalise(tokens[s].astype(F32) + steps[s : s + 1, :])
        grad = nt(flip(turned[s]), weight[...])
        grad_out[s] = h1g[s * rows : (s + 1) * rows, :] + norm_back(grad, gains[0:1, :], xhat, r)


PIECES = [(core, mask + far, far) for core in (0, 1) for mask in (0, 2, 4, 6) for far in (0, 1)]


def place_cross_kernel(meta, *refs):
    pieces, (out_out, query_out, cross_out, keyval_out) = refs[:-4], refs[-4:]
    c, me = meta[1], meta[2]
    for k, (core, mask, index) in enumerate(PIECES):
        block = pieces[k // 2][index].astype(F32)
        a = me ^ mask
        ca = c ^ core
        at = aligned(ca * 128 + a * 16, 16)
        out_out[at, :] = block[0:16]
        query_out[at, :] = block[16:32]
        cross_out[at, :] = block[32:48]
        keyval_out[aligned(a * 32, 32), aligned(ca * 512, 512)] = block[48:80]


def encoder_back_kernel(kv, got, weight, out):
    seqs, span, width = out.shape
    total = (kv[0].astype(F32) + got[0].astype(F32)).astype(BF)
    for s in range(seqs):
        first = s * 2 * span
        keys = nt(total[first : first + span], weight[:, 0:width])
        out[s] = keys + nt(total[first + span : first + 2 * span], weight[:, width:])


def merge_kernel(feed, feed_got, heads, heads_got, out):
    rows = feed.shape[1]
    for k in range(2):
        total = feed[k].astype(F32) + feed_got[1 - k].astype(F32)
        out[0, k * rows : (k + 1) * rows, :] = total.astype(BF)
    total = heads[0].astype(F32) + heads_got[0].astype(F32)
    count, half = total.shape
    split = out.shape[1] - 2 * rows
    out[0, 2 * rows :, 0:half] = total[0:split].astype(BF)
    rest = jnp.concatenate([total[split:], jnp.zeros((2 * split - count, half), F32)], axis=0)
    out[0, 2 * rows :, half:] = rest.astype(BF)


def place_kernel(meta, ids, *refs):
    pieces = refs[:8]
    feed_up, feed_down, grad_out, gain_out, shift_out, table_out, down_out, up_out, stacked = refs[8:]
    c, me, low = meta[1], meta[2], meta[6]
    for k, (core, mask, index) in enumerate(PIECES):
        block = pieces[k // 2][0, index * 128 : (index + 1) * 128, :].astype(F32)
        a = me ^ mask
        ca = c ^ core
        feed_down[aligned(ca * 512 + a * 64, 64), :] = block[0:64]
        feed_up[aligned((a % 4) * 64, 64), aligned(ca * 1024 + (a // 4) * 512, 512)] = block[64:128]
    hd = 64
    half = grad_out.shape[0]
    total = jnp.zeros((16, half), F32)
    for k, mask in enumerate((0, 4, 2, 6, 1, 5, 3, 7)):
        wide = pieces[k][0, 256:368, :].astype(F32)
        block = jnp.concatenate([wide[:, 0:half], wide[0:96, half:]], axis=0)
        head = low ^ mask
        for j in range(3):
            stacked[aligned(j * H * hd + head * hd, hd), :] = block[j * hd : (j + 1) * hd]
        total = total + block[3 * hd :]
    for b in range(3):
        grad_out[:, b * 512 : (b + 1) * 512] = flip(stacked[b * 512 : (b + 1) * 512, :])
    last = total.shape[0] - 10
    for row, (g, b) in enumerate(((0, 1), (last + 7, last + 8), (last + 5, last + 6))):
        gain_out[row : row + 1, :] = total[g : g + 1]
        shift_out[row : row + 1, :] = total[b : b + 1]
    down_out[...] = total[last : last + 1]
    up_out[...] = total[last + 1 : last + 5]
    step = lax.broadcasted_iota(jnp.int32, table_out.shape, 0).astype(F32)
    table = jnp.zeros(table_out.shape, F32)
    for k in range(4):
        lane = (k // 2) * half + k % 2
        table = table + jnp.where(step == ids[:, lane : lane + 1], total[2 + k : 3 + k], 0.0)
    table_out[...] = table


def sums(name, jobs, after=()):
    arrays, plan, outs = [], [], []
    for groups, split in jobs:
        steps, row = [], 0
        for group in groups:
            steps.append((row, range(len(arrays), len(arrays) + len(group))))
            row += group[0].shape[1]
            arrays += group
        blocks, width = groups[0][0].shape[0], groups[0][0].shape[2]
        plan.append((len(outs), blocks, split, steps))
        outs += [((blocks // 2, row, width), BF)] * 2 if split else [((blocks, row, width), BF)]
    count = len(arrays)

    def kernel(*refs):
        results = refs[count:]
        for first, blocks, split, steps in plan:
            for row, which in steps:
                total = refs[which[0]][...].astype(F32)
                for k in which[1:]:
                    total = total + refs[k][...].astype(F32)
                total = total.astype(BF)
                rows = pl.ds(row, total.shape[1])
                if split:
                    results[first][:, rows, :] = total[blocks // 2 :]
                    results[first + 1][:, rows, :] = total[: blocks // 2]
                else:
                    results[first][:, rows, :] = total

    return call(kernel, name, outs, [VM] * count, [], arrays, after=after)


def pair_kernel(mine, got, out):
    for k in range(2):
        out[k] = (mine[k].astype(F32) + got[1 - k].astype(F32)).astype(BF)


def tie(value, *others):
    return lax.optimization_barrier((value,) + others)[0]


def over_ctx(value, mask):
    return lax.ppermute(value, "ctx", [(i, i ^ mask) for i in range(16)])


def over_x(value):
    return lax.ppermute(value, "fsdp", [(0, 1), (1, 0)])


def spread(piece, first=()):
    pieces = [piece] + [over_ctx(piece, mask) for mask in (4, 2, 6)]
    pieces = [tie(p, *first) for p in pieces]
    return pieces + [over_ctx(p, 1) for p in pieces]


def shards(
    tokens, encoder, step_ids, out_grad, self_in, self_out, cross_query, cross_keyval, cross_out,
    ffn_up, up_bias, ffn_down, down_bias, norm_gain, norm_shift, step_table,
):
    nctx, nx = lax.axis_size("ctx"), lax.axis_size("fsdp")
    i, x = lax.axis_index("ctx"), lax.axis_index("fsdp")
    seqs, rows, width = tokens.shape
    hd = width // H
    units = seqs * H
    rep = nctx // units
    unit = i // rep
    s_mine, head = unit // H, unit % H
    n = rows * nctx
    ff = 2048
    fast = nctx == 16 and nx == 2
    steps_count = step_table.shape[0]
    slots = seqs * nx
    extra_rows = -(-(slots + 12) // 16) * 16
    zero = jnp.int32(0)

    xk, c, me = zero, zero, zero
    if fast:
        xk, c, me = x, i & 1, ((i >> 1) & 1) * 4 + ((i >> 2) & 1) * 2 + ((i >> 3) & 1)
    active = (i % rep == 0).astype(jnp.int32)
    meta = jnp.stack([xk, c, me, active, seqs * x + s_mine, seqs * x, i & 7, i, head, s_mine]).astype(jnp.int32)

    if fast:
        mine, others = call(
            split_kernel, "split", [((rows + seqs * encoder.shape[1], width), BF)] * 2, [SM, VM, VM], [], (meta, tokens, encoder),
        )
        got = over_ctx(others, 8)
        blocks = [mine] + [over_ctx(mine, mask) for mask in (4, 2, 6)]
        blocks += [got] + [over_ctx(got, mask) for mask in (4, 2, 6)]

        (small,) = call(
            prepare_kernel, "prepare", [((256, width // 2), BF)], [SM, SM] + [VM] * 6,
            [pltpu.VMEM((2 * hd, width // 2), BF), pltpu.VMEM((64, width // 2), F32)],
            (meta, step_ids, self_in, norm_gain, norm_shift, step_table, down_bias, up_bias),
            after=[mine],
        )
        own = dict(keyval=cross_keyval, out=self_out, query=cross_query, cross=cross_out, up=ffn_up, down=ffn_down, joined=self_in)

        weights = [own[name] for group in GROUPS for name in group]
        sizes = [sum(own[name].size for name in group) // 1024 for group in GROUPS]
        packed = call(
            functools.partial(pack_kernel, [len(group) for group in GROUPS]), "pack", [((size, 512), BF) for size in sizes],
            [SM] + [ANY] * len(weights), [pltpu.SemaphoreType.DMA((13,))], (meta, *weights), after=[small],
        )
        other_small = over_x(small)
        near2, near3 = (over_x(tie(p, other_small, *blocks[1:5])) for p in packed[:2])
        wh, gains, shifts, steps, step_mine, bias_u, bias_d, all_ids = call(
            unpack_kernel, "unpack",
            [((3 * hd, width), BF), ((3, width), F32), ((3, width), F32), ((seqs, width), F32), ((1, width), F32),
             ((1, ff), F32), ((1, width), F32), ((1, width), F32)],
            [SM, SM, VM, VM], [pltpu.VMEM((64, width), F32)], (meta, step_ids, small, other_small), after=[packed[0]],
        )
        blocks += [over_ctx(tie(block, wh), 1) for block in blocks]
    else:
        def gather(w, axis=0):
            return lax.all_gather(w, "fsdp", axis=axis, tiled=True)

        gains, shifts = gather(norm_gain, 1).astype(F32), gather(norm_shift, 1).astype(F32)
        table = gather(step_table, 1)
        bias_d, bias_u = gather(down_bias)[None, :].astype(F32), gather(up_bias)[None, :].astype(F32)
        all_ids = gather(step_ids.astype(BF)).astype(F32)
        full = dict(keyval=gather(cross_keyval), out=gather(self_out), query=gather(cross_query), cross=gather(cross_out),
                    up=gather(ffn_up), down=gather(ffn_down), joined=gather(self_in))
        half_of = {name: w.shape[0] // 2 for name, w in full.items()}
        own = {name: w[: half_of[name]] for name, w in full.items()}

        def group(names, which):
            parts = []
            for name in names:
                rest = full[name][half_of[name] :]
                quarter = half_of[name] // 2
                part = rest[which * quarter : (which + 1) * quarter]
                parts += [part[:, b : b + 512] for b in range(0, part.shape[1], 512)]
            return jnp.concatenate(parts, axis=0)

        (near2, far2), (near3, far3), (near4, far4) = ([group(names, w) for w in (0, 1)] for names in GROUPS)
        by_head = full["joined"].reshape(width, 3, H, hd)
        wh = lax.dynamic_index_in_dim(by_head, head, 2, False).reshape(width, 3 * hd).T
        onehot = (jnp.arange(steps_count, dtype=jnp.int32)[None, :] == step_ids[:, None]).astype(BF)
        steps = jnp.dot(onehot, table, preferred_element_type=F32)
        step_mine = lax.dynamic_index_in_dim(steps, s_mine, 0, True)
        every = lax.all_gather(tokens, "ctx", axis=0, tiled=False)
        chosen = lax.dynamic_index_in_dim(every, s_mine, 1, False)
        encs = lax.all_gather(encoder, "ctx", axis=0, tiled=False)
        blocks = [jnp.concatenate([chosen[j], encs[j].reshape(-1, width)], axis=0) for j in range(nctx)]
    xhat0, joined, heads, attended_full, stats = call(
        attend_kernel, "attend",
        [((n, width), BF), ((3 * hd, n), BF), ((nctx, hd, rows), BF), ((hd, n), F32), ((8, n), F32)],
        [SM] + [VM] * (4 + nctx),
        [pltpu.VMEM((n, width), BF), pltpu.VMEM((n, hd), BF)],
        (meta, step_mine, gains, shifts, wh, *blocks),
    )
    hold = []
    back = lax.all_to_all(heads, "ctx", 0, 0, tiled=True)
    if fast:
        far2 = over_ctx(tie(near2, heads), 1)
    att = back.reshape(units, rep, hd, rows)[:, 0].reshape(seqs, width, rows)

    enc_rows = nctx * encoder.shape[1]
    enc_all, kvt, w_keyval = call(
        encoder_kernel, "encoder_rows",
        [((seqs, enc_rows, width), BF), ((seqs, 2 * width, enc_rows), BF), ((width, 2 * width), BF)],
        [SM, ANY, ANY, ANY] + [VM] * nctx,
        [pltpu.SemaphoreType.DMA((5,))],
        (meta, own["keyval"], near2, far2, *blocks),
    )
    if fast:
        near4 = over_x(tie(packed[2], kvt))
        hold = [near4]

    tall = seqs * rows
    square = pltpu.VMEM((width, width), BF)
    hidden2, hidden1, q, crossed, shares = call(
        forward_kernel, "forward",
        [((tall, width), F32), ((tall, width), F32), ((tall, width), BF), ((seqs, width, rows), BF), ((units, rows, enc_rows), BF)],
        [SM] + [VM] * 6 + [ANY] * 5,
        [square] * 3 + [pltpu.SemaphoreType.DMA((9,))],
        (meta, tokens, steps, att, kvt, gains, shifts, own["out"], own["query"], own["cross"], near2, far2),
    )
    if fast:
        far3 = over_ctx(tie(near3, hidden2), 1)
    mixed, h2g, extra1, down_keep, down_send, up_keep, up_send = call(
        feed_kernel, "feed",
        [((seqs, rows, width), BF), ((tall, width), F32), ((extra_rows, width), F32)] + [((16, 64, width), BF)] * 4,
        [SM] + [VM] * 6 + [ANY] * 6,
        [pltpu.VMEM((width, ff), BF), pltpu.VMEM((ff, width), BF), pltpu.VMEM((ff, tall), BF),
         pltpu.VMEM((width, tall), BF), pltpu.VMEM((tall, ff), BF), pltpu.SemaphoreType.DMA((12,))],
        (meta, hidden2, gains, shifts, bias_u, bias_d, out_grad, own["up"], own["down"], near2, far2, near3, far3),
    )
    hold_far = []
    if fast:
        far4 = over_ctx(tie(near4, h2g), 1)
        late = [far4]
        down_got, up_got = over_ctx(down_send, 1), over_ctx(up_send, 1)
    dq, part = call(
        cross_back_kernel, "cross_back",
        [((tall, width), BF), ((seqs, 2 * width, enc_rows), BF)],
        [SM] + [VM] * 4 + [ANY] * 3,
        [square, pltpu.VMEM((tall, width), BF), pltpu.SemaphoreType.DMA((3,))],
        (meta, h2g, q, shares, kvt, own["cross"], near2, far2),
    )
    hold = []
    if fast:
        down_x, down_kept, up_y, up_kept = sums(
            "reduce_1", [([[down_keep, down_got]], True), ([[up_keep, up_got]], True)], [dq])
        down_x1, up_y1 = over_x(down_x), over_ctx(up_y, 2)
        hold = [down_x]
    h1g, att_grad, extra2 = call(
        hidden_back_kernel, "hidden_back",
        [((tall, width), F32), ((seqs, width, rows), BF), ((extra_rows, width), F32)],
        [SM] + [VM] * 5 + [ANY] * 4,
        [square, square, pltpu.SemaphoreType.DMA((6,))],
        (meta, h2g, hidden1, dq, gains, extra1, own["out"], own["query"], near2, far2),
        after=hold,
    )
    by_unit = att_grad.reshape(units, 1, hd, rows)
    grads = lax.all_to_all(jnp.broadcast_to(by_unit, (units, rep, hd, rows)).reshape(nctx, hd, rows), "ctx", 0, 0, tiled=True)
    keep1, send1, keep0, send0, kv_keep, kv_send = call(
        weights_back_kernel, "weights_back",
        [((8, 80, width), BF)] * 4 + [((8, enc_rows // 4, width), BF)] * 2,
        [SM] + [VM] * 10,
        [pltpu.VMEM((width, tall), BF), pltpu.VMEM((seqs, width, enc_rows), BF), pltpu.VMEM((seqs, enc_rows, 2 * width), BF)],
        (meta, h2g, h1g, hidden1, crossed, att, dq, part, enc_all, gains, shifts), after=hold_far,
    )
    hold = []
    if fast:
        got1, got0, kv_0 = (over_ctx(tie(part, grads, down_x1, up_y1), 1) for part in (send1, send0, kv_send))

        down_y, down_kept, up_x, up_kept = sums(
            "reduce_2", [([[down_kept, down_x1]], True), ([[up_kept, up_y1]], True)], [grads, keep1],
        )
        down_y1, up_x1 = over_ctx(down_y, 2), over_x(up_x)
        hold = [down_y]

    head_scratch = [pltpu.VMEM((n // 2, hd), BF), pltpu.VMEM((n // 2, hd), BF), pltpu.VMEM((hd, n), BF)]
    query_acc, key_half = call(
        attend_back_first, "attend_back_1", [((hd, n), F32), ((2 * hd, n // 2), BF)], [VM] * 4, head_scratch,
        (joined, attended_full, stats, grads), after=hold,
    )
    hold = []
    if fast:
        feed_z, feed_kept, cross_x, cross_kept, kv_y, kv_kept = sums(
            "reduce_3",
            [([[down_kept, down_y1], [up_kept, up_x1]], True), ([[keep1, got1]], False), ([[keep0, got0]], False), ([[kv_keep, kv_0]], True)],
            [query_acc],
        )
        feed_z1, cross_x1, kv_1 = over_ctx(feed_z, 4), over_x(cross_x), over_ctx(kv_y, 2)
        hold = [feed_z]
    joined_grad, u_keep, u_send = call(
        attend_back_second, "attend_back_2",
        [((nctx, 3 * hd, rows), BF), ((3 * hd + extra_rows, width // 2), F32), ((3 * hd + extra_rows, width // 2), BF)],
        [SM] + [VM] * 11,
        head_scratch
        + [pltpu.VMEM((2 * hd, n // 2), BF), pltpu.VMEM((hd, n), F32), pltpu.VMEM((3 * hd + 16, n), BF),
           pltpu.VMEM((3 * hd + extra_rows, width), F32)],
        (meta, joined, attended_full, stats, grads, query_acc, key_half, xhat0, gains, shifts, wh, extra2),
        after=hold,
    )
    if fast:
        joined_grad, u_send = tie(joined_grad, feed_z1, kv_1), tie(u_send, feed_z1, kv_1)
        u_x1 = over_x(u_send)[None]
        feed_w, kv_z, kv_kept, cross_y, cross_kept = sums(
            "reduce_4", [([[feed_kept, feed_z1]], False), ([[kv_kept, kv_1]], True), ([[cross_kept, cross_x1]], True)], [u_send],
        )
        feed_w1, kv_2, cross_y1 = over_ctx(feed_w, 8), over_ctx(kv_z, 4), over_ctx(cross_y, 2)
        cross_z, cross_kept, u_sum = sums("reduce_5", [([[cross_kept, cross_y1]], True), ([[u_keep[None], u_x1]], False)])
        cross_z1, u_8 = over_ctx(cross_z, 4), over_ctx(u_sum, 8)
        (merged,) = call(
            merge_kernel, "reduce_6", [((1, 368, width), BF)], [VM] * 4, [], (feed_w, feed_w1, u_sum, u_8), after=[cross_z1, kv_2],
        )
        cross_w, kv_far, kv_near = sums("reduce_7", [([[cross_kept, cross_z1]], False), ([[kv_kept, kv_2]], True)], [merged] + late)
        cross_w1, kv_got = over_ctx(cross_w, 8), over_ctx(kv_far, 8)
        merged = tie(merged, cross_w)
        spread_out = [over_ctx(merged, mask) for mask in (4, 2, 6)]
        hold = [cross_w]
    dj = lax.all_to_all(joined_grad, "ctx", 0, 0, tiled=True)
    dj = dj.reshape(units, rep, 3 * hd, rows)[:, 0].reshape(seqs, H, 3 * hd, rows)
    (tokens_grad,) = call(
        start_kernel, "start_grad",
        [((seqs, rows, width), F32)],
        [SM] + [VM] * 5 + [ANY] * 3,
        [pltpu.VMEM((width, 3 * width), BF), pltpu.VMEM((seqs, 3 * width, rows), BF), pltpu.SemaphoreType.DMA((7,))],
        (meta, dj, tokens, steps, gains, h1g, own["joined"], near4, far4),
        after=hold,
    )

    if fast:
        (cross_pair,) = call(
            pair_kernel, "reduce_8", [((2, 80, width), BF)], [VM] * 2, [], (cross_w, cross_w1), after=[kv_got, tokens_grad],
        )
        pieces = [tie(piece, cross_pair) for piece in [merged] + spread_out]
        pieces = pieces + [over_ctx(piece, 1) for piece in pieces]
        (enc_grad,) = call(
            encoder_back_kernel, "encoder_back", [(encoder.shape, F32)], [VM] * 3, [], (kv_near, kv_got, w_keyval), after=[cross_pair],
        )
        up_grad, down_grad, self_in_grad, gain_grad, shift_grad, table_grad, down_bias_grad, up_bias_grad = call(
            place_kernel, "place",
            [((width // 2, ff), F32), ((ff // 2, width), F32), ((width // 2, 3 * width), F32), ((3, width // 2), F32),
             ((3, width // 2), F32), ((steps_count, width // 2), F32), ((1, width // 2), F32), ((4, width // 2), F32)],
            [SM] + [VM] * 9, [pltpu.VMEM((3 * width, width // 2), F32)], (meta, all_ids, *pieces), after=[enc_grad],
        )
        down_bias_grad, up_bias_grad = down_bias_grad.reshape(-1), up_bias_grad.reshape(-1)
        cross_pieces = spread(cross_pair, [up_grad])
        out_g, query_g, cross_g, keyval_g = call(
            place_cross_kernel, "place_cross",
            [((width // 2, width), F32)] * 3 + [((width // 2, 2 * width), F32)],
            [SM] + [VM] * 8, [], (meta, *cross_pieces),
        )
    else:
        def scatter(g, axis=0):
            return lax.psum(lax.psum_scatter(g, "fsdp", scatter_dimension=axis, tiled=True), "ctx")

        down_all = jnp.stack([down_keep, down_send]).reshape(2, 2, 8, 64, width).transpose(1, 0, 2, 3, 4)
        up_all = jnp.stack([up_keep, up_send]).reshape(2, 2, 2, 4, 64, width).transpose(2, 3, 4, 0, 1, 5)
        down_grad, up_grad = scatter(down_all.reshape(ff, width).astype(F32)), scatter(up_all.reshape(width, ff).astype(F32))
        c_all = jnp.stack([jnp.stack([keep0, send0]), jnp.stack([keep1, send1])])
        out_g, query_g, cross_g = (scatter(c_all[:, :, :, k : k + 16].reshape(width, width).astype(F32)) for k in (0, 16, 32))
        keyval_g = scatter(c_all[:, :, :, 48:80].transpose(0, 2, 3, 1, 4).reshape(width, 2 * width).astype(F32))
        kv = jnp.stack([kv_keep, kv_send]).reshape(2, 2, 2, 2, seqs, 2, enc_rows // 16, width).transpose(4, 3, 2, 1, 0, 6, 5, 7)
        kv = lax.psum_scatter(kv.reshape(seqs, enc_rows, 2 * width), "ctx", scatter_dimension=1, tiled=True)
        enc_grad = jnp.einsum("sre,de->srd", kv, w_keyval, preferred_element_type=F32)
        u = jnp.concatenate([u_keep, u_send.astype(F32)], axis=1)
        every_u = lax.all_gather(lax.psum(u[: 3 * hd], "fsdp"), "ctx", axis=0, tiled=False)
        by_head = every_u.reshape(seqs, H, rep, 3, hd, width).sum(axis=(0, 2))
        joined_g = by_head.transpose(3, 1, 0, 2).reshape(width, 3 * width)
        self_in_grad = lax.dynamic_slice_in_dim(joined_g, x * self_in.shape[0], self_in.shape[0], 0)
        total = lax.psum(u[3 * hd :], ("ctx", "fsdp"))
        wide = norm_gain.shape[1]
        extra = lax.dynamic_slice_in_dim(total, x * wide, wide, 1)
        last = extra_rows - 10
        down_bias_grad = extra[last]
        up_bias_all = total[last + 1 : last + 5].reshape(4, 2, width // 2).transpose(1, 0, 2).reshape(-1)
        up_bias_grad = lax.dynamic_slice_in_dim(up_bias_all, x * up_bias.shape[0], up_bias.shape[0], 0)
        gain_grad = jnp.stack([extra[0], extra[last + 7], extra[last + 5]])
        shift_grad = jnp.stack([extra[1], extra[last + 8], extra[last + 6]])
        hot = (jnp.arange(steps_count, dtype=jnp.int32).astype(F32)[:, None, None] == all_ids[None, :, None]).astype(F32)
        table_grad = jnp.sum(hot * extra[None, 2 : 2 + slots, :], axis=1)

    return (
        mixed, tokens_grad, enc_grad, self_in_grad, out_g, query_g, keyval_g, cross_g, up_grad, up_bias_grad,
        down_grad, down_bias_grad, gain_grad, shift_grad, table_grad,
    )


def solution(mesh):
    tok = P("fsdp", "ctx", None)
    row, vec, col = P("fsdp", None), P("fsdp"), P(None, "fsdp")
    in_specs = (tok, tok, vec, tok, row, row, row, row, row, row, vec, row, vec, col, col, col)
    out_specs = (tok, tok, tok, row, row, row, row, row, row, vec, row, vec, col, col, col)
    return jax.shard_map(shards, mesh=mesh, in_specs=in_specs, out_specs=out_specs, check_vma=False)
```
